128 devices in a mesh: group: 8 (over x, y_lo), blk: 16 (over y_hi, z, core).
Axes of the slice: x: 4, y: 4 (y_hi: 2, y_lo: 2; y = y_hi * 2 + y_lo), z: 4, core: 2. Of those that a mesh axis runs over, the one named last changes fastest.
Arguments:
- spectra: bfloat16 [2048, 2, 2048], P(('group', 'blk')), may hold values from -6 to 6
- live_count: int32 [128], P(('group', 'blk')), may hold values from 12 to 16
- owner_list: int32 [262144, 1], P(('group', 'blk')), may hold values from 0 to 127; in each aligned block of 2048 rows (0 to 2047, 2048 to 4095, ...) at most 32 rows name the same one
- bin_list: int32 [262144], P(('group', 'blk')), may hold values from 0 to 63
Outputs:
- stacks: float32 [8192, 256], P(('group', 'blk'))
The draws below stay inside these ranges and needn't reach their ends.
Inputs may be any that keep to these rules, and one draw needn't show every extreme that they name: `owner_list`: among the rows of one channel block, no owner is named by more than 32 rows, and some block names some owner exactly 32 times; every owner is named somewhere.
All inputs are finite; a program needn't handle non-finite values.
Results may differ from the reference program's by a relative error of at most 0.012.
Values may be sent and summed in bfloat16 or wider, within the bound.
A program may use at most 64 MiB of HBM per device.

```python
import math
import jax
import jax.numpy as jnp
import numpy as np
from jax import lax

C_DEV = 16
FREQS = 2048
LAGS = 256
SMOOTH = 8
BINS_DEV = 64
CHANNELS = 2048
ROWS_DEV = 2048
CAP = 32
N_GROUP = 8
N_BLK = 16
DEVICES = 128


def with_ends(drawn, stream_key, low, largest):
    longest = drawn.shape.index(max(drawn.shape))
    spots = []
    for shift in (0, 1):
        where = [jax.random.randint(jax.random.fold_in(stream_key, axis), (), 0, length) for axis, length in enumerate(drawn.shape)]
        where[longest] = (where[longest] + shift) % drawn.shape[longest]
        spots.append(tuple(where))
    return drawn.at[spots[0]].set(low).at[spots[1]].set(largest)


def level_of(stream_key, shape, split, low, top_value):
    def one(axis_at, shards_of):
        draws = jax.random.uniform(jax.random.fold_in(jax.random.fold_in(stream_key, 6), axis_at), (shards_of,), jnp.float32, low / len(split), top_value / len(split))
        return jnp.repeat(jnp.exp(draws), shape[axis_at] // shards_of).reshape((-1,) + (1,) * (len(shape) - axis_at - 1))

    loudness = one(*split[0])
    for cut in split[1:]:
        loudness = loudness * one(*cut)
    return loudness


def deal_out(stream_key, own, number, rows, number_of, top, bound, slope):
    ranking = jax.random.permutation(stream_key, number_of)
    packed, ordinary = shares(number_of, rows * top, bound, slope, True), shares(number_of, rows * top, bound, slope, False)
    places = jnp.arange(number_of)

    def named(lengths, offset_by):
        used = int((lengths > 0).sum())
        fixed = max(1, used // 4)
        passed = fixed + (places - fixed + offset_by * (used - fixed)) % max(1, number_of - fixed)
        return jnp.zeros((number_of,), jnp.int32).at[ranking[jnp.where(places < fixed, places, passed)]].set(jnp.asarray(lengths, jnp.int32))

    lengths = jnp.where(number % 4 == 0, named(packed, number // 4), named(ordinary, number - number // 4 - 1))
    mixed = jax.random.permutation(jax.random.fold_in(own, 3), number_of)
    donor, taker = mixed[0:number_of // 2 * 2:2], mixed[1:number_of // 2 * 2:2]
    room = jnp.minimum(lengths[donor] - 1, bound - lengths[taker]) // 2
    room = jnp.where((donor == ranking[0]) | (taker == ranking[0]) | (lengths[taker] == 0), 0, jnp.maximum(room, 0))
    passed = jax.random.randint(jax.random.fold_in(own, 4), (number_of // 2,), 0, 1 << 20) % (room + 1)
    lengths = lengths.at[donor].add(-passed).at[taker].add(passed)
    members = jnp.searchsorted(jnp.cumsum(lengths), jnp.arange(rows * top), side="right").astype(jnp.int32)
    listing = members.reshape(top, rows).T
    listing = listing[jax.random.permutation(jax.random.fold_in(own, 1), rows)]
    offset_by = jax.random.randint(jax.random.fold_in(own, 2), (rows, 1), 0, top)
    return jnp.take_along_axis(listing, (jnp.arange(top)[None, :] + offset_by) % top, axis=1)


def shares(number_of, total, most, skew, full):
    weights = [(1 << 20) // math.isqrt(rank ** skew) + 1 for rank in range(1, number_of + 1)]
    largest = most if full else min(most, max(-(-total // number_of), total * weights[0] // sum(weights)))
    least = 1 if total - largest >= number_of - 1 else 0
    given, spare = [largest] + [least] * (number_of - 1), total - largest - least * (number_of - 1)
    while spare > 0:
        movable = [i for i in range(1, number_of) if given[i] < largest] or [i for i in range(1, number_of) if given[i] < most]
        pool, remaining = sum([weights[i] for i in movable]), spare
        for i in movable:
            addition = min(most - given[i], max(1, remaining * weights[i] // pool), spare)
            given[i] = given[i] + addition
            spare = spare - addition
    return np.array(given)


def normal_values(own_key, shape, deviation, limit, pieces=(), kind=jnp.bfloat16):
    entries = jax.random.normal(own_key, shape, jnp.float32) * deviation
    if len(pieces) > 0:
        entries = level_of(own_key, shape, pieces, -0.22, 0.18) * entries
    return jnp.clip(entries, min=-limit, max=limit).astype(kind)


def setup_inputs(seed: int = 0) -> dict:
    arg_keys = jax.random.split(jax.random.key(seed), 5)
    spectra = normal_values(arg_keys[0], (CHANNELS, 2, FREQS), 1.0, 6.0, ((0, 128),))
    live_count = with_ends(jax.random.randint(arg_keys[1], (DEVICES,), C_DEV - max(1, C_DEV // 4), C_DEV + 1), jax.random.fold_in(arg_keys[1], 1), C_DEV - max(1, C_DEV // 4), C_DEV).astype(jnp.int32)
    owner_list_keys = jax.random.split(jax.random.fold_in(arg_keys[2], 1), (DEVICES * ROWS_DEV) // ROWS_DEV)
    owner_list_turns = jax.random.permutation(jax.random.fold_in(arg_keys[2], 3), (DEVICES * ROWS_DEV) // ROWS_DEV)
    owner_list = jax.vmap(lambda own, number: deal_out(jax.random.fold_in(arg_keys[2], 2), own, number, ROWS_DEV, DEVICES, 1, CAP, 2))(owner_list_keys, owner_list_turns).reshape((DEVICES * ROWS_DEV, 1))
    bin_list = with_ends(jax.random.randint(arg_keys[3], (DEVICES * ROWS_DEV,), 0, BINS_DEV), jax.random.fold_in(arg_keys[3], 1), 0, BINS_DEV - 1).astype(jnp.int32)
    return dict(spectra=spectra, live_count=live_count, owner_list=owner_list, bin_list=bin_list)


def whiten(block, live):
    values = block.astype(jnp.float32)
    energy = values[:, 0] * values[:, 0] + values[:, 1] * values[:, 1]
    width = energy.shape[1]
    smooth = lax.optimization_barrier(jnp.mean(energy.reshape(energy.shape[0], width // SMOOTH, SMOOTH), axis=2))
    smooth = jnp.repeat(smooth, SMOOTH, axis=1)
    level = lax.optimization_barrier(jnp.mean(energy, axis=1, keepdims=True))
    alive = (jnp.arange(energy.shape[0], dtype=jnp.int32) < live).astype(jnp.float32)
    inverse_amp = lax.rsqrt(smooth + 0.1 * level + 1e-06) * alive[:, None]
    return (values * inverse_amp[:, None, :]).astype(jnp.bfloat16)

def build_table(width, lag_count):
    frequency = jnp.arange(width, dtype=jnp.int32)
    lag_offset = jnp.arange(lag_count, dtype=jnp.int32) - lag_count // 2
    product = frequency[:, None] * lag_offset[None, :] % (2 * width)
    angles = product.astype(jnp.float32) * (math.pi / width)
    norm_factor = 1.0 / math.sqrt(width)
    return (jnp.concatenate([jnp.cos(angles), -jnp.sin(angles)], axis=0) * norm_factor).astype(jnp.bfloat16)

def correlate(own_block, far_block, lag_table):
    near_vals = own_block.astype(jnp.float32)
    far_vals = far_block.astype(jnp.float32)
    real_own, imag_own = (near_vals[:, 0][:, None, :], near_vals[:, 1][:, None, :])
    real_far, imag_far = (far_vals[:, 0][None, :, :], far_vals[:, 1][None, :, :])
    real_part = real_own * real_far + imag_own * imag_far
    imag_part = imag_own * real_far - real_own * imag_far
    cross_spec = jnp.concatenate([real_part, imag_part], axis=2).astype(jnp.bfloat16)
    pairs = cross_spec.shape[0] * cross_spec.shape[1]
    return jnp.dot(cross_spec.reshape(pairs, cross_spec.shape[2]), lag_table, preferred_element_type=jnp.float32)

def reference(spectra, live_count, owner_list, bin_list):
    device_count = N_GROUP * N_BLK
    blocks = spectra.reshape(device_count, C_DEV, 2, FREQS)
    whitened = jax.vmap(whiten)(blocks, live_count)
    lag_table = build_table(FREQS, LAGS)

    def per_device(device):
        group_index = device // N_BLK
        blk_index = device % N_BLK
        own_block = whitened[device]
        row_list = []
        for step in range(1, N_BLK // 2 + 1):
            partner = group_index * N_BLK + (blk_index - step) % N_BLK
            row_list.append(correlate(own_block, whitened[partner], lag_table))
        return jnp.concatenate(row_list, axis=0)
    all_rows = lax.map(per_device, jnp.arange(device_count, dtype=jnp.int32))
    all_rows = all_rows.reshape(-1, LAGS)
    global_bin = owner_list[:, 0] * BINS_DEV + bin_list
    stack_sums = jax.ops.segment_sum(all_rows, global_bin, num_segments=device_count * BINS_DEV)
    counts = jax.ops.segment_sum(jnp.ones(global_bin.shape, jnp.float32), global_bin, num_segments=device_count * BINS_DEV)
    return stack_sums / jnp.sqrt(counts + 1.0)[:, None]
```

```python
import functools
import math

import jax
import jax.numpy as jnp
import numpy as np
from jax import lax
from jax.experimental import pallas as pl
from jax.experimental.pallas import tpu as pltpu
from jax.sharding import PartitionSpec as P

CH = 16
FREQS = 2048
LAGS = 256
BINS_DEV = 64
MESH = pl.DeviceIdType.MESH
BF = jnp.bfloat16
F32 = jnp.float32

S_SIB, S_FLIP, S_Z, S_RELAY, S_ROWS, S_CODE, S_A, S_B = 0, 1, 1, 5, 8, 13, 14, 30
N_SEM = S_B + 64


def table_constant(width, lag_count):
    frequency = np.arange(width, dtype=np.int32)
    lag_offset = np.arange(lag_count, dtype=np.int32) - lag_count // 2
    product = frequency[:, None] * lag_offset[None, :] % (2 * width)
    angles = product.astype(np.float32) * np.float32(math.pi / width)
    norm = np.float32(1.0 / math.sqrt(width))
    whole = np.concatenate([np.cos(angles), -np.sin(angles)], axis=0) * norm
    return whole.astype(jnp.bfloat16)


def place(x, y, z, core):
    return (x * 2 + lax.rem(y, 2), lax.div(y, 2) * 8 + z * 2 + core)


def kernel(spec_ref, live_ref, code_ref, table_hbm, out_ref, own, spread, blocks, table, cross,
           rows, codes, own_sum, dense, got_a, part, got_b, send_sem, recv_sem, table_sem):
    group, blk = lax.axis_index("group"), lax.axis_index("blk")
    mx, core = lax.div(group, 2), lax.rem(blk, 2)
    my = lax.div(blk, 8) * 2 + lax.rem(group, 2)
    mz = lax.rem(lax.div(blk, 2), 4)

    def at(dx, dy, dz):
        return place(lax.rem(mx + dx, 4), lax.rem(my + dy, 4), lax.rem(mz + dz, 4), core)

    sibling = place(mx, my, mz, 1 - core)

    def send(src, dst, number, device):
        return pltpu.make_async_remote_copy(
            src_ref=src, dst_ref=dst, send_sem=send_sem.at[number], recv_sem=recv_sem.at[number],
            device_id=device, device_id_type=MESH)

    barrier = pltpu.get_barrier_semaphore()
    near = [(dx, dy, dz) for dx in range(4) for dy in range(4) for dz in range(4)
            if 0 < (dx > 0) + (dy > 0) + (dz > 0) < 3]
    pl.semaphore_signal(barrier, inc=1, device_id=sibling, device_id_type=MESH)
    for offset in near:
        pl.semaphore_signal(barrier, inc=1, device_id=at(*offset), device_id_type=MESH)

    table_copy = pltpu.make_async_copy(table_hbm, table, table_sem)
    table_copy.start()

    values = spec_ref[...].astype(F32)
    real, imag = values[:, 0, :], values[:, 1, :]
    energy = real * real + imag * imag
    lane = lax.broadcasted_iota(jnp.int32, energy.shape, 1)
    smooth = energy
    for bit in (1, 2, 4):
        other = jnp.where((lane & bit) == 0, pltpu.roll(smooth, FREQS - bit, 1),
                          pltpu.roll(smooth, bit, 1))
        smooth = smooth + other
    smooth = smooth * 0.125
    level = jnp.sum(energy, axis=1, keepdims=True) * (1.0 / FREQS)
    row = lax.broadcasted_iota(jnp.int32, (CH, 1), 0)
    alive = jnp.where(row < live_ref[0], 1.0, 0.0).astype(F32)
    inverse = lax.rsqrt(smooth + 0.1 * level + 1e-06) * alive
    own[0] = (real * inverse).astype(BF)
    own[1] = (imag * inverse).astype(BF)

    pl.semaphore_wait(barrier, len(near) + 1)

    sib_copy = send(own, blocks.at[0, core], S_SIB, sibling)
    flip_copy = send(own, blocks.at[4, core], S_FLIP, at(0, 2, 0))
    code_copy = send(code_ref, codes, S_CODE, sibling)
    sib_copy.start()
    flip_copy.start()
    code_copy.start()
    blocks[0, core] = own[...]

    z_copies = [None]
    for k in range(1, 4):
        source = lax.div(mz + k, 4) * 4
        z_copies.append(send(blocks.at[source, core], blocks.at[k, core], S_Z + k, at(0, 0, k)))
    for k in range(1, 4):
        @pl.when(mz + k < 4)
        def _(k=k):
            z_copies[k].start()
    flip_copy.wait_recv()
    for k in range(1, 4):
        @pl.when(mz + k >= 4)
        def _(k=k):
            z_copies[k].start()

    def relay(k):
        return send(blocks.at[k, core], blocks.at[k, core], S_RELAY + k - 1, sibling)

    relay(4).start()

    for part_of in range(2):
        for i in range(CH):
            spread[part_of, i] = jnp.broadcast_to(own[part_of, i:i + 1, :], (CH, FREQS))

    def form(place_in, k, far_core):
        def columns(c, carry):
            cols = pl.ds(pl.multiple_of(c * 256, 256), 256)
            cols_imag = pl.ds(pl.multiple_of(c * 256 + FREQS, 256), 256)
            far_r = blocks[k, far_core, 0, :, cols]
            far_i = blocks[k, far_core, 1, :, cols]
            for i in range(CH):
                near_r = spread[0, i, :, cols]
                near_i = spread[1, i, :, cols]
                here = pl.ds(place_in * 256 + i * CH, CH)
                cross[here, cols] = near_r * far_r + near_i * far_i
                cross[here, cols_imag] = near_i * far_r - near_r * far_i
            return carry
        lax.fori_loop(0, FREQS // 256, columns, 0)

    row_copies = []
    sib_copy.wait_recv()
    for k in range(1, 5):
        if k < 4:
            z_copies[k].wait_recv()
            relay(k).start()
        relay(k).wait_recv()
        form(0, k - core, 1 - core)
        form(1, k, core)
        if k == 1:
            table_copy.wait()
        here = pl.ds((k - 1) * 512, 512)
        rows[0, here] = jnp.dot(cross[...], table[...], preferred_element_type=F32).astype(BF)
        copy = send(rows.at[0, here], rows.at[1, here], S_ROWS + k, sibling)
        copy.start()
        row_copies.append(copy)

    code_copy.wait_recv()

    def place_of(code):
        owner, slot = code // 64, code % 64
        ox, oz, oc = owner // 32, owner // 2 % 4, owner % 2
        oy = owner // 8 % 2 * 2 + owner // 16 % 2
        dx, dy, dz = (ox - mx + 4) % 4, (oy - my + 4) % 4, (oz - mz + 4) % 4
        kind = slot // 16
        axis = jnp.where(kind == 3, core, kind)
        along = jnp.where(axis == 0, dx, jnp.where(axis == 1, dy, dz))
        first = jnp.where(axis == 0, dy, dx)
        second = jnp.where(axis == 2, dy, dz)
        spot = (kind * 4 + along) * 256 + (first * 4 + second) * 16 + slot % 16
        return jnp.where(oc == core, spot, -1)

    spots = [place_of(code_ref[...]), place_of(codes[...])]

    for copy in row_copies:
        copy.wait_recv()

    def axis_of(kind):
        axis = kind - lax.div(kind, 3) * (3 - core)
        ex, ez = lax.div(2 - axis, 2), lax.div(axis, 2)
        return ex, 1 - ex - ez, ez

    def copy_a(kind, along):
        ex, ey, ez = axis_of(kind)
        number = kind * 4 + along
        return send(dense.at[number], got_a.at[number], S_A + number,
                    at(ex * along, ey * along, ez * along))

    def tile_sum(number):
        sub = lax.broadcasted_iota(jnp.int32, (256, 2048), 0) + number * 256
        total = None
        for half in range(2):
            hot = jnp.where(sub == spots[half], 1.0, 0.0).astype(BF)
            term = jnp.dot(hot, rows[half], preferred_element_type=F32)
            total = term if total is None else total + term
        return total

    def tile(step, carry):
        along, kind = 3 - lax.div(step, 4), lax.rem(step, 4)
        number = kind * 4 + along
        dense[number] = tile_sum(number).astype(BF)
        copy_a(kind, along).start()
        return carry

    lax.fori_loop(0, 12, tile, 0)

    def tile_own(kind, carry):
        own_sum[kind] = tile_sum(kind * 4)
        return carry

    lax.fori_loop(0, 4, tile_own, 0)

    def copy_b(kind, spot):
        ex, ey, ez = axis_of(kind)
        first, second = lax.div(spot, 4), lax.rem(spot, 4)
        dx = (1 - ex) * first
        dy = ex * first + ez * second
        dz = (1 - ez) * second
        return send(part.at[kind, spot], got_b.at[kind, spot], S_B + kind * 16 + spot,
                    at(dx, dy, dz))

    def finish_a(kind, carry):
        total = own_sum[kind]
        for along in range(1, 4):
            copy_a(kind, along).wait_recv()
            total = total + got_a[kind * 4 + along].astype(F32)
        part[kind] = total.astype(BF).reshape(16, 16, LAGS)

        def go(spot, inner):
            copy_b(kind, spot).start()
            return inner
        lax.fori_loop(1, 16, go, 0)
        return carry

    lax.fori_loop(0, 4, finish_a, 0)

    def finish_b(kind, carry):
        def take(spot, total):
            copy_b(kind, spot).wait_recv()
            return total + got_b[kind, spot].astype(F32)
        total = lax.fori_loop(1, 16, take, part[kind, 0].astype(F32))
        out_ref[pl.ds(pl.multiple_of(kind * 16, 16), 16), :] = total
        return carry

    lax.fori_loop(0, 4, finish_b, 0)

    sib_copy.wait_send()
    flip_copy.wait_send()
    code_copy.wait_send()
    for k in range(1, 4):
        z_copies[k].wait_send()
    for k in range(1, 5):
        relay(k).wait_send()
        row_copies[k - 1].wait_send()

    def sent_a(step, carry):
        copy_a(lax.rem(step, 4), 3 - lax.div(step, 4)).wait_send()
        return carry
    lax.fori_loop(0, 12, sent_a, 0)

    def sent_b(step, carry):
        copy_b(lax.div(step, 15), lax.rem(step, 15) + 1).wait_send()
        return carry
    lax.fori_loop(0, 60, sent_b, 0)


def stack_sums(spectra, live_count, code, table):
    vmem = pl.BlockSpec(memory_space=pltpu.VMEM)
    return pl.pallas_call(
        kernel,
        out_shape=jax.ShapeDtypeStruct((BINS_DEV, LAGS), F32),
        in_specs=[vmem, pl.BlockSpec(memory_space=pltpu.SMEM), vmem,
                  pl.BlockSpec(memory_space=pl.ANY)],
        out_specs=vmem,
        scratch_shapes=[
            pltpu.VMEM((2, CH, FREQS), BF),
            pltpu.VMEM((2, CH, CH, FREQS), BF),
            pltpu.VMEM((5, 2, 2, CH, FREQS), BF),
            pltpu.VMEM((2 * FREQS, LAGS), BF),
            pltpu.VMEM((512, 2 * FREQS), BF),
            pltpu.VMEM((2, 2048, LAGS), BF),
            pltpu.VMEM((1, 2048), jnp.int32),
            pltpu.VMEM((4, 256, LAGS), F32),
            pltpu.VMEM((16, 256, LAGS), BF),
            pltpu.VMEM((16, 256, LAGS), BF),
            pltpu.VMEM((4, 16, 16, LAGS), BF),
            pltpu.VMEM((4, 16, 16, LAGS), BF),
            pltpu.SemaphoreType.DMA((N_SEM,)),
            pltpu.SemaphoreType.DMA((N_SEM,)),
            pltpu.SemaphoreType.DMA,
        ],
        compiler_params=pltpu.CompilerParams(
            collective_id=0, has_side_effects=True, vmem_limit_bytes=56 * 1024 * 1024),
        cost_estimate=pl.CostEstimate(
            flops=13_000_000_000, bytes_accessed=4_000_000, transcendentals=40_000),
    )(spectra, live_count, code, table)


def on_device(spectra, live_count, owner_list, bin_list):
    owner = owner_list[:, 0]
    code = (owner * BINS_DEV + bin_list).reshape(1, -1)
    named = (jnp.arange(128, dtype=jnp.int32)[:, None] == owner[None, :]).astype(BF)
    binned = (jnp.arange(BINS_DEV, dtype=jnp.int32)[:, None] == bin_list[None, :]).astype(BF)
    hits = lax.dot_general(named, binned, (((1,), (1,)), ((), ())), preferred_element_type=F32)
    counts = lax.psum_scatter(hits, ("group", "blk"), scatter_dimension=0, tiled=True)
    table = jnp.asarray(table_constant(FREQS, LAGS))
    sums = stack_sums(spectra, live_count, code, table)
    return sums / jnp.sqrt(counts.reshape(BINS_DEV, 1) + 1.0)


def solution(mesh):
    return jax.shard_map(
        on_device,
        mesh=mesh,
        in_specs=(
            P(("group", "blk"), None, None),
            P(("group", "blk")),
            P(("group", "blk"), None),
            P(("group", "blk")),
        ),
        out_specs=P(("group", "blk"), None),
        check_vma=False,
    )
```

```python
import functools
import math

import jax
import jax.numpy as jnp
import numpy as np
from jax import lax
from jax.experimental import pallas as pl
from jax.experimental.pallas import tpu as pltpu
from jax.sharding import PartitionSpec as P

CH = 16
FREQS = 2048
LAGS = 256
BINS_DEV = 64
MESH = pl.DeviceIdType.MESH
BF = jnp.bfloat16
F32 = jnp.float32

S_SIB, S_FLIP, S_Z, S_RELAY, S_ROWS, S_CODE, S_N, S_A, S_B = 0, 2, 4, 12, 20, 28, 29, 38, 54
N_SEM = S_B + 4
ORDER = (4, 1, 3, 2)


def table_constant(width, lag_count):
    frequency = np.arange(width, dtype=np.int32)
    lag_offset = np.arange(lag_count, dtype=np.int32) - lag_count // 2
    product = frequency[:, None] * lag_offset[None, :] % (2 * width)
    angles = product.astype(np.float32) * np.float32(math.pi / width)
    norm = np.float32(1.0 / math.sqrt(width))
    whole = np.concatenate([np.cos(angles), -np.sin(angles)], axis=0) * norm
    return whole.astype(jnp.bfloat16)


def place(x, y, z, core):
    return (x * 2 + lax.rem(y, 2), lax.div(y, 2) * 8 + z * 2 + core)


def kernel(spec_ref, live_ref, owner_ref, bin_ref, table_hbm, out_ref, own, spread, blocks, table,
           cross, rows, codes, own_sum, dense, got_a, part, got_b, tally, got_n,
           send_sem, recv_sem, table_sem):
    group, blk = lax.axis_index("group"), lax.axis_index("blk")
    mx, core = lax.div(group, 2), lax.rem(blk, 2)
    my = lax.div(blk, 8) * 2 + lax.rem(group, 2)
    mz = lax.rem(lax.div(blk, 2), 4)

    def at(dx, dy, dz):
        return place(lax.rem(mx + dx, 4), lax.rem(my + dy, 4), lax.rem(mz + dz, 4), core)

    sibling = place(mx, my, mz, 1 - core)

    def send(src, dst, number, device):
        return pltpu.make_async_remote_copy(
            src_ref=src, dst_ref=dst, send_sem=send_sem.at[number], recv_sem=recv_sem.at[number],
            device_id=device, device_id_type=MESH)

    barrier = pltpu.get_barrier_semaphore()
    pl.semaphore_signal(barrier, inc=1, device_id=sibling, device_id_type=MESH)
    for v in range(1, 4):
        for device in (at(0, 0, v), at(0, v, 0), at(v, 0, 0)):
            pl.semaphore_signal(barrier, inc=1, device_id=device, device_id_type=MESH)

    table_copy = pltpu.make_async_copy(table_hbm, table, table_sem)
    table_copy.start()

    values = spec_ref[...].astype(F32)
    real, imag = values[:, 0, :], values[:, 1, :]
    energy = real * real + imag * imag
    lane = lax.broadcasted_iota(jnp.int32, energy.shape, 1)
    smooth = energy
    for bit in (1, 2, 4):
        other = jnp.where((lane & bit) == 0, pltpu.roll(smooth, FREQS - bit, 1),
                          pltpu.roll(smooth, bit, 1))
        smooth = smooth + other
    smooth = smooth * 0.125
    level = jnp.sum(energy, axis=1, keepdims=True) * (1.0 / FREQS)
    row = lax.broadcasted_iota(jnp.int32, (CH, 1), 0)
    alive = jnp.where(row < live_ref[0], 1.0, 0.0).astype(F32)
    inverse = lax.rsqrt(smooth + 0.1 * level + 1e-06) * alive
    own[0] = (real * inverse).astype(BF)
    own[1] = (imag * inverse).astype(BF)
    codes[0] = owner_ref[...] * BINS_DEV + bin_ref[...]
    blocks[0, core] = own[...]

    for part_of in range(2):
        for i in range(CH):
            spread[part_of, i] = jnp.broadcast_to(own[part_of, i:i + 1, :], (CH, FREQS))

    pl.semaphore_wait(barrier, 10)

    def flip(half):
        return send(own.at[half], blocks.at[4, core, half], S_FLIP + half, at(0, 2, 0))

    def along_z(k, half):
        source = lax.div(mz + k, 4) * 4
        return send(blocks.at[source, core, half], blocks.at[k, core, half],
                    S_Z + 2 * k + half - 2, at(0, 0, k))

    def relay(k, half):
        return send(blocks.at[k, core, half], blocks.at[k, core, half],
                    S_RELAY + 2 * k + half - 2, sibling)

    def first_relay(half):
        spot = core * 4
        return send(blocks.at[spot, core, half], blocks.at[spot, core, half], S_SIB + half, sibling)

    code_copy = send(codes.at[0], codes.at[1], S_CODE, sibling)
    code_copy.start()
    for half in range(2):
        flip(half).start()

    @pl.when(core == 0)
    def _():
        for half in range(2):
            first_relay(half).start()

    for half in range(2):
        for k in ORDER[1:]:
            @pl.when(mz + k < 4)
            def _(k=k, half=half):
                along_z(k, half).start()

    def offsets_of(code):
        owner = code // 64
        ox, oz, oc = owner // 32, owner // 2 % 4, owner % 2
        oy = owner // 8 % 2 * 2 + owner // 16 % 2
        return (ox - mx + 4) % 4, (oy - my + 4) % 4, (oz - mz + 4) % 4, oc

    def hits_of(code):
        dx, dy, dz, oc = offsets_of(code)
        whose = jnp.where(oc == core, dx * 32 + dy * 8 + dz, -1)
        down = lax.broadcasted_iota(jnp.int32, (128, 2048), 0)
        named = jnp.where(down == whose, 1.0, 0.0).astype(BF)
        binned = jnp.where(down == code % 64, 1.0, 0.0).astype(BF)
        return lax.dot_general(named, binned, (((1,), (1,)), ((), ())), preferred_element_type=F32)

    def copy_n(stage, v):
        spot = stage * 3 + v - 1
        if stage == 0:
            return send(tally.at[pl.ds(32 * v, 32)], got_n.at[spot], S_N + spot, at(v, 0, 0))
        if stage == 1:
            return send(tally.at[pl.ds(8 * v, 8)], got_n.at[spot, pl.ds(0, 8)], S_N + spot,
                        at(0, v, 0))
        return send(tally.at[pl.ds(0, 8)], got_n.at[spot, pl.ds(0, 8)], S_N + spot, at(0, 0, v))

    def tally_stage(stage):
        if stage > 0:
            rows_of = 32 if stage == 1 else 8
            total = tally[0:rows_of]
            for v in range(1, 4):
                copy_n(stage - 1, v).wait()
                total = total + got_n[(stage - 1) * 3 + v - 1, 0:rows_of]
            tally[0:rows_of] = total
        for v in range(1, 4):
            copy_n(stage, v).start()

    hits = hits_of(codes[0])

    for half in range(2):
        flip(half).wait_recv()
        for k in ORDER[1:]:
            @pl.when(mz + k >= 4)
            def _(k=k, half=half):
                along_z(k, half).start()

        @pl.when(core == 1)
        def _(half=half):
            first_relay(half).start()

    code_copy.wait_recv()
    tally[...] = hits + hits_of(codes[1])
    tally_stage(0)

    def form(place_in, k, far_core):
        far_r, far_i = blocks[k, far_core, 0], blocks[k, far_core, 1]
        for i in range(CH):
            near_r, near_i = spread[0, i], spread[1, i]
            here = pl.ds(place_in * 256 + i * CH, CH)
            cross[here, 0:FREQS] = near_r * far_r + near_i * far_i
            cross[here, FREQS:2 * FREQS] = near_i * far_r - near_r * far_i

    def row_copy(step):
        k = ORDER[step // 2]
        if step % 2:
            begin = (2 * k - 1) * 256
        else:
            far = k if k < 4 else 4 * (1 - core)
            begin = pl.multiple_of((2 * far - 2 + 2 * core) * 256, 256)
        here = pl.ds(begin, 256)
        return here, send(rows.at[0, here], rows.at[1, here], S_ROWS + step, sibling)

    def correlate(p):
        k = ORDER[p]
        form(1, k, core)
        if p == 0:
            for half in range(2):
                first_relay(half).wait_recv()
            table_copy.wait()
            form(0, 4 * (1 - core), 1 - core)
        else:
            for half in range(2):
                relay(k, half).wait_recv()
            form(0, k, 1 - core)
        made = jnp.dot(cross[...], table[...], preferred_element_type=F32).astype(BF)
        for side in range(2):
            here, copy = row_copy(2 * p + side)
            rows[0, here] = made[side * 256:(side + 1) * 256]
            copy.start()

    def arrive(k):
        for half in range(2):
            along_z(k, half).wait_recv()
            relay(k, half).start()

    correlate(0)
    arrive(1)
    tally_stage(1)
    arrive(3)
    correlate(1)
    arrive(2)
    tally_stage(2)
    correlate(2)

    def place_of(code):
        slot = code % 64
        dx, dy, dz, oc = offsets_of(code)
        kind = slot // 16
        axis = jnp.where(kind == 3, core, kind)
        along = jnp.where(axis == 0, dx, jnp.where(axis == 1, dy, dz))
        first = jnp.where(axis == 0, dy, dx)
        second = jnp.where(axis == 2, dy, dz)
        spot = (along * 4 + kind) * 256 + (first * 4 + second) * 16 + slot % 16
        return jnp.where(oc == core, spot, -1)

    code_copy.wait_send()
    codes[0] = place_of(codes[0])
    codes[1] = place_of(codes[1])

    correlate(3)

    def axis_of(kind):
        axis = kind - lax.div(kind, 3) * (3 - core)
        ex, ez = lax.div(2 - axis, 2), lax.div(axis, 2)
        return ex, 1 - ex - ez, ez

    def copy_a(kind, along):
        ex, ey, ez = axis_of(kind)
        here = pl.ds(pl.multiple_of(kind * 256, 256), 256)
        return send(dense.at[along, here], got_a.at[along, here], S_A + along * 4 + kind,
                    at(ex * along, ey * along, ez * along))

    def group_half(along, half):
        down = lax.broadcasted_iota(jnp.int32, (1024, 2048), 0)
        hot = jnp.where(down == codes[half] - along * 1024, 1.0, 0.0).astype(BF)
        return jnp.dot(hot, rows[half], preferred_element_type=F32)

    own_sum[...] = group_half(2, 0)
    for step in range(8):
        row_copy(step)[1].wait_recv()

    def send_group(along):
        for kind in range(4):
            copy_a(kind, along).start()

    dense[2] = (own_sum[...] + group_half(2, 1)).astype(BF)
    send_group(2)
    for along in (1, 3):
        dense[along] = (group_half(along, 0) + group_half(along, 1)).astype(BF)
        send_group(along)
    own_sum[...] = group_half(0, 0) + group_half(0, 1)

    def copy_b(kind, spot):
        ex, ey, ez = axis_of(kind)
        first, second = lax.div(spot, 4), lax.rem(spot, 4)
        dx = (1 - ex) * first
        dy = ex * first + ez * second
        dz = (1 - ez) * second
        return send(part.at[kind, spot], got_b.at[kind, spot], S_B + kind, at(dx, dy, dz))

    def all_b(kind):
        rest = pl.ds(1, 15)
        return send(part.at[kind, rest], got_b.at[kind, rest], S_B + kind, sibling)

    for kind in range(4):
        here = pl.ds(kind * 256, 256)
        total = own_sum[here]
        for along in (2, 1, 3):
            copy_a(kind, along).wait_recv()
            total = total + got_a[along, here].astype(F32)
        part[kind] = total.astype(BF).reshape(16, 16, LAGS)

        def go(spot, carry, kind=kind):
            copy_b(kind, spot).start()
            return carry
        lax.fori_loop(1, 16, go, 0)

    count = tally[0:1]
    for v in range(1, 4):
        copy_n(2, v).wait()
        count = count + got_n[5 + v, v:v + 1]
    shape = (BINS_DEV, 128)
    diagonal = lax.broadcasted_iota(jnp.int32, shape, 0) == lax.broadcasted_iota(jnp.int32, shape, 1)
    count = jnp.sum(jnp.where(diagonal, count, 0.0), axis=1, keepdims=True)
    scale = lax.rsqrt(count + 1.0)

    for half in range(2):
        flip(half).wait_send()
        first_relay(half).wait_send()
        for k in range(1, 4):
            relay(k, half).wait_send()
            along_z(k, half).wait_send()
    for step in range(8):
        row_copy(step)[1].wait_send()
    for along in range(1, 4):
        for kind in range(4):
            copy_a(kind, along).wait_send()

    for kind in range(4):
        all_b(kind).wait_recv()
        total = part[kind, 0].astype(F32)
        for spot in range(1, 16):
            total = total + got_b[kind, spot].astype(F32)
        out_ref[kind * 16:(kind + 1) * 16, :] = total * scale[kind * 16:(kind + 1) * 16]

    for kind in range(4):
        all_b(kind).wait_send()


def stacks(spectra, live_count, owner, slot, table):
    vmem = pl.BlockSpec(memory_space=pltpu.VMEM)
    return pl.pallas_call(
        kernel,
        out_shape=jax.ShapeDtypeStruct((BINS_DEV, LAGS), F32),
        in_specs=[vmem, pl.BlockSpec(memory_space=pltpu.SMEM), vmem, vmem,
                  pl.BlockSpec(memory_space=pl.ANY)],
        out_specs=vmem,
        scratch_shapes=[
            pltpu.VMEM((2, CH, FREQS), BF),
            pltpu.VMEM((2, CH, CH, FREQS), BF),
            pltpu.VMEM((5, 2, 2, CH, FREQS), BF),
            pltpu.VMEM((2 * FREQS, LAGS), BF),
            pltpu.VMEM((512, 2 * FREQS), BF),
            pltpu.VMEM((2, 2048, LAGS), BF),
            pltpu.VMEM((2, 1, 2048), jnp.int32),
            pltpu.VMEM((1024, LAGS), F32),
            pltpu.VMEM((4, 1024, LAGS), BF),
            pltpu.VMEM((4, 1024, LAGS), BF),
            pltpu.VMEM((4, 16, 16, LAGS), BF),
            pltpu.VMEM((4, 16, 16, LAGS), BF),
            pltpu.VMEM((128, 128), F32),
            pltpu.VMEM((9, 32, 128), F32),
            pltpu.SemaphoreType.DMA((N_SEM,)),
            pltpu.SemaphoreType.DMA((N_SEM,)),
            pltpu.SemaphoreType.DMA,
        ],
        compiler_params=pltpu.CompilerParams(
            collective_id=0, has_side_effects=True, vmem_limit_bytes=56 * 1024 * 1024),
        cost_estimate=pl.CostEstimate(
            flops=13_000_000_000, bytes_accessed=4_000_000, transcendentals=40_000),
    )(spectra, live_count, owner, slot, table)


def on_device(spectra, live_count, owner_list, bin_list):
    table = jnp.asarray(table_constant(FREQS, LAGS))
    return stacks(spectra, live_count, owner_list.reshape(1, -1), bin_list.reshape(1, -1), table)


def solution(mesh):
    return jax.shard_map(
        on_device,
        mesh=mesh,
        in_specs=(
            P(("group", "blk"), None, None),
            P(("group", "blk")),
            P(("group", "blk"), None),
            P(("group", "blk")),
        ),
        out_specs=P(("group", "blk"), None),
        check_vma=False,
    )
```

```python
import functools
import math

import jax
import jax.numpy as jnp
import numpy as np
from jax import lax
from jax.experimental import pallas as pl
from jax.experimental.pallas import tpu as pltpu
from jax.sharding import PartitionSpec as P

CH = 16
FREQS = 2048
LAGS = 256
BINS_DEV = 64
MESH = pl.DeviceIdType.MESH
BF = jnp.bfloat16
F32 = jnp.float32

S_SIB, S_FAR, S_CODE, S_ROWS, S_N, S_A, S_B = 0, 1, 7, 11, 15, 24, 40
N_SEM = S_B + 4
OWN, BACK, OPPOSITE, FLIP = 0, 1, 2, 3
HALF = FREQS // 2


def table_constant(width, lag_count):
    frequency = np.arange(width, dtype=np.int32)
    lag_offset = np.arange(lag_count, dtype=np.int32) - lag_count // 2
    product = frequency[:, None] * lag_offset[None, :] % (2 * width)
    angles = product.astype(np.float32) * np.float32(math.pi / width)
    norm = np.float32(1.0 / math.sqrt(width))
    whole = np.concatenate([np.cos(angles), -np.sin(angles)], axis=0) * norm
    return whole.astype(jnp.bfloat16)


def place(x, y, z, core):
    return (x * 2 + lax.rem(y, 2), lax.div(y, 2) * 8 + z * 2 + core)


def kernel(spec_ref, live_ref, owner_ref, bin_ref, table_hbm, out_ref, own, blocks, table, cross,
           codes, spots, mine, leaving, coming, rows, own_sum, dense, got_a, part, got_b, tally, got_n,
           send_sem, recv_sem, table_sem):
    group, blk = lax.axis_index("group"), lax.axis_index("blk")
    mx, core = lax.div(group, 2), lax.rem(blk, 2)
    my = lax.div(blk, 8) * 2 + lax.rem(group, 2)
    mz = lax.rem(lax.div(blk, 2), 4)

    def at(dx, dy, dz):
        return place(lax.rem(mx + dx, 4), lax.rem(my + dy, 4), lax.rem(mz + dz, 4), core)

    sibling = place(mx, my, mz, 1 - core)

    def send(src, dst, number, device):
        return pltpu.make_async_remote_copy(
            src_ref=src, dst_ref=dst, send_sem=send_sem.at[number], recv_sem=recv_sem.at[number],
            device_id=device, device_id_type=MESH)

    barrier = pltpu.get_barrier_semaphore()
    pl.semaphore_signal(barrier, inc=1, device_id=sibling, device_id_type=MESH)
    for v in range(1, 4):
        for device in (at(0, 0, v), at(0, v, 0), at(v, 0, 0)):
            pl.semaphore_signal(barrier, inc=1, device_id=device, device_id_type=MESH)

    table_copies = []
    for side in range(2):
        here = pl.ds(pl.multiple_of(side * FREQS + core * HALF, HALF), HALF)
        table_copies.append(pltpu.make_async_copy(
            table_hbm.at[here], table.at[pl.ds(side * HALF, HALF)], table_sem.at[side]))
        table_copies[side].start()

    values = spec_ref[...].astype(F32)
    real, imag = values[:, 0, :], values[:, 1, :]
    energy = real * real + imag * imag
    lane = lax.broadcasted_iota(jnp.int32, energy.shape, 1)
    smooth = energy
    for bit in (1, 2, 4):
        other = jnp.where((lane & bit) == 0, pltpu.roll(smooth, FREQS - bit, 1),
                          pltpu.roll(smooth, bit, 1))
        smooth = smooth + other
    smooth = smooth * 0.125
    level = jnp.sum(energy, axis=1, keepdims=True) * (1.0 / FREQS)
    row = lax.broadcasted_iota(jnp.int32, (CH, 1), 0)
    alive = jnp.where(row < live_ref[0], 1.0, 0.0).astype(F32)
    inverse = lax.rsqrt(smooth + 0.1 * level + 1e-06) * alive
    for side, values in enumerate((real, imag)):
        white = (values * inverse).astype(BF)
        for half in range(2):
            own[half, side] = white[:, half * HALF:(half + 1) * HALF]
    blocks[OWN, core] = own[core]
    codes[OWN, core] = owner_ref[...] * BINS_DEV + bin_ref[...]

    pl.semaphore_wait(barrier, 10)

    toward = {BACK: at(0, 0, 1), OPPOSITE: at(0, 0, 2), FLIP: at(0, 2, 0)}
    sib_copy = send(own.at[1 - core], blocks.at[OWN, core], S_SIB, sibling)
    sib_copy.start()
    code_copy = send(codes.at[OWN, core], codes.at[OWN, core], S_CODE, sibling)
    code_copy.start()

    def far_copy(r, j):
        q = core if j == 0 else 1 - core
        return send(blocks.at[OWN, q], blocks.at[r, q], S_FAR + 2 * (r - 1) + j, toward[r])

    def far_code(r):
        return send(codes.at[OWN], codes.at[r], S_CODE + r, toward[r])

    for r in (FLIP, BACK, OPPOSITE):
        far_copy(r, 0).start()
    sib_copy.wait_recv()
    for r in (FLIP, BACK, OPPOSITE):
        far_copy(r, 1).start()
    code_copy.wait_recv()
    for r in (FLIP, BACK, OPPOSITE):
        far_code(r).start()

    def offsets_of(code):
        owner = code // 64
        ox, oz, oc = owner // 32, owner // 2 % 4, owner % 2
        oy = owner // 8 % 2 * 2 + owner // 16 % 2
        return (ox - mx + 4) % 4, (oy - my + 4) % 4, (oz - mz + 4) % 4, oc

    def hits_of(code):
        dx, dy, dz, oc = offsets_of(code)
        whose = jnp.where(oc == core, dx * 32 + dy * 8 + dz, -1)
        down = lax.broadcasted_iota(jnp.int32, (128, 2048), 0)
        named = jnp.where(down == whose, 1.0, 0.0).astype(BF)
        binned = jnp.where(down == code % 64, 1.0, 0.0).astype(BF)
        return lax.dot_general(named, binned, (((1,), (1,)), ((), ())), preferred_element_type=F32)

    def copy_n(stage, v):
        spot = stage * 3 + v - 1
        if stage == 0:
            return send(tally.at[pl.ds(32 * v, 32)], got_n.at[spot], S_N + spot, at(v, 0, 0))
        if stage == 1:
            return send(tally.at[pl.ds(8 * v, 8)], got_n.at[spot, pl.ds(0, 8)], S_N + spot,
                        at(0, v, 0))
        return send(tally.at[pl.ds(0, 8)], got_n.at[spot, pl.ds(0, 8)], S_N + spot, at(0, 0, v))

    def tally_stage(stage):
        if stage > 0:
            rows_of = 32 if stage == 1 else 8
            total = tally[0:rows_of]
            for v in range(1, 4):
                copy_n(stage - 1, v).wait()
                total = total + got_n[(stage - 1) * 3 + v - 1, 0:rows_of]
            tally[0:rows_of] = total
        for v in range(1, 4):
            copy_n(stage, v).start()

    tally[...] = hits_of(codes[OWN, 0]) + hits_of(codes[OWN, 1])
    tally_stage(0)

    def pair_of(first, q, second, r, steps):
        return first, q, second, r, steps + q - r

    low = 1 - lax.div(mz + 3, 4)
    high = lax.div(mz, 2)

    def pick(flag, one, other):
        return flag * one + (1 - flag) * other

    near_first, near_second = pick(low, BACK, OWN), pick(low, OWN, BACK)
    cross_first, cross_second = pick(low, FLIP, BACK), pick(low, BACK, FLIP)
    far_first, far_second = pick(high, OWN, OPPOSITE), pick(high, OPPOSITE, OWN)
    flip_first, flip_second = pick(high, OPPOSITE, FLIP), pick(high, FLIP, OPPOSITE)
    pairs = [
        [pair_of(OWN, 0, FLIP, 0, 8), pair_of(OWN, 0, FLIP, 1, 8),
         pair_of(OWN, 1, FLIP, 1, 8), pair_of(OWN, 1, OWN, 0, 0)],
        [pair_of(near_first, q, near_second, r, pick(low, 6, 2)) for q in (0, 1) for r in (0, 1)],
        [pair_of(cross_first, q, cross_second, r, pick(low, 2, 6)) for q in (0, 1) for r in (0, 1)],
        [pair_of(far_first, high, far_second, r, 4) for r in (0, 1)]
        + [pair_of(flip_first, high, flip_second, r, 4) for r in (0, 1)],
    ]

    def form(slot, first, q, second, r):
        far_r, far_i = blocks[second, r, 0], blocks[second, r, 1]
        for i in range(CH):
            near_r = jnp.broadcast_to(blocks[first, q, 0, i:i + 1, :], (CH, HALF))
            near_i = jnp.broadcast_to(blocks[first, q, 1, i:i + 1, :], (CH, HALF))
            here = pl.ds(slot * 256 + i * CH, CH)
            cross[here, 0:HALF] = near_r * far_r + near_i * far_i
            cross[here, HALF:FREQS] = near_i * far_r - near_r * far_i

    def row_copy(p):
        return send(leaving.at[p], coming.at[p], S_ROWS + p, sibling)

    def correlate(p):
        for slot, (first, q, second, r, step) in enumerate(pairs[p]):
            form(slot, first, q, second, r)
        made = jnp.dot(cross[...], table[...], preferred_element_type=F32)
        mine[p] = made
        leaving[p] = made.astype(BF)
        row_copy(p).start()

    def complete(p):
        row_copy(p).wait_recv()
        rows[pl.ds(p * 1024, 1024)] = (mine[p] + coming[p].astype(F32)).astype(BF)

    def arrive(r):
        for j in range(2):
            far_copy(r, j).wait_recv()

    arrive(FLIP)
    for copy in table_copies:
        copy.wait()
    correlate(0)
    arrive(BACK)
    correlate(1)
    tally_stage(1)
    complete(0)
    correlate(2)
    for r in (FLIP, BACK, OPPOSITE):
        far_code(r).wait_recv()
    for p in range(4):
        for slot, (first, q, second, r, step) in enumerate(pairs[p]):
            from_row = pl.multiple_of((step - 1) * 256, 256)
            spots[:, pl.ds(p * 1024 + slot * 256, 256)] = codes[first, q, :, pl.ds(from_row, 256)]
    complete(1)
    arrive(OPPOSITE)
    correlate(3)
    tally_stage(2)

    def place_of(code):
        slot = code % 64
        dx, dy, dz, oc = offsets_of(code)
        kind = slot // 16
        axis = jnp.where(kind == 3, core, kind)
        along = jnp.where(axis == 0, dx, jnp.where(axis == 1, dy, dz))
        first = jnp.where(axis == 0, dy, dx)
        second = jnp.where(axis == 2, dy, dz)
        spot = (along * 4 + kind) * 256 + (first * 4 + second) * 16 + slot % 16
        return jnp.where(oc == core, spot, -1)

    spots[...] = place_of(spots[...])
    complete(2)

    def axis_of(kind):
        axis = kind - lax.div(kind, 3) * (3 - core)
        ex, ez = lax.div(2 - axis, 2), lax.div(axis, 2)
        return ex, 1 - ex - ez, ez

    def copy_a(kind, along):
        ex, ey, ez = axis_of(kind)
        here = pl.ds(pl.multiple_of(kind * 256, 256), 256)
        return send(dense.at[along, here], got_a.at[along, here], S_A + along * 4 + kind,
                    at(ex * along, ey * along, ez * along))

    def group_of(along, begin, end):
        down = lax.broadcasted_iota(jnp.int32, (1024, end - begin), 0)
        hot = jnp.where(down == spots[:, begin:end] - along * 1024, 1.0, 0.0).astype(BF)
        return jnp.dot(hot, rows[begin:end], preferred_element_type=F32)

    def send_group(along):
        for kind in range(4):
            copy_a(kind, along).start()

    own_sum[...] = group_of(2, 0, 3072)
    complete(3)
    dense[2] = (own_sum[...] + group_of(2, 3072, 4096)).astype(BF)
    send_group(2)
    for along in (1, 3):
        dense[along] = group_of(along, 0, 4096).astype(BF)
        send_group(along)
    own_sum[...] = group_of(0, 0, 4096)

    def copy_b(kind, spot):
        ex, ey, ez = axis_of(kind)
        first, second = lax.div(spot, 4), lax.rem(spot, 4)
        dx = (1 - ex) * first
        dy = ex * first + ez * second
        dz = (1 - ez) * second
        return send(part.at[kind, spot], got_b.at[kind, spot], S_B + kind, at(dx, dy, dz))

    def all_b(kind):
        rest = pl.ds(1, 15)
        return send(part.at[kind, rest], got_b.at[kind, rest], S_B + kind, sibling)

    for kind in range(4):
        here = pl.ds(kind * 256, 256)
        total = own_sum[here]
        for along in (2, 1, 3):
            copy_a(kind, along).wait_recv()
            total = total + got_a[along, here].astype(F32)
        part[kind] = total.astype(BF).reshape(16, 16, LAGS)

        def go(spot, carry, kind=kind):
            copy_b(kind, spot).start()
            return carry
        lax.fori_loop(1, 16, go, 0)

    count = tally[0:1]
    for v in range(1, 4):
        copy_n(2, v).wait()
        count = count + got_n[5 + v, v:v + 1]
    shape = (BINS_DEV, 128)
    diagonal = lax.broadcasted_iota(jnp.int32, shape, 0) == lax.broadcasted_iota(jnp.int32, shape, 1)
    count = jnp.sum(jnp.where(diagonal, count, 0.0), axis=1, keepdims=True)
    scale = lax.rsqrt(count + 1.0)

    sib_copy.wait_send()
    code_copy.wait_send()
    for r in (FLIP, BACK, OPPOSITE):
        far_code(r).wait_send()
        for j in range(2):
            far_copy(r, j).wait_send()
    for p in range(4):
        row_copy(p).wait_send()
    for along in range(1, 4):
        for kind in range(4):
            copy_a(kind, along).wait_send()

    for kind in range(4):
        all_b(kind).wait_recv()
        total = part[kind, 0].astype(F32)
        for spot in range(1, 16):
            total = total + got_b[kind, spot].astype(F32)
        out_ref[kind * 16:(kind + 1) * 16, :] = total * scale[kind * 16:(kind + 1) * 16]

    for kind in range(4):
        all_b(kind).wait_send()


def stacks(spectra, live_count, owner, slot, table):
    vmem = pl.BlockSpec(memory_space=pltpu.VMEM)
    return pl.pallas_call(
        kernel,
        out_shape=jax.ShapeDtypeStruct((BINS_DEV, LAGS), F32),
        in_specs=[vmem, pl.BlockSpec(memory_space=pltpu.SMEM), vmem, vmem,
                  pl.BlockSpec(memory_space=pl.ANY)],
        out_specs=vmem,
        scratch_shapes=[
            pltpu.VMEM((2, 2, CH, HALF), BF),
            pltpu.VMEM((4, 2, 2, CH, HALF), BF),
            pltpu.VMEM((FREQS, LAGS), BF),
            pltpu.VMEM((1024, FREQS), BF),
            pltpu.VMEM((4, 2, 1, 2048), jnp.int32),
            pltpu.VMEM((1, 4096), jnp.int32),
            pltpu.VMEM((4, 1024, LAGS), F32),
            pltpu.VMEM((4, 1024, LAGS), BF),
            pltpu.VMEM((4, 1024, LAGS), BF),
            pltpu.VMEM((4096, LAGS), BF),
            pltpu.VMEM((1024, LAGS), F32),
            pltpu.VMEM((4, 1024, LAGS), BF),
            pltpu.VMEM((4, 1024, LAGS), BF),
            pltpu.VMEM((4, 16, 16, LAGS), BF),
            pltpu.VMEM((4, 16, 16, LAGS), BF),
            pltpu.VMEM((128, 128), F32),
            pltpu.VMEM((9, 32, 128), F32),
            pltpu.SemaphoreType.DMA((N_SEM,)),
            pltpu.SemaphoreType.DMA((N_SEM,)),
            pltpu.SemaphoreType.DMA((2,)),
        ],
        compiler_params=pltpu.CompilerParams(
            collective_id=0, has_side_effects=True, vmem_limit_bytes=56 * 1024 * 1024),
        cost_estimate=pl.CostEstimate(
            flops=13_000_000_000, bytes_accessed=4_000_000, transcendentals=40_000),
    )(spectra, live_count, owner, slot, table)


def on_device(spectra, live_count, owner_list, bin_list):
    table = jnp.asarray(table_constant(FREQS, LAGS))
    return stacks(spectra, live_count, owner_list.reshape(1, -1), bin_list.reshape(1, -1), table)


def solution(mesh):
    return jax.shard_map(
        on_device,
        mesh=mesh,
        in_specs=(
            P(("group", "blk"), None, None),
            P(("group", "blk")),
            P(("group", "blk"), None),
            P(("group", "blk")),
        ),
        out_specs=P(("group", "blk"), None),
        check_vma=False,
    )
```

```python
import functools
import math

import jax
import jax.numpy as jnp
import numpy as np
from jax import lax
from jax.experimental import pallas as pl
from jax.experimental.pallas import tpu as pltpu
from jax.sharding import PartitionSpec as P

CH = 16
FREQS = 2048
LAGS = 256
BINS_DEV = 64
MESH = pl.DeviceIdType.MESH
BF = jnp.bfloat16
F32 = jnp.float32

S_SIB, S_FAR, S_CODE, S_ROWS, S_N, S_A, S_B = 0, 1, 7, 11, 15, 24, 40
N_SEM = S_B + 4
OWN, BACK, OPPOSITE, FLIP = 0, 1, 2, 3
HALF = FREQS // 2


def table_constant(width, lag_count):
    frequency = np.arange(width, dtype=np.int32)
    lag_offset = np.arange(lag_count, dtype=np.int32) - lag_count // 2
    product = frequency[:, None] * lag_offset[None, :] % (2 * width)
    angles = product.astype(np.float32) * np.float32(math.pi / width)
    norm = np.float32(1.0 / math.sqrt(width))
    whole = np.concatenate([np.cos(angles), -np.sin(angles)], axis=0) * norm
    return whole.astype(jnp.bfloat16)


def place(x, y, z, core):
    return (x * 2 + lax.rem(y, 2), lax.div(y, 2) * 8 + z * 2 + core)


def kernel(spec_ref, live_ref, owner_ref, bin_ref, table_hbm, out_ref, own, blocks, table, cross,
           codes, spots, mine, leaving, coming, rows, own_sum, dense, got_a, part, got_b, tally, got_n,
           send_sem, recv_sem, table_sem):
    group, blk = lax.axis_index("group"), lax.axis_index("blk")
    mx, core = lax.div(group, 2), lax.rem(blk, 2)
    my = lax.div(blk, 8) * 2 + lax.rem(group, 2)
    mz = lax.rem(lax.div(blk, 2), 4)

    def at(dx, dy, dz):
        return place(lax.rem(mx + dx, 4), lax.rem(my + dy, 4), lax.rem(mz + dz, 4), core)

    sibling = place(mx, my, mz, 1 - core)

    def send(src, dst, number, device):
        return pltpu.make_async_remote_copy(
            src_ref=src, dst_ref=dst, send_sem=send_sem.at[number], recv_sem=recv_sem.at[number],
            device_id=device, device_id_type=MESH)

    def apart(work):
        pl.when(core < 2)(work)

    barrier = pltpu.get_barrier_semaphore()
    pl.semaphore_signal(barrier, inc=1, device_id=sibling, device_id_type=MESH)
    for v in range(1, 4):
        for device in (at(0, 0, v), at(0, v, 0), at(v, 0, 0)):
            pl.semaphore_signal(barrier, inc=1, device_id=device, device_id_type=MESH)

    table_copies = []
    for side in range(2):
        here = pl.ds(pl.multiple_of(side * FREQS + core * HALF, HALF), HALF)
        table_copies.append(pltpu.make_async_copy(
            table_hbm.at[here], table.at[pl.ds(side * HALF, HALF)], table_sem.at[side]))
        table_copies[side].start()

    values = spec_ref[...].astype(F32)
    real, imag = values[:, 0, :], values[:, 1, :]
    energy = real * real + imag * imag
    lane = lax.broadcasted_iota(jnp.int32, energy.shape, 1)
    smooth = energy
    for bit in (1, 2, 4):
        other = jnp.where((lane & bit) == 0, pltpu.roll(smooth, FREQS - bit, 1),
                          pltpu.roll(smooth, bit, 1))
        smooth = smooth + other
    smooth = smooth * 0.125
    level = jnp.sum(energy, axis=1, keepdims=True) * (1.0 / FREQS)
    row = lax.broadcasted_iota(jnp.int32, (CH, 1), 0)
    alive = jnp.where(row < live_ref[0], 1.0, 0.0).astype(F32)
    inverse = lax.rsqrt(smooth + 0.1 * level + 1e-06) * alive
    for side, values in enumerate((real, imag)):
        white = (values * inverse).astype(BF)
        for half in range(2):
            own[half, side] = white[:, half * HALF:(half + 1) * HALF]
    blocks[OWN, core] = own[core]
    codes[OWN, core] = owner_ref[...] * BINS_DEV + bin_ref[...]

    pl.semaphore_wait(barrier, 10)

    toward = {BACK: at(0, 0, 1), OPPOSITE: at(0, 0, 2), FLIP: at(0, 2, 0)}
    sib_copy = send(own.at[1 - core], blocks.at[OWN, core], S_SIB, sibling)
    sib_copy.start()
    code_copy = send(codes.at[OWN, core], codes.at[OWN, core], S_CODE, sibling)
    code_copy.start()

    def far_copy(r, j):
        q = core if j == 0 else 1 - core
        return send(blocks.at[OWN, q], blocks.at[r, q], S_FAR + 2 * (r - 1) + j, toward[r])

    def far_code(r):
        return send(codes.at[OWN], codes.at[r], S_CODE + r, toward[r])

    for r in (FLIP, BACK, OPPOSITE):
        far_copy(r, 0).start()
    sib_copy.wait_recv()
    for r in (FLIP, BACK, OPPOSITE):
        far_copy(r, 1).start()
    code_copy.wait_recv()
    for r in (FLIP, BACK, OPPOSITE):
        far_code(r).start()

    def offsets_of(code):
        owner = code // 64
        ox, oz, oc = owner // 32, owner // 2 % 4, owner % 2
        oy = owner // 8 % 2 * 2 + owner // 16 % 2
        return (ox - mx + 4) % 4, (oy - my + 4) % 4, (oz - mz + 4) % 4, oc

    def hits_of(code):
        dx, dy, dz, oc = offsets_of(code)
        whose = jnp.where(oc == core, dx * 32 + dy * 8 + dz, -1)
        down = lax.broadcasted_iota(jnp.int32, (128, 2048), 0)
        named = jnp.where(down == whose, 1.0, 0.0).astype(BF)
        binned = jnp.where(down == code % 64, 1.0, 0.0).astype(BF)
        return lax.dot_general(named, binned, (((1,), (1,)), ((), ())), preferred_element_type=F32)

    def copy_n(stage, v):
        spot = stage * 3 + v - 1
        if stage == 0:
            return send(tally.at[pl.ds(32 * v, 32)], got_n.at[spot], S_N + spot, at(v, 0, 0))
        if stage == 1:
            return send(tally.at[pl.ds(8 * v, 8)], got_n.at[spot, pl.ds(0, 8)], S_N + spot,
                        at(0, v, 0))
        return send(tally.at[pl.ds(0, 8)], got_n.at[spot, pl.ds(0, 8)], S_N + spot, at(0, 0, v))

    def tally_stage(stage):
        if stage > 0:
            rows_of = 32 if stage == 1 else 8
            total = tally[0:rows_of]
            for v in range(1, 4):
                copy_n(stage - 1, v).wait()
                total = total + got_n[(stage - 1) * 3 + v - 1, 0:rows_of]
            tally[0:rows_of] = total
        for v in range(1, 4):
            copy_n(stage, v).start()

    @apart
    def _():
        tally[...] = hits_of(codes[OWN, 0]) + hits_of(codes[OWN, 1])

    tally_stage(0)

    def pair_of(first, q, second, r, steps):
        return first, q, second, r, steps + q - r

    low = 1 - lax.div(mz + 3, 4)
    high = lax.div(mz, 2)

    def pick(flag, one, other):
        return flag * one + (1 - flag) * other

    near_first, near_second = pick(low, BACK, OWN), pick(low, OWN, BACK)
    cross_first, cross_second = pick(low, FLIP, BACK), pick(low, BACK, FLIP)
    far_first, far_second = pick(high, OWN, OPPOSITE), pick(high, OPPOSITE, OWN)
    flip_first, flip_second = pick(high, OPPOSITE, FLIP), pick(high, FLIP, OPPOSITE)
    pairs = [
        [pair_of(OWN, 0, FLIP, 0, 8), pair_of(OWN, 0, FLIP, 1, 8),
         pair_of(OWN, 1, FLIP, 1, 8), pair_of(OWN, 1, OWN, 0, 0)],
        [pair_of(near_first, q, near_second, r, pick(low, 6, 2)) for q in (0, 1) for r in (0, 1)],
        [pair_of(cross_first, q, cross_second, r, pick(low, 2, 6)) for q in (0, 1) for r in (0, 1)],
        [pair_of(far_first, high, far_second, r, 4) for r in (0, 1)]
        + [pair_of(flip_first, high, flip_second, r, 4) for r in (0, 1)],
    ]

    def form(slot, first, q, second, r):
        far_r, far_i = blocks[second, r, 0], blocks[second, r, 1]
        for i in range(CH):
            near_r = jnp.broadcast_to(blocks[first, q, 0, i:i + 1, :], (CH, HALF))
            near_i = jnp.broadcast_to(blocks[first, q, 1, i:i + 1, :], (CH, HALF))
            here = pl.ds(slot * 256 + i * CH, CH)
            cross[here, 0:HALF] = near_r * far_r + near_i * far_i
            cross[here, HALF:FREQS] = near_i * far_r - near_r * far_i

    def row_copy(p):
        return send(leaving.at[p], coming.at[p], S_ROWS + p, sibling)

    def correlate(p):
        @apart
        def _():
            for slot, (first, q, second, r, step) in enumerate(pairs[p]):
                form(slot, first, q, second, r)
            made = jnp.dot(cross[...], table[...], preferred_element_type=F32)
            mine[p] = made
            leaving[p] = made.astype(BF)
        row_copy(p).start()

    def complete(p):
        row_copy(p).wait_recv()

        @apart
        def _():
            rows[pl.ds(p * 1024, 1024)] = (mine[p] + coming[p].astype(F32)).astype(BF)

    def arrive(r):
        for j in range(2):
            far_copy(r, j).wait_recv()

    arrive(FLIP)
    for copy in table_copies:
        copy.wait()
    correlate(0)
    arrive(BACK)
    correlate(1)
    tally_stage(1)
    complete(0)
    correlate(2)
    for r in (FLIP, BACK, OPPOSITE):
        far_code(r).wait_recv()
    for p in range(4):
        for slot, (first, q, second, r, step) in enumerate(pairs[p]):
            from_row = pl.multiple_of((step - 1) * 256, 256)
            spots[:, pl.ds(p * 1024 + slot * 256, 256)] = codes[first, q, :, pl.ds(from_row, 256)]
    complete(1)
    arrive(OPPOSITE)
    correlate(3)
    tally_stage(2)

    def place_of(code):
        slot = code % 64
        dx, dy, dz, oc = offsets_of(code)
        kind = slot // 16
        axis = jnp.where(kind == 3, core, kind)
        along = jnp.where(axis == 0, dx, jnp.where(axis == 1, dy, dz))
        first = jnp.where(axis == 0, dy, dx)
        second = jnp.where(axis == 2, dy, dz)
        spot = (along * 4 + kind) * 256 + (first * 4 + second) * 16 + slot % 16
        return jnp.where(oc == core, spot, -1)

    spots[...] = place_of(spots[...])
    complete(2)

    def axis_of(kind):
        axis = kind - lax.div(kind, 3) * (3 - core)
        ex, ez = lax.div(2 - axis, 2), lax.div(axis, 2)
        return ex, 1 - ex - ez, ez

    def copy_a(kind, along):
        ex, ey, ez = axis_of(kind)
        here = pl.ds(pl.multiple_of(kind * 256, 256), 256)
        return send(dense.at[along, here], got_a.at[along, here], S_A + along * 4 + kind,
                    at(ex * along, ey * along, ez * along))

    def group_of(along, begin, end):
        down = lax.broadcasted_iota(jnp.int32, (1024, end - begin), 0)
        hot = jnp.where(down == spots[:, begin:end] - along * 1024, 1.0, 0.0).astype(BF)
        return jnp.dot(hot, rows[begin:end], preferred_element_type=F32)

    def send_group(along):
        for kind in range(4):
            copy_a(kind, along).start()

    @apart
    def _():
        own_sum[...] = group_of(2, 0, 3072)

    complete(3)

    @apart
    def _():
        dense[2] = (own_sum[...] + group_of(2, 3072, 4096)).astype(BF)

    send_group(2)
    for along in (1, 3):
        @apart
        def _(along=along):
            dense[along] = group_of(along, 0, 4096).astype(BF)

        send_group(along)

    @apart
    def _():
        own_sum[...] = group_of(0, 0, 4096)

    def copy_b(kind, spot):
        ex, ey, ez = axis_of(kind)
        first, second = lax.div(spot, 4), lax.rem(spot, 4)
        dx = (1 - ex) * first
        dy = ex * first + ez * second
        dz = (1 - ez) * second
        return send(part.at[kind, spot], got_b.at[kind, spot], S_B + kind, at(dx, dy, dz))

    def all_b(kind):
        rest = pl.ds(1, 15)
        return send(part.at[kind, rest], got_b.at[kind, rest], S_B + kind, sibling)

    for kind in range(4):
        here = pl.ds(kind * 256, 256)
        total = own_sum[here]
        for along in (2, 1, 3):
            copy_a(kind, along).wait_recv()
            total = total + got_a[along, here].astype(F32)
        part[kind] = total.astype(BF).reshape(16, 16, LAGS)

        def go(spot, carry, kind=kind):
            copy_b(kind, spot).start()
            return carry
        lax.fori_loop(1, 16, go, 0)

    count = tally[0:1]
    for v in range(1, 4):
        copy_n(2, v).wait()
        count = count + got_n[5 + v, v:v + 1]
    shape = (BINS_DEV, 128)
    diagonal = lax.broadcasted_iota(jnp.int32, shape, 0) == lax.broadcasted_iota(jnp.int32, shape, 1)
    count = jnp.sum(jnp.where(diagonal, count, 0.0), axis=1, keepdims=True)
    scale = lax.rsqrt(count + 1.0)

    sib_copy.wait_send()
    code_copy.wait_send()
    for r in (FLIP, BACK, OPPOSITE):
        far_code(r).wait_send()
        for j in range(2):
            far_copy(r, j).wait_send()
    for p in range(4):
        row_copy(p).wait_send()
    for along in range(1, 4):
        for kind in range(4):
            copy_a(kind, along).wait_send()

    for kind in range(4):
        all_b(kind).wait_recv()
        total = part[kind, 0].astype(F32)
        for spot in range(1, 16):
            total = total + got_b[kind, spot].astype(F32)
        out_ref[kind * 16:(kind + 1) * 16, :] = total * scale[kind * 16:(kind + 1) * 16]

    for kind in range(4):
        all_b(kind).wait_send()


def stacks(spectra, live_count, owner, slot, table):
    vmem = pl.BlockSpec(memory_space=pltpu.VMEM)
    return pl.pallas_call(
        kernel,
        out_shape=jax.ShapeDtypeStruct((BINS_DEV, LAGS), F32),
        in_specs=[vmem, pl.BlockSpec(memory_space=pltpu.SMEM), vmem, vmem,
                  pl.BlockSpec(memory_space=pl.ANY)],
        out_specs=vmem,
        scratch_shapes=[
            pltpu.VMEM((2, 2, CH, HALF), BF),
            pltpu.VMEM((4, 2, 2, CH, HALF), BF),
            pltpu.VMEM((FREQS, LAGS), BF),
            pltpu.VMEM((1024, FREQS), BF),
            pltpu.VMEM((4, 2, 1, 2048), jnp.int32),
            pltpu.VMEM((1, 4096), jnp.int32),
            pltpu.VMEM((4, 1024, LAGS), F32),
            pltpu.VMEM((4, 1024, LAGS), BF),
            pltpu.VMEM((4, 1024, LAGS), BF),
            pltpu.VMEM((4096, LAGS), BF),
            pltpu.VMEM((1024, LAGS), F32),
            pltpu.VMEM((4, 1024, LAGS), BF),
            pltpu.VMEM((4, 1024, LAGS), BF),
            pltpu.VMEM((4, 16, 16, LAGS), BF),
            pltpu.VMEM((4, 16, 16, LAGS), BF),
            pltpu.VMEM((128, 128), F32),
            pltpu.VMEM((9, 32, 128), F32),
            pltpu.SemaphoreType.DMA((N_SEM,)),
            pltpu.SemaphoreType.DMA((N_SEM,)),
            pltpu.SemaphoreType.DMA((2,)),
        ],
        compiler_params=pltpu.CompilerParams(
            collective_id=0, has_side_effects=True, vmem_limit_bytes=56 * 1024 * 1024),
        cost_estimate=pl.CostEstimate(
            flops=13_000_000_000, bytes_accessed=4_000_000, transcendentals=40_000),
    )(spectra, live_count, owner, slot, table)


def on_device(spectra, live_count, owner_list, bin_list):
    table = jnp.asarray(table_constant(FREQS, LAGS))
    return stacks(spectra, live_count, owner_list.reshape(1, -1), bin_list.reshape(1, -1), table)


def solution(mesh):
    return jax.shard_map(
        on_device,
        mesh=mesh,
        in_specs=(
            P(("group", "blk"), None, None),
            P(("group", "blk")),
            P(("group", "blk"), None),
            P(("group", "blk")),
        ),
        out_specs=P(("group", "blk"), None),
        check_vma=False,
    )
```

```python
import functools
import math

import jax
import jax.numpy as jnp
import numpy as np
from jax import lax
from jax.experimental import pallas as pl
from jax.experimental.pallas import tpu as pltpu
from jax.sharding import PartitionSpec as P

CH = 16
FREQS = 2048
LAGS = 256
BINS_DEV = 64
MESH = pl.DeviceIdType.MESH
BF = jnp.bfloat16
F32 = jnp.float32

S_SIB, S_FAR, S_CODE, S_ROWS, S_N, S_A, S_B = 0, 1, 7, 11, 15, 24, 40
N_SEM = S_B + 4
OWN, BACK, OPPOSITE, FLIP = 0, 1, 2, 3
HALF = FREQS // 2


def table_constant(width, lag_count):
    frequency = np.arange(width, dtype=np.int32)
    lag_offset = np.arange(lag_count, dtype=np.int32) - lag_count // 2
    product = frequency[:, None] * lag_offset[None, :] % (2 * width)
    angles = product.astype(np.float32) * np.float32(math.pi / width)
    norm = np.float32(1.0 / math.sqrt(width))
    whole = np.concatenate([np.cos(angles), -np.sin(angles)], axis=0) * norm
    return whole.astype(jnp.bfloat16)


def place(x, y, z, core):
    return (x * 2 + lax.rem(y, 2), lax.div(y, 2) * 8 + z * 2 + core)


def kernel(spec_hbm, live_ref, owner_hbm, bin_hbm, table_hbm, out_ref, spec, owner, bins, own, blocks, table, cross,
           codes, spots, mine, leaving, coming, rows, own_sum, dense, got_a, part, got_b, tally, got_n,
           send_sem, recv_sem, table_sem, in_sem):
    group, blk = lax.axis_index("group"), lax.axis_index("blk")
    mx, core = lax.div(group, 2), lax.rem(blk, 2)
    my = lax.div(blk, 8) * 2 + lax.rem(group, 2)
    mz = lax.rem(lax.div(blk, 2), 4)

    part_x = [lax.rem(mx + v, 4) * 2 for v in range(4)]
    part_y = [(lax.rem(lax.rem(my + v, 4), 2), lax.div(lax.rem(my + v, 4), 2) * 8) for v in range(4)]
    part_z = [lax.rem(mz + v, 4) * 2 + core for v in range(4)]

    def at(dx, dy, dz):
        return part_x[dx] + part_y[dy][0], part_y[dy][1] + part_z[dz]

    sibling = place(mx, my, mz, 1 - core)

    def send(src, dst, number, device):
        return pltpu.make_async_remote_copy(
            src_ref=src, dst_ref=dst, send_sem=send_sem.at[number], recv_sem=recv_sem.at[number],
            device_id=device, device_id_type=MESH)

    def apart(work):
        pl.when(core < 2)(work)

    barrier = pltpu.get_barrier_semaphore()
    pl.semaphore_signal(barrier, inc=1, device_id=sibling, device_id_type=MESH)
    for v in range(1, 4):
        for device in (at(0, 0, v), at(0, v, 0), at(v, 0, 0)):
            pl.semaphore_signal(barrier, inc=1, device_id=device, device_id_type=MESH)

    inputs = []
    for number, pair in enumerate(((spec_hbm, spec), (owner_hbm, owner), (bin_hbm, bins))):
        inputs.append(pltpu.make_async_copy(*pair, in_sem.at[number]))
        inputs[number].start()

    table_copies = []
    for side in range(2):
        here = pl.ds(pl.multiple_of(side * FREQS + core * HALF, HALF), HALF)
        table_copies.append(pltpu.make_async_copy(
            table_hbm.at[here], table.at[pl.ds(side * HALF, HALF)], table_sem.at[side]))
        table_copies[side].start()

    for copy in inputs:
        copy.wait()
    values = spec[...].astype(F32)
    real, imag = values[:, 0, :], values[:, 1, :]
    energy = real * real + imag * imag
    lane = lax.broadcasted_iota(jnp.int32, energy.shape, 1)
    smooth = energy
    for bit in (1, 2, 4):
        other = jnp.where((lane & bit) == 0, pltpu.roll(smooth, FREQS - bit, 1),
                          pltpu.roll(smooth, bit, 1))
        smooth = smooth + other
    smooth = smooth * 0.125
    level = jnp.sum(energy, axis=1, keepdims=True) * (1.0 / FREQS)
    row = lax.broadcasted_iota(jnp.int32, (CH, 1), 0)
    alive = jnp.where(row < live_ref[0], 1.0, 0.0).astype(F32)
    inverse = lax.rsqrt(smooth + 0.1 * level + 1e-06) * alive
    for side, values in enumerate((real, imag)):
        white = (values * inverse).astype(BF)
        for half in range(2):
            own[half, side] = white[:, half * HALF:(half + 1) * HALF]
    blocks[OWN, core] = own[core]
    codes[OWN, core] = owner[...] * BINS_DEV + bins[...]

    pl.semaphore_wait(barrier, 10)

    toward = {BACK: at(0, 0, 1), OPPOSITE: at(0, 0, 2), FLIP: at(0, 2, 0)}
    sib_copy = send(own.at[1 - core], blocks.at[OWN, core], S_SIB, sibling)
    sib_copy.start()
    code_copy = send(codes.at[OWN, core], codes.at[OWN, core], S_CODE, sibling)
    code_copy.start()

    def far_copy(r, j):
        q = core if j == 0 else 1 - core
        return send(blocks.at[OWN, q], blocks.at[r, q], S_FAR + 2 * (r - 1) + j, toward[r])

    def far_code(r):
        return send(codes.at[OWN], codes.at[r], S_CODE + r, toward[r])

    far_copy(FLIP, 0).start()
    far_copy(BACK, 0).start()
    sib_copy.wait_recv()
    for r, j in ((FLIP, 1), (BACK, 1), (OPPOSITE, 0), (OPPOSITE, 1)):
        far_copy(r, j).start()
    code_copy.wait_recv()
    for r in (FLIP, BACK, OPPOSITE):
        far_code(r).start()

    def offsets_of(code):
        owner = code // 64
        ox, oz, oc = owner // 32, owner // 2 % 4, owner % 2
        oy = owner // 8 % 2 * 2 + owner // 16 % 2
        return (ox - mx + 4) % 4, (oy - my + 4) % 4, (oz - mz + 4) % 4, oc

    def hits_of(code):
        dx, dy, dz, oc = offsets_of(code)
        whose = jnp.where(oc == core, dx * 32 + dy * 8 + dz, -1)
        down = lax.broadcasted_iota(jnp.int32, (128, 2048), 0)
        named = jnp.where(down == whose, 1.0, 0.0).astype(BF)
        binned = jnp.where(down == code % 64, 1.0, 0.0).astype(BF)
        return lax.dot_general(named, binned, (((1,), (1,)), ((), ())), preferred_element_type=F32)

    def copy_n(stage, v):
        spot = stage * 3 + v - 1
        if stage == 0:
            return send(tally.at[pl.ds(32 * v, 32)], got_n.at[spot], S_N + spot, at(v, 0, 0))
        if stage == 1:
            return send(tally.at[pl.ds(8 * v, 8)], got_n.at[spot, pl.ds(0, 8)], S_N + spot,
                        at(0, v, 0))
        return send(tally.at[pl.ds(0, 8)], got_n.at[spot, pl.ds(0, 8)], S_N + spot, at(0, 0, v))

    def tally_stage(stage):
        if stage > 0:
            rows_of = 32 if stage == 1 else 8
            total = tally[0:rows_of]
            for v in range(1, 4):
                copy_n(stage - 1, v).wait()
                total = total + got_n[(stage - 1) * 3 + v - 1, 0:rows_of]
            tally[0:rows_of] = total
        for v in range(1, 4):
            copy_n(stage, v).start()

    @apart
    def _():
        tally[...] = hits_of(codes[OWN, 0]) + hits_of(codes[OWN, 1])

    tally_stage(0)

    def pair_of(first, q, second, r, steps):
        return first, q, second, r, steps + q - r

    low = 1 - lax.div(mz + 3, 4)
    high = lax.div(mz, 2)

    def pick(flag, one, other):
        return flag * one + (1 - flag) * other

    near_first, near_second = pick(low, BACK, OWN), pick(low, OWN, BACK)
    cross_first, cross_second = pick(low, FLIP, BACK), pick(low, BACK, FLIP)
    far_first, far_second = pick(high, OWN, OPPOSITE), pick(high, OPPOSITE, OWN)
    flip_first, flip_second = pick(high, OPPOSITE, FLIP), pick(high, FLIP, OPPOSITE)
    pairs = [
        [pair_of(OWN, 0, FLIP, 0, 8), pair_of(OWN, 0, FLIP, 1, 8),
         pair_of(OWN, 1, FLIP, 1, 8), pair_of(OWN, 1, OWN, 0, 0)],
        [pair_of(near_first, q, near_second, r, pick(low, 6, 2)) for q in (0, 1) for r in (0, 1)],
        [pair_of(cross_first, q, cross_second, r, pick(low, 2, 6)) for q in (0, 1) for r in (0, 1)],
        [pair_of(far_first, high, far_second, r, 4) for r in (0, 1)]
        + [pair_of(flip_first, high, flip_second, r, 4) for r in (0, 1)],
    ]

    def form(slot, first, q, second, r):
        far_r, far_i = blocks[second, r, 0], blocks[second, r, 1]
        for i in range(CH):
            near_r = jnp.broadcast_to(blocks[first, q, 0, i:i + 1, :], (CH, HALF))
            near_i = jnp.broadcast_to(blocks[first, q, 1, i:i + 1, :], (CH, HALF))
            here = pl.ds(slot * 256 + i * CH, CH)
            cross[here, 0:HALF] = near_r * far_r + near_i * far_i
            cross[here, HALF:FREQS] = near_i * far_r - near_r * far_i

    def row_copy(p):
        return send(leaving.at[p], coming.at[p], S_ROWS + p, sibling)

    def correlate(p):
        @apart
        def _():
            for slot, (first, q, second, r, step) in enumerate(pairs[p]):
                form(slot, first, q, second, r)
            made = jnp.dot(cross[...], table[...], preferred_element_type=F32)
            mine[p] = made
            leaving[p] = made.astype(BF)
        row_copy(p).start()

    def complete(p):
        row_copy(p).wait_recv()

        @apart
        def _():
            rows[pl.ds(p * 1024, 1024)] = (mine[p] + coming[p].astype(F32)).astype(BF)

    def arrive(r):
        for j in range(2):
            far_copy(r, j).wait_recv()

    arrive(FLIP)
    for copy in table_copies:
        copy.wait()
    correlate(0)
    arrive(BACK)
    correlate(1)
    complete(0)
    correlate(2)
    for r in (FLIP, BACK, OPPOSITE):
        far_code(r).wait_recv()
    for p in range(4):
        for slot, (first, q, second, r, step) in enumerate(pairs[p]):
            from_row = pl.multiple_of((step - 1) * 256, 256)
            spots[:, pl.ds(p * 1024 + slot * 256, 256)] = codes[first, q, :, pl.ds(from_row, 256)]
    def place_of(code):
        slot = code % 64
        dx, dy, dz, oc = offsets_of(code)
        kind = slot // 16
        axis = jnp.where(kind == 3, core, kind)
        along = jnp.where(axis == 0, dx, jnp.where(axis == 1, dy, dz))
        first = jnp.where(axis == 0, dy, dx)
        second = jnp.where(axis == 2, dy, dz)
        spot = (along * 4 + kind) * 256 + (first * 4 + second) * 16 + slot % 16
        return jnp.where(oc == core, spot, -1)

    spots[...] = place_of(spots[...])
    tally_stage(1)
    complete(1)
    arrive(OPPOSITE)
    correlate(3)
    tally_stage(2)
    complete(2)

    def device_of(kind, offsets):
        if kind < 3:
            return at(*offsets[kind])
        one, other = at(*offsets[0]), at(*offsets[1])
        return tuple(pick(core, b, a) for a, b in zip(one, other))

    def copy_a(kind, along):
        here = pl.ds(kind * 256, 256)
        return send(dense.at[along, here], got_a.at[along, here], S_A + along * 4 + kind,
                    device_of(kind, ((along, 0, 0), (0, along, 0), (0, 0, along))))

    def group_of(along, begin, end):
        down = lax.broadcasted_iota(jnp.int32, (1024, end - begin), 0)
        hot = jnp.where(down == spots[:, begin:end] - along * 1024, 1.0, 0.0).astype(BF)
        return jnp.dot(hot, rows[begin:end], preferred_element_type=F32)

    def send_group(along):
        for kind in range(4):
            copy_a(kind, along).start()

    @apart
    def _():
        own_sum[...] = group_of(2, 0, 3072)

    complete(3)

    @apart
    def _():
        dense[2] = (own_sum[...] + group_of(2, 3072, 4096)).astype(BF)

    send_group(2)
    for along in (1, 3):
        @apart
        def _(along=along):
            dense[along] = group_of(along, 0, 4096).astype(BF)

        send_group(along)

    @apart
    def _():
        own_sum[...] = group_of(0, 0, 4096)

    def copy_b(kind, spot):
        first, second = spot // 4, spot % 4
        return send(part.at[kind, spot], got_b.at[kind, spot], S_B + kind,
                    device_of(kind, ((0, first, second), (first, 0, second), (first, second, 0))))

    def all_b(kind):
        rest = pl.ds(1, 15)
        return send(part.at[kind, rest], got_b.at[kind, rest], S_B + kind, sibling)

    for kind in range(4):
        for along in (2, 1, 3):
            copy_a(kind, along).wait_recv()

        @apart
        def _(kind=kind):
            here = pl.ds(kind * 256, 256)
            total = own_sum[here]
            for along in (2, 1, 3):
                total = total + got_a[along, here].astype(F32)
            part[kind] = total.astype(BF).reshape(16, 16, LAGS)

        for spot in range(1, 16):
            copy_b(kind, spot).start()

    count = tally[0:1]
    for v in range(1, 4):
        copy_n(2, v).wait()
        count = count + got_n[5 + v, v:v + 1]
    shape = (BINS_DEV, 128)
    diagonal = lax.broadcasted_iota(jnp.int32, shape, 0) == lax.broadcasted_iota(jnp.int32, shape, 1)
    count = jnp.sum(jnp.where(diagonal, count, 0.0), axis=1, keepdims=True)
    scale = lax.rsqrt(count + 1.0)

    sib_copy.wait_send()
    code_copy.wait_send()
    for r in (FLIP, BACK, OPPOSITE):
        far_code(r).wait_send()
        for j in range(2):
            far_copy(r, j).wait_send()
    for p in range(4):
        row_copy(p).wait_send()
    for along in range(1, 4):
        for kind in range(4):
            copy_a(kind, along).wait_send()

    for kind in range(4):
        all_b(kind).wait_recv()
        total = part[kind, 0].astype(F32)
        for spot in range(1, 16):
            total = total + got_b[kind, spot].astype(F32)
        out_ref[kind * 16:(kind + 1) * 16, :] = total * scale[kind * 16:(kind + 1) * 16]

    for kind in range(4):
        all_b(kind).wait_send()


def stacks(spectra, live_count, owner, slot, table):
    vmem, anywhere = pl.BlockSpec(memory_space=pltpu.VMEM), pl.BlockSpec(memory_space=pl.ANY)
    return pl.pallas_call(
        kernel,
        out_shape=jax.ShapeDtypeStruct((BINS_DEV, LAGS), F32),
        in_specs=[anywhere, pl.BlockSpec(memory_space=pltpu.SMEM), anywhere, anywhere, anywhere],
        out_specs=vmem,
        scratch_shapes=[
            pltpu.VMEM((CH, 2, FREQS), BF),
            pltpu.VMEM((1, 2048), jnp.int32),
            pltpu.VMEM((1, 2048), jnp.int32),
            pltpu.VMEM((2, 2, CH, HALF), BF),
            pltpu.VMEM((4, 2, 2, CH, HALF), BF),
            pltpu.VMEM((FREQS, LAGS), BF),
            pltpu.VMEM((1024, FREQS), BF),
            pltpu.VMEM((4, 2, 1, 2048), jnp.int32),
            pltpu.VMEM((1, 4096), jnp.int32),
            pltpu.VMEM((4, 1024, LAGS), F32),
            pltpu.VMEM((4, 1024, LAGS), BF),
            pltpu.VMEM((4, 1024, LAGS), BF),
            pltpu.VMEM((4096, LAGS), BF),
            pltpu.VMEM((1024, LAGS), F32),
            pltpu.VMEM((4, 1024, LAGS), BF),
            pltpu.VMEM((4, 1024, LAGS), BF),
            pltpu.VMEM((4, 16, 16, LAGS), BF),
            pltpu.VMEM((4, 16, 16, LAGS), BF),
            pltpu.VMEM((128, 128), F32),
            pltpu.VMEM((9, 32, 128), F32),
            pltpu.SemaphoreType.DMA((N_SEM,)),
            pltpu.SemaphoreType.DMA((N_SEM,)),
            pltpu.SemaphoreType.DMA((2,)),
            pltpu.SemaphoreType.DMA((3,)),
        ],
        compiler_params=pltpu.CompilerParams(
            collective_id=0, has_side_effects=True, vmem_limit_bytes=56 * 1024 * 1024),
        cost_estimate=pl.CostEstimate(
            flops=13_000_000_000, bytes_accessed=4_000_000, transcendentals=40_000),
    )(spectra, live_count, owner, slot, table)


def on_device(spectra, live_count, owner_list, bin_list):
    table = jnp.asarray(table_constant(FREQS, LAGS))
    return stacks(spectra, live_count, owner_list.reshape(1, -1), bin_list.reshape(1, -1), table)


def solution(mesh):
    return jax.shard_map(
        on_device,
        mesh=mesh,
        in_specs=(
            P(("group", "blk"), None, None),
            P(("group", "blk")),
            P(("group", "blk"), None),
            P(("group", "blk")),
        ),
        out_specs=P(("group", "blk"), None),
        check_vma=False,
    )
```

```python
import functools
import math

import jax
import jax.numpy as jnp
import numpy as np
from jax import lax
from jax.experimental import pallas as pl
from jax.experimental.pallas import tpu as pltpu
from jax.sharding import PartitionSpec as P

CH = 16
FREQS = 2048
LAGS = 256
BINS_DEV = 64
MESH = pl.DeviceIdType.MESH
BF = jnp.bfloat16
F32 = jnp.float32

S_SIB, S_FAR, S_CODE, S_ROWS, S_N, S_A, S_B = 0, 1, 7, 11, 16, 25, 89
N_SEM = S_B + 16
OWN, BACK, OPPOSITE, FLIP = 0, 1, 2, 3
HALF = FREQS // 2


def table_constant(width, lag_count):
    frequency = np.arange(width, dtype=np.int32)
    lag_offset = np.arange(lag_count, dtype=np.int32) - lag_count // 2
    product = frequency[:, None] * lag_offset[None, :] % (2 * width)
    angles = product.astype(np.float32) * np.float32(math.pi / width)
    norm = np.float32(1.0 / math.sqrt(width))
    whole = np.concatenate([np.cos(angles), -np.sin(angles)], axis=0) * norm
    return whole.astype(jnp.bfloat16)


def place(x, y, z, core):
    return (x * 2 + lax.rem(y, 2), lax.div(y, 2) * 8 + z * 2 + core)


def kernel(spec_hbm, live_ref, owner_hbm, bin_hbm, table_hbm, out_ref, spec, owner, bins, own, blocks, table, cross,
           codes, spots, mine, leaving, coming, rows, early, own_sum, dense, got_a, part, got_b, tally, got_n,
           send_sem, recv_sem, table_sem, in_sem):
    group, blk = lax.axis_index("group"), lax.axis_index("blk")
    mx, core = lax.div(group, 2), lax.rem(blk, 2)
    my = lax.div(blk, 8) * 2 + lax.rem(group, 2)
    mz = lax.rem(lax.div(blk, 2), 4)

    part_x = [lax.rem(mx + v, 4) * 2 for v in range(4)]
    part_y = [(lax.rem(lax.rem(my + v, 4), 2), lax.div(lax.rem(my + v, 4), 2) * 8) for v in range(4)]
    part_z = [lax.rem(mz + v, 4) * 2 + core for v in range(4)]

    def at(dx, dy, dz):
        return part_x[dx] + part_y[dy][0], part_y[dy][1] + part_z[dz]

    sibling = place(mx, my, mz, 1 - core)

    def send(src, dst, number, device):
        return pltpu.make_async_remote_copy(
            src_ref=src, dst_ref=dst, send_sem=send_sem.at[number], recv_sem=recv_sem.at[number],
            device_id=device, device_id_type=MESH)

    def apart(work):
        pl.when(core < 2)(work)

    barrier = pltpu.get_barrier_semaphore()
    pl.semaphore_signal(barrier, inc=1, device_id=sibling, device_id_type=MESH)
    for v in range(1, 4):
        for device in (at(0, 0, v), at(0, v, 0), at(v, 0, 0)):
            pl.semaphore_signal(barrier, inc=1, device_id=device, device_id_type=MESH)

    inputs = []
    for number, pair in enumerate(((spec_hbm, spec), (owner_hbm, owner), (bin_hbm, bins))):
        inputs.append(pltpu.make_async_copy(*pair, in_sem.at[number]))
        inputs[number].start()

    table_copies = []
    for side in range(2):
        here = pl.ds(pl.multiple_of(side * FREQS + core * HALF, HALF), HALF)
        table_copies.append(pltpu.make_async_copy(
            table_hbm.at[here], table.at[pl.ds(side * HALF, HALF)], table_sem.at[side]))
        table_copies[side].start()

    for copy in inputs:
        copy.wait()
    values = spec[...].astype(F32)
    real, imag = values[:, 0, :], values[:, 1, :]
    energy = real * real + imag * imag
    lane = lax.broadcasted_iota(jnp.int32, energy.shape, 1)
    smooth = energy
    for bit in (1, 2, 4):
        other = jnp.where((lane & bit) == 0, pltpu.roll(smooth, FREQS - bit, 1),
                          pltpu.roll(smooth, bit, 1))
        smooth = smooth + other
    smooth = smooth * 0.125
    level = jnp.sum(energy, axis=1, keepdims=True) * (1.0 / FREQS)
    row = lax.broadcasted_iota(jnp.int32, (CH, 1), 0)
    alive = jnp.where(row < live_ref[0], 1.0, 0.0).astype(F32)
    inverse = lax.rsqrt(smooth + 0.1 * level + 1e-06) * alive
    for side, values in enumerate((real, imag)):
        white = (values * inverse).astype(BF)
        for half in range(2):
            own[half, side] = white[:, half * HALF:(half + 1) * HALF]
    blocks[OWN, core] = own[core]
    codes[OWN, core] = owner[...] * BINS_DEV + bins[...]

    pl.semaphore_wait(barrier, 10)

    toward = {BACK: at(0, 0, 1), OPPOSITE: at(0, 0, 2), FLIP: at(0, 2, 0)}
    sib_copy = send(own.at[1 - core], blocks.at[OWN, core], S_SIB, sibling)
    sib_copy.start()
    code_copy = send(codes.at[OWN, core], codes.at[OWN, core], S_CODE, sibling)
    code_copy.start()

    def far_copy(r, j):
        q = core if j == 0 else 1 - core
        return send(blocks.at[OWN, q], blocks.at[r, q], S_FAR + 2 * (r - 1) + j, toward[r])

    def far_code(r):
        return send(codes.at[OWN], codes.at[r], S_CODE + r, toward[r])

    far_copy(FLIP, 0).start()
    far_copy(BACK, 0).start()
    sib_copy.wait_recv()
    for r, j in ((FLIP, 1), (BACK, 1), (OPPOSITE, 0), (OPPOSITE, 1)):
        far_copy(r, j).start()
    code_copy.wait_recv()
    for r in (FLIP, BACK, OPPOSITE):
        far_code(r).start()

    def offsets_of(code):
        owner = code // 64
        ox, oz, oc = owner // 32, owner // 2 % 4, owner % 2
        oy = owner // 8 % 2 * 2 + owner // 16 % 2
        return (ox - mx + 4) % 4, (oy - my + 4) % 4, (oz - mz + 4) % 4, oc

    def hits_of(code):
        dx, dy, dz, oc = offsets_of(code)
        whose = jnp.where(oc == core, dx * 32 + dy * 8 + dz, -1)
        down = lax.broadcasted_iota(jnp.int32, (128, 2048), 0)
        named = jnp.where(down == whose, 1.0, 0.0).astype(BF)
        binned = jnp.where(down == code % 64, 1.0, 0.0).astype(BF)
        return lax.dot_general(named, binned, (((1,), (1,)), ((), ())), preferred_element_type=F32)

    def copy_n(stage, v):
        spot = stage * 3 + v - 1
        if stage == 0:
            return send(tally.at[pl.ds(32 * v, 32)], got_n.at[spot], S_N + spot, at(v, 0, 0))
        if stage == 1:
            return send(tally.at[pl.ds(8 * v, 8)], got_n.at[spot, pl.ds(0, 8)], S_N + spot,
                        at(0, v, 0))
        return send(tally.at[pl.ds(0, 8)], got_n.at[spot, pl.ds(0, 8)], S_N + spot, at(0, 0, v))

    def tally_stage(stage):
        if stage > 0:
            rows_of = 32 if stage == 1 else 8
            total = tally[0:rows_of]
            for v in range(1, 4):
                copy_n(stage - 1, v).wait()
                total = total + got_n[(stage - 1) * 3 + v - 1, 0:rows_of]
            tally[0:rows_of] = total
        for v in range(1, 4):
            copy_n(stage, v).start()

    @apart
    def _():
        tally[...] = hits_of(codes[OWN, 0]) + hits_of(codes[OWN, 1])

    tally_stage(0)

    def pair_of(first, q, second, r, steps):
        return first, q, second, r, steps + q - r

    low = 1 - lax.div(mz + 3, 4)
    high = lax.div(mz, 2)

    def pick(flag, one, other):
        return flag * one + (1 - flag) * other

    near_first, near_second = pick(low, BACK, OWN), pick(low, OWN, BACK)
    cross_first, cross_second = pick(low, FLIP, BACK), pick(low, BACK, FLIP)
    far_first, far_second = pick(high, OWN, OPPOSITE), pick(high, OPPOSITE, OWN)
    flip_first, flip_second = pick(high, OPPOSITE, FLIP), pick(high, FLIP, OPPOSITE)
    pairs = [
        [pair_of(OWN, 0, FLIP, 0, 8), pair_of(OWN, 0, FLIP, 1, 8),
         pair_of(OWN, 1, FLIP, 1, 8), pair_of(OWN, 1, OWN, 0, 0)],
        [pair_of(near_first, q, near_second, r, pick(low, 6, 2)) for q in (0, 1) for r in (0, 1)],
        [pair_of(cross_first, q, cross_second, r, pick(low, 2, 6)) for q in (0, 1) for r in (0, 1)],
        [pair_of(far_first, high, far_second, r, 4) for r in (0, 1)]
        + [pair_of(flip_first, high, flip_second, r, 4) for r in (0, 1)],
    ]

    def form(slot, first, q, second, r):
        far_r, far_i = blocks[second, r, 0], blocks[second, r, 1]
        for i in range(CH):
            near_r = jnp.broadcast_to(blocks[first, q, 0, i:i + 1, :], (CH, HALF))
            near_i = jnp.broadcast_to(blocks[first, q, 1, i:i + 1, :], (CH, HALF))
            here = pl.ds(slot * 256 + i * CH, CH)
            cross[here, 0:HALF] = near_r * far_r + near_i * far_i
            cross[here, HALF:FREQS] = near_i * far_r - near_r * far_i

    runs = [(0, 0, 4), (1, 0, 4), (2, 0, 4), (3, 0, 2), (3, 2, 4)]

    def row_copy(run):
        p, begin, end = runs[run]
        here = pl.ds(begin * 256, (end - begin) * 256)
        return send(leaving.at[p, here], coming.at[p, here], S_ROWS + run, sibling)

    def correlate(run):
        p, begin, end = runs[run]
        here = pl.ds(begin * 256, (end - begin) * 256)

        @apart
        def _():
            for slot in range(begin, end):
                first, q, second, r, step = pairs[p][slot]
                form(slot, first, q, second, r)
            made = jnp.dot(cross[here], table[...], preferred_element_type=F32)
            mine[p, here] = made
            leaving[p, here] = made.astype(BF)
        row_copy(run).start()

    def complete(run):
        p, begin, end = runs[run]
        here = pl.ds(begin * 256, (end - begin) * 256)
        row_copy(run).wait_recv()

        @apart
        def _():
            total = mine[p, here] + coming[p, here].astype(F32)
            rows[pl.ds(p * 1024 + begin * 256, (end - begin) * 256)] = total.astype(BF)

    def arrive(r):
        for j in range(2):
            far_copy(r, j).wait_recv()

    arrive(FLIP)
    for copy in table_copies:
        copy.wait()
    correlate(0)
    arrive(BACK)
    correlate(1)
    complete(0)
    correlate(2)
    for r in (FLIP, BACK, OPPOSITE):
        far_code(r).wait_recv()
    for p in range(4):
        for slot, (first, q, second, r, step) in enumerate(pairs[p]):
            from_row = pl.multiple_of((step - 1) * 256, 256)
            spots[:, pl.ds(p * 1024 + slot * 256, 256)] = codes[first, q, :, pl.ds(from_row, 256)]
    def place_of(code):
        slot = code % 64
        dx, dy, dz, oc = offsets_of(code)
        kind = slot // 16
        side = jnp.where(core == 0, dy, dx)
        axis = jnp.where(kind == 3, jnp.where(side == 1, 2, core), kind)
        first = jnp.where(kind == 3, side, jnp.where(kind == 0, dy, dx))
        along = jnp.where(axis == 0, dx, jnp.where(axis == 1, dy, dz))
        second = jnp.where(axis < 2, dz, jnp.where((kind == 3) & (core == 0), dx, dy))
        spot = first * 1024 + (along * 4 + kind) * 64 + second * 16 + slot % 16
        return jnp.where(oc == core, spot, -1)

    spots[...] = place_of(spots[...])
    tally_stage(1)
    complete(1)
    arrive(OPPOSITE)
    correlate(3)
    correlate(4)
    tally_stage(2)
    complete(2)

    def device_of(kind, offsets):
        if kind < 3:
            return at(*offsets[kind])
        one, other = at(*offsets[3]), at(*offsets[4])
        return tuple(pick(core, b, a) for a, b in zip(one, other))

    def copy_a(group, along, kind):
        here = pl.ds(kind * 64, 64)
        x, y, z = (along, 0, 0), (0, along, 0), (0, 0, along)
        last = (z, z) if group == 1 else (x, y)
        return send(dense.at[group, along, here], got_a.at[group, along, here],
                    S_A + group * 16 + along * 4 + kind, device_of(kind, (x, y, z) + last))

    def copy_b(group, kind, second):
        if group == 1:
            last = ((second, group, 0), (group, second, 0))
        else:
            last = ((0, group, second), (group, 0, second))
        spot = kind * 4 + second
        offsets = ((0, group, second), (group, 0, second), (group, second, 0)) + last
        return send(part.at[group, spot], got_b.at[group, spot], S_B + group * 4 + kind,
                    device_of(kind, offsets))

    def all_b(group, kind):
        skip = 1 if group == 0 else 0
        here = pl.ds(kind * 4 + skip, 4 - skip)
        return send(part.at[group, here], got_b.at[group, here], S_B + group * 4 + kind, sibling)

    def hot_sum(group, begin, end):
        down = lax.broadcasted_iota(jnp.int32, (1024, end - begin), 0)
        hot = jnp.where(down == spots[:, begin:end] - group * 1024, 1.0, 0.0).astype(BF)
        return jnp.dot(hot, rows[begin:end], preferred_element_type=F32)

    def keep(group, total):
        own_sum[group] = total[0:256]
        dense[group] = total.astype(BF).reshape(4, 256, LAGS)

    def send_a(group):
        for along in (2, 1, 3):
            for kind in range(4):
                copy_a(group, along, kind).start()

    def pass_on(group):
        for along in (2, 1, 3):
            for kind in range(4):
                copy_a(group, along, kind).wait_recv()

        @apart
        def _():
            total = own_sum[group]
            for along in (2, 1, 3):
                total = total + got_a[group, along].astype(F32)
            part[group] = total.astype(BF).reshape(16, 16, LAGS)

        for second in range(4):
            for kind in range(4):
                if group or second:
                    copy_b(group, kind, second).start()

    @apart
    def _():
        early[...] = hot_sum(0, 0, 3072)

    complete(3)
    complete(4)

    @apart
    def _():
        keep(0, early[...] + hot_sum(0, 3072, 4096))

    send_a(0)
    for group in range(1, 4):
        @apart
        def _(group=group):
            keep(group, hot_sum(group, 0, 4096))

        send_a(group)
        if group == 3:
            pass_on(0)
    for group in range(1, 4):
        pass_on(group)

    count = tally[0:1]
    for v in range(1, 4):
        copy_n(2, v).wait()
        count = count + got_n[5 + v, v:v + 1]
    shape = (BINS_DEV, 128)
    diagonal = lax.broadcasted_iota(jnp.int32, shape, 0) == lax.broadcasted_iota(jnp.int32, shape, 1)
    count = jnp.sum(jnp.where(diagonal, count, 0.0), axis=1, keepdims=True)
    scale = lax.rsqrt(count + 1.0)

    sib_copy.wait_send()
    code_copy.wait_send()
    for r in (FLIP, BACK, OPPOSITE):
        far_code(r).wait_send()
        for j in range(2):
            far_copy(r, j).wait_send()
    for run in range(5):
        row_copy(run).wait_send()
    for group in range(4):
        for along in range(1, 4):
            for kind in range(4):
                copy_a(group, along, kind).wait_send()

    def gather(group):
        for kind in range(4):
            all_b(group, kind).wait_recv()

        @apart
        def _():
            for kind in range(4):
                here = pl.ds(kind * 16, 16)
                total = part[0, kind * 4].astype(F32) if group == 0 else out_ref[here]
                for second in range(4):
                    if group or second:
                        total = total + got_b[group, kind * 4 + second].astype(F32)
                out_ref[here] = total if group < 3 else total * scale[kind * 16:(kind + 1) * 16]

    for group in range(4):
        gather(group)
    for group in range(4):
        for kind in range(4):
            all_b(group, kind).wait_send()


def stacks(spectra, live_count, owner, slot, table):
    vmem, anywhere = pl.BlockSpec(memory_space=pltpu.VMEM), pl.BlockSpec(memory_space=pl.ANY)
    return pl.pallas_call(
        kernel,
        out_shape=jax.ShapeDtypeStruct((BINS_DEV, LAGS), F32),
        in_specs=[anywhere, pl.BlockSpec(memory_space=pltpu.SMEM), anywhere, anywhere, anywhere],
        out_specs=vmem,
        scratch_shapes=[
            pltpu.VMEM((CH, 2, FREQS), BF),
            pltpu.VMEM((1, 2048), jnp.int32),
            pltpu.VMEM((1, 2048), jnp.int32),
            pltpu.VMEM((2, 2, CH, HALF), BF),
            pltpu.VMEM((4, 2, 2, CH, HALF), BF),
            pltpu.VMEM((FREQS, LAGS), BF),
            pltpu.VMEM((1024, FREQS), BF),
            pltpu.VMEM((4, 2, 1, 2048), jnp.int32),
            pltpu.VMEM((1, 4096), jnp.int32),
            pltpu.VMEM((4, 1024, LAGS), F32),
            pltpu.VMEM((4, 1024, LAGS), BF),
            pltpu.VMEM((4, 1024, LAGS), BF),
            pltpu.VMEM((4096, LAGS), BF),
            pltpu.VMEM((1024, LAGS), F32),
            pltpu.VMEM((4, 256, LAGS), F32),
            pltpu.VMEM((4, 4, 256, LAGS), BF),
            pltpu.VMEM((4, 4, 256, LAGS), BF),
            pltpu.VMEM((4, 16, 16, LAGS), BF),
            pltpu.VMEM((4, 16, 16, LAGS), BF),
            pltpu.VMEM((128, 128), F32),
            pltpu.VMEM((9, 32, 128), F32),
            pltpu.SemaphoreType.DMA((N_SEM,)),
            pltpu.SemaphoreType.DMA((N_SEM,)),
            pltpu.SemaphoreType.DMA((2,)),
            pltpu.SemaphoreType.DMA((3,)),
        ],
        compiler_params=pltpu.CompilerParams(
            collective_id=0, has_side_effects=True, vmem_limit_bytes=56 * 1024 * 1024),
        cost_estimate=pl.CostEstimate(
            flops=13_000_000_000, bytes_accessed=4_000_000, transcendentals=40_000),
    )(spectra, live_count, owner, slot, table)


def on_device(spectra, live_count, owner_list, bin_list):
    table = jnp.asarray(table_constant(FREQS, LAGS))
    return stacks(spectra, live_count, owner_list.reshape(1, -1), bin_list.reshape(1, -1), table)


def solution(mesh):
    return jax.shard_map(
        on_device,
        mesh=mesh,
        in_specs=(
            P(("group", "blk"), None, None),
            P(("group", "blk")),
            P(("group", "blk"), None),
            P(("group", "blk")),
        ),
        out_specs=P(("group", "blk"), None),
        check_vma=False,
    )
```

```python
import functools
import math

import jax
import jax.numpy as jnp
import numpy as np
from jax import lax
from jax.experimental import pallas as pl
from jax.experimental.pallas import tpu as pltpu
from jax.sharding import PartitionSpec as P

CH = 16
FREQS = 2048
LAGS = 256
BINS_DEV = 64
MESH = pl.DeviceIdType.MESH
BF = jnp.bfloat16
F32 = jnp.float32

S_SIB, S_FAR, S_CODE, S_ROWS, S_N, S_A, S_B = 0, 1, 7, 11, 27, 36, 56
N_SEM = S_B + 4
OWN, BACK, OPPOSITE, FLIP = 0, 1, 2, 3
HALF = FREQS // 2


def table_constant(width, lag_count):
    frequency = np.arange(width, dtype=np.int32)
    lag_offset = np.arange(lag_count, dtype=np.int32) - lag_count // 2
    product = frequency[:, None] * lag_offset[None, :] % (2 * width)
    angles = product.astype(np.float32) * np.float32(math.pi / width)
    norm = np.float32(1.0 / math.sqrt(width))
    whole = np.concatenate([np.cos(angles), -np.sin(angles)], axis=0) * norm
    return whole.astype(jnp.bfloat16)


def place(x, y, z, core):
    return (x * 2 + lax.rem(y, 2), lax.div(y, 2) * 8 + z * 2 + core)


def kernel(spec_hbm, live_ref, owner_hbm, bin_hbm, table_hbm, out_ref, spec, owner, bins, own, blocks, table, cross,
           codes, spots, mine, leaving, coming, rows, own_sum, dense, got_a, part, got_b, tally, got_n,
           send_sem, recv_sem, table_sem, in_sem):
    group, blk = lax.axis_index("group"), lax.axis_index("blk")
    mx, core = lax.div(group, 2), lax.rem(blk, 2)
    my = lax.div(blk, 8) * 2 + lax.rem(group, 2)
    mz = lax.rem(lax.div(blk, 2), 4)

    part_x = [lax.rem(mx + v, 4) * 2 for v in range(4)]
    part_y = [(lax.rem(lax.rem(my + v, 4), 2), lax.div(lax.rem(my + v, 4), 2) * 8) for v in range(4)]
    part_z = [lax.rem(mz + v, 4) * 2 + core for v in range(4)]

    def at(dx, dy, dz):
        return part_x[dx] + part_y[dy][0], part_y[dy][1] + part_z[dz]

    sibling = place(mx, my, mz, 1 - core)

    def send(src, dst, number, device):
        return pltpu.make_async_remote_copy(
            src_ref=src, dst_ref=dst, send_sem=send_sem.at[number], recv_sem=recv_sem.at[number],
            device_id=device, device_id_type=MESH)

    def apart(work):
        pl.when(core < 2)(work)

    barrier = pltpu.get_barrier_semaphore()
    pl.semaphore_signal(barrier, inc=1, device_id=sibling, device_id_type=MESH)
    for v in range(1, 4):
        for device in (at(0, 0, v), at(0, v, 0), at(v, 0, 0)):
            pl.semaphore_signal(barrier, inc=1, device_id=device, device_id_type=MESH)

    inputs = []
    for number, pair in enumerate(((spec_hbm, spec), (owner_hbm, owner), (bin_hbm, bins))):
        inputs.append(pltpu.make_async_copy(*pair, in_sem.at[number]))
        inputs[number].start()

    table_copies = []
    for side in range(2):
        here = pl.ds(pl.multiple_of(side * FREQS + core * HALF, HALF), HALF)
        table_copies.append(pltpu.make_async_copy(
            table_hbm.at[here], table.at[pl.ds(side * HALF, HALF)], table_sem.at[side]))
        table_copies[side].start()

    for copy in inputs:
        copy.wait()
    values = spec[...].astype(F32)
    real, imag = values[:, 0, :], values[:, 1, :]
    energy = real * real + imag * imag
    lane = lax.broadcasted_iota(jnp.int32, energy.shape, 1)
    smooth = energy
    for bit in (1, 2, 4):
        other = jnp.where((lane & bit) == 0, pltpu.roll(smooth, FREQS - bit, 1),
                          pltpu.roll(smooth, bit, 1))
        smooth = smooth + other
    smooth = smooth * 0.125
    level = jnp.sum(energy, axis=1, keepdims=True) * (1.0 / FREQS)
    row = lax.broadcasted_iota(jnp.int32, (CH, 1), 0)
    alive = jnp.where(row < live_ref[0], 1.0, 0.0).astype(F32)
    inverse = lax.rsqrt(smooth + 0.1 * level + 1e-06) * alive
    for side, values in enumerate((real, imag)):
        white = (values * inverse).astype(BF)
        for half in range(2):
            own[half, side] = white[:, half * HALF:(half + 1) * HALF]
    blocks[OWN, core] = own[core]
    codes[OWN, core] = owner[...] * BINS_DEV + bins[...]

    pl.semaphore_wait(barrier, 10)

    toward = {BACK: at(0, 0, 1), OPPOSITE: at(0, 0, 2), FLIP: at(0, 2, 0)}
    sib_copy = send(own.at[1 - core], blocks.at[OWN, core], S_SIB, sibling)
    sib_copy.start()
    code_copy = send(codes.at[OWN, core], codes.at[OWN, core], S_CODE, sibling)
    code_copy.start()

    def far_copy(r, j):
        q = core if j == 0 else 1 - core
        return send(blocks.at[OWN, q], blocks.at[r, q], S_FAR + 2 * (r - 1) + j, toward[r])

    def far_code(r):
        return send(codes.at[OWN], codes.at[r], S_CODE + r, toward[r])

    far_copy(FLIP, 0).start()
    far_copy(BACK, 0).start()
    sib_copy.wait_recv()
    for r, j in ((FLIP, 1), (BACK, 1), (OPPOSITE, 0), (OPPOSITE, 1)):
        far_copy(r, j).start()
    code_copy.wait_recv()
    for r in (FLIP, BACK, OPPOSITE):
        far_code(r).start()

    def offsets_of(code):
        owner = code // 64
        ox, oz, oc = owner // 32, owner // 2 % 4, owner % 2
        oy = owner // 8 % 2 * 2 + owner // 16 % 2
        return (ox - mx + 4) % 4, (oy - my + 4) % 4, (oz - mz + 4) % 4, oc

    def hits_of(code):
        dx, dy, dz, oc = offsets_of(code)
        whose = jnp.where(oc == core, dx * 32 + dy * 8 + dz, -1)
        down = lax.broadcasted_iota(jnp.int32, (128, 2048), 0)
        named = jnp.where(down == whose, 1.0, 0.0).astype(BF)
        binned = jnp.where(down == code % 64, 1.0, 0.0).astype(BF)
        return lax.dot_general(named, binned, (((1,), (1,)), ((), ())), preferred_element_type=F32)

    def copy_n(stage, v):
        spot = stage * 3 + v - 1
        if stage == 0:
            return send(tally.at[pl.ds(32 * v, 32)], got_n.at[spot], S_N + spot, at(v, 0, 0))
        if stage == 1:
            return send(tally.at[pl.ds(8 * v, 8)], got_n.at[spot, pl.ds(0, 8)], S_N + spot,
                        at(0, v, 0))
        return send(tally.at[pl.ds(0, 8)], got_n.at[spot, pl.ds(0, 8)], S_N + spot, at(0, 0, v))

    def tally_stage(stage):
        if stage > 0:
            rows_of = 32 if stage == 1 else 8
            total = tally[0:rows_of]
            for v in range(1, 4):
                copy_n(stage - 1, v).wait()
                total = total + got_n[(stage - 1) * 3 + v - 1, 0:rows_of]
            tally[0:rows_of] = total
        for v in range(1, 4):
            copy_n(stage, v).start()

    @apart
    def _():
        tally[...] = hits_of(codes[OWN, 0]) + hits_of(codes[OWN, 1])

    tally_stage(0)

    def pair_of(first, q, second, r, steps):
        return first, q, second, r, steps + q - r

    low = 1 - lax.div(mz + 3, 4)
    high = lax.div(mz, 2)

    def pick(flag, one, other):
        return flag * one + (1 - flag) * other

    near_first, near_second = pick(low, BACK, OWN), pick(low, OWN, BACK)
    cross_first, cross_second = pick(low, FLIP, BACK), pick(low, BACK, FLIP)
    far_first, far_second = pick(high, OWN, OPPOSITE), pick(high, OPPOSITE, OWN)
    flip_first, flip_second = pick(high, OPPOSITE, FLIP), pick(high, FLIP, OPPOSITE)
    pairs = (
        [pair_of(OWN, 0, FLIP, 0, 8), pair_of(OWN, 0, FLIP, 1, 8),
         pair_of(OWN, 1, FLIP, 1, 8), pair_of(OWN, 1, OWN, 0, 0)]
        + [pair_of(near_first, q, near_second, r, pick(low, 6, 2)) for q in (0, 1) for r in (0, 1)]
        + [pair_of(cross_first, q, cross_second, r, pick(low, 2, 6)) for q in (0, 1) for r in (0, 1)]
        + [pair_of(far_first, high, far_second, r, 4) for r in (0, 1)]
        + [pair_of(flip_first, high, flip_second, r, 4) for r in (0, 1)])

    def near(mate, far):
        q, r = pick(low, far, mate), pick(low, mate, far)
        return 4 + 2 * q + r, (near_first, q, near_second, r)

    def listed(number):
        return number, pairs[number][:4]

    runs = [
        [listed(3), (core, (OWN, 0, FLIP, core)), near(0, core), near(1, core)],
        [(1 - core, (OWN, 0, FLIP, 1 - core)), listed(2), near(0, 1 - core), near(1, 1 - core)],
        [listed(number) for number in range(8, 12)],
        [listed(number) for number in range(12, 16)],
    ]

    def form(slot, first, q, second, r):
        far_r, far_i = blocks[second, r, 0], blocks[second, r, 1]
        for i in range(CH):
            near_r = jnp.broadcast_to(blocks[first, q, 0, i:i + 1, :], (CH, HALF))
            near_i = jnp.broadcast_to(blocks[first, q, 1, i:i + 1, :], (CH, HALF))
            here = pl.ds(slot * 256 + i * CH, CH)
            cross[here, 0:HALF] = near_r * far_r + near_i * far_i
            cross[here, HALF:FREQS] = near_i * far_r - near_r * far_i

    def row_copy(number):
        return send(leaving.at[number], coming.at[number], S_ROWS + number, sibling)

    def correlate(run):
        @apart
        def _():
            for slot, (number, pair) in enumerate(run):
                form(slot, *pair)
            made = jnp.dot(cross[...], table[...], preferred_element_type=F32)
            for slot, (number, pair) in enumerate(run):
                here = made[slot * 256:(slot + 1) * 256]
                mine[number] = here
                leaving[number] = here.astype(BF)
        for number, pair in run:
            row_copy(number).start()

    def complete(begin, end):
        for number in range(begin, end):
            row_copy(number).wait_recv()

        @apart
        def _():
            for number in range(begin, end):
                total = mine[number] + coming[number].astype(F32)
                rows[number * 256:(number + 1) * 256] = total.astype(BF)

    for copy in table_copies:
        copy.wait()
    far_copy(FLIP, 0).wait_recv()
    far_copy(BACK, 0).wait_recv()
    correlate(runs[0])
    far_copy(FLIP, 1).wait_recv()
    far_copy(BACK, 1).wait_recv()
    correlate(runs[1])
    correlate(runs[2])
    tally_stage(1)
    far_copy(OPPOSITE, 0).wait_recv()
    far_copy(OPPOSITE, 1).wait_recv()
    correlate(runs[3])
    tally_stage(2)

    def place_of(code):
        slot = code % 64
        dx, dy, dz, oc = offsets_of(code)
        kind = slot // 16
        side = jnp.where(core == 0, dy, dx)
        axis = jnp.where(kind == 3, jnp.where(side == 3, 2, core), kind)
        first = jnp.where(kind == 3, side, jnp.where(kind == 0, dy, dx))
        along = jnp.where(axis == 0, dx, jnp.where(axis == 1, dy, dz))
        second = jnp.where(axis < 2, dz, jnp.where((kind == 3) & (core == 0), dx, dy))
        spot = (along * 4 + kind) * 256 + (first * 4 + second) * 16 + slot % 16
        return jnp.where(oc == core, spot, -1)

    for r in (FLIP, BACK, OPPOSITE):
        far_code(r).wait_recv()

    @apart
    def _():
        for number, (first, q, second, r, step) in enumerate(pairs):
            from_row = pl.multiple_of((step - 1) * 256, 256)
            spots[:, number * 256:(number + 1) * 256] = codes[first, q, :, pl.ds(from_row, 256)]
        spots[...] = place_of(spots[...])

    complete(0, 12)

    def device_of(kind, offsets):
        if kind < 3:
            return at(*offsets[kind])
        one, other = at(*offsets[3]), at(*offsets[4])
        return tuple(pick(core, b, a) for a, b in zip(one, other))

    pieces = [(0, 0, 256), (1, 256, 256), (2, 512, 256), (3, 768, 192), (3, 960, 64)]

    def copy_a(along, piece):
        kind, begin, count = pieces[piece]
        here = pl.ds(begin, count)
        x, y, z = (along, 0, 0), (0, along, 0), (0, 0, along)
        last = (z, z) if piece == 4 else (x, y)
        return send(dense.at[along, here], got_a.at[along, here], S_A + along * 5 + piece,
                    device_of(kind, (x, y, z) + last))

    def group_of(along, begin, end):
        down = lax.broadcasted_iota(jnp.int32, (1024, end - begin), 0)
        hot = jnp.where(down == spots[:, begin:end] - along * 1024, 1.0, 0.0).astype(BF)
        return jnp.dot(hot, rows[begin:end], preferred_element_type=F32)

    def send_group(along):
        for piece in range(5):
            copy_a(along, piece).start()

    @apart
    def _():
        own_sum[...] = group_of(2, 0, 3072)

    complete(12, 16)

    @apart
    def _():
        dense[2] = (own_sum[...] + group_of(2, 3072, 4096)).astype(BF)

    send_group(2)
    for along in (1, 3):
        @apart
        def _(along=along):
            dense[along] = group_of(along, 0, 4096).astype(BF)

        send_group(along)

    @apart
    def _():
        own_sum[...] = group_of(0, 0, 4096)

    def copy_b(kind, spot):
        first, second = spot // 4, spot % 4
        last = ((second, 3, 0), (3, second, 0)) if first == 3 else ((0, first, second), (first, 0, second))
        offsets = ((0, first, second), (first, 0, second), (first, second, 0)) + last
        return send(part.at[kind, spot], got_b.at[kind, spot], S_B + kind, device_of(kind, offsets))

    def all_b(kind):
        rest = pl.ds(1, 15)
        return send(part.at[kind, rest], got_b.at[kind, rest], S_B + kind, sibling)

    for kind in range(4):
        for along in (2, 1, 3):
            copy_a(along, kind).wait_recv()
            if kind == 3:
                copy_a(along, 4).wait_recv()

        @apart
        def _(kind=kind):
            here = pl.ds(kind * 256, 256)
            total = own_sum[here]
            for along in (2, 1, 3):
                total = total + got_a[along, here].astype(F32)
            part[kind] = total.astype(BF).reshape(16, 16, LAGS)

        for spot in range(1, 16):
            copy_b(kind, spot).start()

    count = tally[0:1]
    for v in range(1, 4):
        copy_n(2, v).wait()
        count = count + got_n[5 + v, v:v + 1]
    shape = (BINS_DEV, 128)
    diagonal = lax.broadcasted_iota(jnp.int32, shape, 0) == lax.broadcasted_iota(jnp.int32, shape, 1)
    count = jnp.sum(jnp.where(diagonal, count, 0.0), axis=1, keepdims=True)
    scale = lax.rsqrt(count + 1.0)

    sib_copy.wait_send()
    code_copy.wait_send()
    for r in (FLIP, BACK, OPPOSITE):
        far_code(r).wait_send()
        for j in range(2):
            far_copy(r, j).wait_send()
    for number in range(16):
        row_copy(number).wait_send()
    for along in range(1, 4):
        for piece in range(5):
            copy_a(along, piece).wait_send()

    for kind in range(4):
        all_b(kind).wait_recv()
        total = part[kind, 0].astype(F32)
        for spot in range(1, 16):
            total = total + got_b[kind, spot].astype(F32)
        out_ref[kind * 16:(kind + 1) * 16, :] = total * scale[kind * 16:(kind + 1) * 16]

    for kind in range(4):
        all_b(kind).wait_send()


def stacks(spectra, live_count, owner, slot, table):
    vmem, anywhere = pl.BlockSpec(memory_space=pltpu.VMEM), pl.BlockSpec(memory_space=pl.ANY)
    return pl.pallas_call(
        kernel,
        out_shape=jax.ShapeDtypeStruct((BINS_DEV, LAGS), F32),
        in_specs=[anywhere, pl.BlockSpec(memory_space=pltpu.SMEM), anywhere, anywhere, anywhere],
        out_specs=vmem,
        scratch_shapes=[
            pltpu.VMEM((CH, 2, FREQS), BF),
            pltpu.VMEM((1, 2048), jnp.int32),
            pltpu.VMEM((1, 2048), jnp.int32),
            pltpu.VMEM((2, 2, CH, HALF), BF),
            pltpu.VMEM((4, 2, 2, CH, HALF), BF),
            pltpu.VMEM((FREQS, LAGS), BF),
            pltpu.VMEM((1024, FREQS), BF),
            pltpu.VMEM((4, 2, 1, 2048), jnp.int32),
            pltpu.VMEM((1, 4096), jnp.int32),
            pltpu.VMEM((16, 256, LAGS), F32),
            pltpu.VMEM((16, 256, LAGS), BF),
            pltpu.VMEM((16, 256, LAGS), BF),
            pltpu.VMEM((4096, LAGS), BF),
            pltpu.VMEM((1024, LAGS), F32),
            pltpu.VMEM((4, 1024, LAGS), BF),
            pltpu.VMEM((4, 1024, LAGS), BF),
            pltpu.VMEM((4, 16, 16, LAGS), BF),
            pltpu.VMEM((4, 16, 16, LAGS), BF),
            pltpu.VMEM((128, 128), F32),
            pltpu.VMEM((9, 32, 128), F32),
            pltpu.SemaphoreType.DMA((N_SEM,)),
            pltpu.SemaphoreType.DMA((N_SEM,)),
            pltpu.SemaphoreType.DMA((2,)),
            pltpu.SemaphoreType.DMA((3,)),
        ],
        compiler_params=pltpu.CompilerParams(
            collective_id=0, has_side_effects=True, vmem_limit_bytes=56 * 1024 * 1024),
        cost_estimate=pl.CostEstimate(
            flops=13_000_000_000, bytes_accessed=4_000_000, transcendentals=40_000),
    )(spectra, live_count, owner, slot, table)


def on_device(spectra, live_count, owner_list, bin_list):
    table = jnp.asarray(table_constant(FREQS, LAGS))
    return stacks(spectra, live_count, owner_list.reshape(1, -1), bin_list.reshape(1, -1), table)


def solution(mesh):
    return jax.shard_map(
        on_device,
        mesh=mesh,
        in_specs=(
            P(("group", "blk"), None, None),
            P(("group", "blk")),
            P(("group", "blk"), None),
            P(("group", "blk")),
        ),
        out_specs=P(("group", "blk"), None),
        check_vma=False,
    )
```

```python
import functools
import math

import jax
import jax.numpy as jnp
import numpy as np
from jax import lax
from jax.experimental import pallas as pl
from jax.experimental.pallas import tpu as pltpu
from jax.sharding import PartitionSpec as P

CH = 16
FREQS = 2048
LAGS = 256
BINS_DEV = 64
MESH = pl.DeviceIdType.MESH
BF = jnp.bfloat16
F32 = jnp.float32

S_SIB, S_FAR, S_CODE, S_ROWS, S_N, S_A, S_B = 0, 1, 7, 11, 27, 36, 66
N_SEM = S_B + 8
OWN, BACK, OPPOSITE, FLIP = 0, 1, 2, 3
HALF = FREQS // 2


def table_constant(width, lag_count):
    frequency = np.arange(width, dtype=np.int32)
    lag_offset = np.arange(lag_count, dtype=np.int32) - lag_count // 2
    product = frequency[:, None] * lag_offset[None, :] % (2 * width)
    angles = product.astype(np.float32) * np.float32(math.pi / width)
    norm = np.float32(1.0 / math.sqrt(width))
    whole = np.concatenate([np.cos(angles), -np.sin(angles)], axis=0) * norm
    return whole.astype(jnp.bfloat16)


def place(x, y, z, core):
    return (x * 2 + lax.rem(y, 2), lax.div(y, 2) * 8 + z * 2 + core)


def kernel(spec_hbm, live_ref, owner_hbm, bin_hbm, table_hbm, out_ref, spec, owner, bins, own, blocks, table, cross,
           codes, spots, mine, leaving, coming, rows, early, own_sum, dense, got_a, part, got_b, tally, got_n,
           send_sem, recv_sem, table_sem, in_sem):
    group, blk = lax.axis_index("group"), lax.axis_index("blk")
    mx, core = lax.div(group, 2), lax.rem(blk, 2)
    my = lax.div(blk, 8) * 2 + lax.rem(group, 2)
    mz = lax.rem(lax.div(blk, 2), 4)

    part_x = [lax.rem(mx + v, 4) * 2 for v in range(4)]
    part_y = [(lax.rem(lax.rem(my + v, 4), 2), lax.div(lax.rem(my + v, 4), 2) * 8) for v in range(4)]
    part_z = [lax.rem(mz + v, 4) * 2 + core for v in range(4)]

    def at(dx, dy, dz):
        return part_x[dx] + part_y[dy][0], part_y[dy][1] + part_z[dz]

    sibling = place(mx, my, mz, 1 - core)

    def send(src, dst, number, device):
        return pltpu.make_async_remote_copy(
            src_ref=src, dst_ref=dst, send_sem=send_sem.at[number], recv_sem=recv_sem.at[number],
            device_id=device, device_id_type=MESH)

    def apart(work):
        pl.when(core < 2)(work)

    barrier = pltpu.get_barrier_semaphore()
    pl.semaphore_signal(barrier, inc=1, device_id=sibling, device_id_type=MESH)
    for v in range(1, 4):
        for device in (at(0, 0, v), at(0, v, 0), at(v, 0, 0)):
            pl.semaphore_signal(barrier, inc=1, device_id=device, device_id_type=MESH)

    inputs = []
    for number, pair in enumerate(((spec_hbm, spec), (owner_hbm, owner), (bin_hbm, bins))):
        inputs.append(pltpu.make_async_copy(*pair, in_sem.at[number]))
        inputs[number].start()

    table_copies = []
    for side in range(2):
        here = pl.ds(pl.multiple_of(side * FREQS + core * HALF, HALF), HALF)
        table_copies.append(pltpu.make_async_copy(
            table_hbm.at[here], table.at[pl.ds(side * HALF, HALF)], table_sem.at[side]))
        table_copies[side].start()

    for copy in inputs:
        copy.wait()
    values = spec[...].astype(F32)
    real, imag = values[:, 0, :], values[:, 1, :]
    energy = real * real + imag * imag
    lane = lax.broadcasted_iota(jnp.int32, energy.shape, 1)
    smooth = energy
    for bit in (1, 2, 4):
        other = jnp.where((lane & bit) == 0, pltpu.roll(smooth, FREQS - bit, 1),
                          pltpu.roll(smooth, bit, 1))
        smooth = smooth + other
    smooth = smooth * 0.125
    level = jnp.sum(energy, axis=1, keepdims=True) * (1.0 / FREQS)
    row = lax.broadcasted_iota(jnp.int32, (CH, 1), 0)
    alive = jnp.where(row < live_ref[0], 1.0, 0.0).astype(F32)
    inverse = lax.rsqrt(smooth + 0.1 * level + 1e-06) * alive
    for side, values in enumerate((real, imag)):
        white = (values * inverse).astype(BF)
        for half in range(2):
            own[half, side] = white[:, half * HALF:(half + 1) * HALF]
    blocks[OWN, core] = own[core]
    codes[OWN, core] = owner[...] * BINS_DEV + bins[...]

    pl.semaphore_wait(barrier, 10)

    toward = {BACK: at(0, 0, 1), OPPOSITE: at(0, 0, 2), FLIP: at(0, 2, 0)}
    sib_copy = send(own.at[1 - core], blocks.at[OWN, core], S_SIB, sibling)
    sib_copy.start()
    code_copy = send(codes.at[OWN, core], codes.at[OWN, core], S_CODE, sibling)
    code_copy.start()

    def far_copy(r, j):
        q = core if j == 0 else 1 - core
        return send(blocks.at[OWN, q], blocks.at[r, q], S_FAR + 2 * (r - 1) + j, toward[r])

    def far_code(r):
        return send(codes.at[OWN], codes.at[r], S_CODE + r, toward[r])

    far_copy(FLIP, 0).start()
    far_copy(BACK, 0).start()
    sib_copy.wait_recv()
    for r in (FLIP, BACK):
        far_copy(r, 1).start()
    code_copy.wait_recv()
    for r in (FLIP, BACK, OPPOSITE):
        far_code(r).start()

    def offsets_of(code):
        owner = code // 64
        ox, oz, oc = owner // 32, owner // 2 % 4, owner % 2
        oy = owner // 8 % 2 * 2 + owner // 16 % 2
        return (ox - mx + 4) % 4, (oy - my + 4) % 4, (oz - mz + 4) % 4, oc

    def hits_of(code):
        dx, dy, dz, oc = offsets_of(code)
        whose = jnp.where(oc == core, dx * 32 + dy * 8 + dz, -1)
        down = lax.broadcasted_iota(jnp.int32, (128, 2048), 0)
        named = jnp.where(down == whose, 1.0, 0.0).astype(BF)
        binned = jnp.where(down == code % 64, 1.0, 0.0).astype(BF)
        return lax.dot_general(named, binned, (((1,), (1,)), ((), ())), preferred_element_type=F32)

    def copy_n(stage, v):
        spot = stage * 3 + v - 1
        if stage == 0:
            return send(tally.at[pl.ds(32 * v, 32)], got_n.at[spot], S_N + spot, at(v, 0, 0))
        if stage == 1:
            return send(tally.at[pl.ds(8 * v, 8)], got_n.at[spot, pl.ds(0, 8)], S_N + spot,
                        at(0, v, 0))
        return send(tally.at[pl.ds(0, 8)], got_n.at[spot, pl.ds(0, 8)], S_N + spot, at(0, 0, v))

    def tally_stage(stage):
        if stage > 0:
            rows_of = 32 if stage == 1 else 8
            total = tally[0:rows_of]
            for v in range(1, 4):
                copy_n(stage - 1, v).wait()
                total = total + got_n[(stage - 1) * 3 + v - 1, 0:rows_of]
            tally[0:rows_of] = total
        for v in range(1, 4):
            copy_n(stage, v).start()

    @apart
    def _():
        tally[...] = hits_of(codes[OWN, 0]) + hits_of(codes[OWN, 1])

    far_copy(BACK, 1).wait_send()
    for j in range(2):
        far_copy(OPPOSITE, j).start()
    tally_stage(0)

    def pair_of(first, q, second, r, steps):
        return first, q, second, r, steps + q - r

    low = 1 - lax.div(mz + 3, 4)
    high = lax.div(mz, 2)

    def pick(flag, one, other):
        return flag * one + (1 - flag) * other

    near_first, near_second = pick(low, BACK, OWN), pick(low, OWN, BACK)
    cross_first, cross_second = pick(low, FLIP, BACK), pick(low, BACK, FLIP)
    far_first, far_second = pick(high, OWN, OPPOSITE), pick(high, OPPOSITE, OWN)
    flip_first, flip_second = pick(high, OPPOSITE, FLIP), pick(high, FLIP, OPPOSITE)
    pairs = (
        [pair_of(OWN, 0, FLIP, 0, 8), pair_of(OWN, 0, FLIP, 1, 8),
         pair_of(OWN, 1, FLIP, 1, 8), pair_of(OWN, 1, OWN, 0, 0)]
        + [pair_of(near_first, q, near_second, r, pick(low, 6, 2)) for q in (0, 1) for r in (0, 1)]
        + [pair_of(cross_first, q, cross_second, r, pick(low, 2, 6)) for q in (0, 1) for r in (0, 1)]
        + [pair_of(far_first, high, far_second, r, 4) for r in (0, 1)]
        + [pair_of(flip_first, high, flip_second, r, 4) for r in (0, 1)])

    def near(mate, far):
        q, r = pick(low, far, mate), pick(low, mate, far)
        return 4 + 2 * q + r, (near_first, q, near_second, r)

    def listed(number):
        return number, pairs[number][:4]

    runs = [
        [listed(3), (core, (OWN, 0, FLIP, core)), near(0, core), near(1, core)],
        [(1 - core, (OWN, 0, FLIP, 1 - core)), listed(2), near(0, 1 - core), near(1, 1 - core)],
        [listed(number) for number in range(8, 12)],
        [listed(number) for number in range(12, 16)],
    ]

    def form(slot, first, q, second, r):
        far_r, far_i = blocks[second, r, 0], blocks[second, r, 1]
        for i in range(CH):
            near_r = jnp.broadcast_to(blocks[first, q, 0, i:i + 1, :], (CH, HALF))
            near_i = jnp.broadcast_to(blocks[first, q, 1, i:i + 1, :], (CH, HALF))
            here = pl.ds(slot * 256 + i * CH, CH)
            cross[here, 0:HALF] = near_r * far_r + near_i * far_i
            cross[here, HALF:FREQS] = near_i * far_r - near_r * far_i

    def row_copy(number):
        return send(leaving.at[number], coming.at[number], S_ROWS + number, sibling)

    def correlate(run):
        @apart
        def _():
            for slot, (number, pair) in enumerate(run):
                form(slot, *pair)
            made = jnp.dot(cross[...], table[...], preferred_element_type=F32)
            for slot, (number, pair) in enumerate(run):
                here = made[slot * 256:(slot + 1) * 256]
                mine[number] = here
                leaving[number] = here.astype(BF)
        for number, pair in run:
            row_copy(number).start()

    def complete(begin, end):
        for number in range(begin, end):
            row_copy(number).wait_recv()

        @apart
        def _():
            for number in range(begin, end):
                total = mine[number] + coming[number].astype(F32)
                rows[number * 256:(number + 1) * 256] = total.astype(BF)

    for copy in table_copies:
        copy.wait()
    far_copy(FLIP, 0).wait_recv()
    far_copy(BACK, 0).wait_recv()
    correlate(runs[0])
    far_copy(FLIP, 1).wait_recv()
    far_copy(BACK, 1).wait_recv()
    correlate(runs[1])
    correlate(runs[2])
    tally_stage(1)
    far_copy(OPPOSITE, 0).wait_recv()
    far_copy(OPPOSITE, 1).wait_recv()
    correlate(runs[3])
    tally_stage(2)

    def place_of(code):
        slot = code % 64
        dx, dy, dz, oc = offsets_of(code)
        kind = slot // 16
        side = jnp.where(core == 0, dy, dx)
        axis = jnp.where(kind == 3, jnp.where(side == 3, 2, core), kind)
        first = jnp.where(kind == 3, side, jnp.where(kind == 0, dy, dx))
        along = jnp.where(axis == 0, dx, jnp.where(axis == 1, dy, dz))
        second = jnp.where(axis < 2, dz, jnp.where((kind == 3) & (core == 0), dx, dy))
        spot = first // 2 * 2048 + (along * 4 + kind) * 128 + (first % 2 * 4 + second) * 16 + slot % 16
        return jnp.where(oc == core, spot, -1)

    for r in (FLIP, BACK, OPPOSITE):
        far_code(r).wait_recv()

    @apart
    def _():
        for number, (first, q, second, r, step) in enumerate(pairs):
            from_row = pl.multiple_of((step - 1) * 256, 256)
            spots[:, number * 256:(number + 1) * 256] = codes[first, q, :, pl.ds(from_row, 256)]
        spots[...] = place_of(spots[...])

    complete(0, 12)

    def device_of(kind, offsets):
        if kind < 3:
            return at(*offsets[kind])
        one, other = at(*offsets[3]), at(*offsets[4])
        return tuple(pick(core, b, a) for a, b in zip(one, other))

    pieces = [[(0, 0, 128), (1, 128, 128), (2, 256, 128), (3, 384, 128)],
              [(0, 0, 128), (1, 128, 128), (2, 256, 128), (3, 384, 64), (3, 448, 64)]]

    def copy_a(half, along, piece):
        kind, begin, count = pieces[half][piece]
        here = pl.ds(begin, count)
        x, y, z = (along, 0, 0), (0, along, 0), (0, 0, along)
        last = (z, z) if piece == 4 else (x, y)
        return send(dense.at[half, along, here], got_a.at[half, along, here],
                    S_A + (half * 3 + along - 1) * 5 + piece, device_of(kind, (x, y, z) + last))

    def group_of(half, along, begin, end):
        down = lax.broadcasted_iota(jnp.int32, (512, end - begin), 0)
        hot = jnp.where(down == spots[:, begin:end] - (half * 4 + along) * 512, 1.0, 0.0).astype(BF)
        return jnp.dot(hot, rows[begin:end], preferred_element_type=F32)

    def send_group(half, along):
        for piece in range(len(pieces[half])):
            copy_a(half, along, piece).start()

    @apart
    def _():
        early[0] = group_of(0, 2, 0, 3072)
        early[1] = group_of(0, 1, 0, 3072)

    complete(12, 16)
    for half, along in ((0, 2), (0, 1), (0, 3), (1, 2), (1, 1), (1, 3)):
        @apart
        def _(half=half, along=along):
            if half == 0 and along < 3:
                total = early[2 - along] + group_of(half, along, 3072, 4096)
            else:
                total = group_of(half, along, 0, 4096)
            dense[half, along] = total.astype(BF)

        send_group(half, along)

    @apart
    def _():
        for half in range(2):
            own_sum[half] = group_of(half, 0, 0, 4096)

    def copy_b(kind, spot):
        first, second = spot // 4, spot % 4
        last = ((second, 3, 0), (3, second, 0)) if first == 3 else ((0, first, second), (first, 0, second))
        offsets = ((0, first, second), (first, 0, second), (first, second, 0)) + last
        return send(part.at[kind, spot], got_b.at[kind, spot], S_B + kind * 2 + spot // 8,
                    device_of(kind, offsets))

    def all_b(kind, half):
        here = pl.ds(1, 7) if half == 0 else pl.ds(8, 8)
        return send(part.at[kind, here], got_b.at[kind, here], S_B + kind * 2 + half, sibling)

    for half in range(2):
        for along in (2, 1, 3):
            for piece in range(len(pieces[half])):
                copy_a(half, along, piece).wait_recv()

        @apart
        def _(half=half):
            total = own_sum[half]
            for along in (2, 1, 3):
                total = total + got_a[half, along].astype(F32)
            total = total.astype(BF)
            for kind in range(4):
                here = total[kind * 128:(kind + 1) * 128]
                part[kind, half * 8:half * 8 + 8] = here.reshape(8, 16, LAGS)

        for spot in range(half * 8, half * 8 + 8):
            for kind in range(4):
                if spot:
                    copy_b(kind, spot).start()

    count = tally[0:1]
    for v in range(1, 4):
        copy_n(2, v).wait()
        count = count + got_n[5 + v, v:v + 1]
    shape = (BINS_DEV, 128)
    diagonal = lax.broadcasted_iota(jnp.int32, shape, 0) == lax.broadcasted_iota(jnp.int32, shape, 1)
    count = jnp.sum(jnp.where(diagonal, count, 0.0), axis=1, keepdims=True)
    scale = lax.rsqrt(count + 1.0)

    sib_copy.wait_send()
    code_copy.wait_send()
    for r in (FLIP, BACK, OPPOSITE):
        far_code(r).wait_send()
        for j in range(2):
            if (r, j) != (BACK, 1):
                far_copy(r, j).wait_send()
    for number in range(16):
        row_copy(number).wait_send()
    for half in range(2):
        for along in range(1, 4):
            for piece in range(len(pieces[half])):
                copy_a(half, along, piece).wait_send()

    def gather(half):
        for kind in range(4):
            all_b(kind, half).wait_recv()

        @apart
        def _():
            for kind in range(4):
                here = pl.ds(kind * 16, 16)
                total = part[kind, 0].astype(F32) if half == 0 else out_ref[here]
                for spot in range(half * 8, half * 8 + 8):
                    if spot:
                        total = total + got_b[kind, spot].astype(F32)
                out_ref[here] = total if half == 0 else total * scale[kind * 16:(kind + 1) * 16]

    for half in range(2):
        gather(half)
    for half in range(2):
        for kind in range(4):
            all_b(kind, half).wait_send()


def stacks(spectra, live_count, owner, slot, table):
    vmem, anywhere = pl.BlockSpec(memory_space=pltpu.VMEM), pl.BlockSpec(memory_space=pl.ANY)
    return pl.pallas_call(
        kernel,
        out_shape=jax.ShapeDtypeStruct((BINS_DEV, LAGS), F32),
        in_specs=[anywhere, pl.BlockSpec(memory_space=pltpu.SMEM), anywhere, anywhere, anywhere],
        out_specs=vmem,
        scratch_shapes=[
            pltpu.VMEM((CH, 2, FREQS), BF),
            pltpu.VMEM((1, 2048), jnp.int32),
            pltpu.VMEM((1, 2048), jnp.int32),
            pltpu.VMEM((2, 2, CH, HALF), BF),
            pltpu.VMEM((4, 2, 2, CH, HALF), BF),
            pltpu.VMEM((FREQS, LAGS), BF),
            pltpu.VMEM((1024, FREQS), BF),
            pltpu.VMEM((4, 2, 1, 2048), jnp.int32),
            pltpu.VMEM((1, 4096), jnp.int32),
            pltpu.VMEM((16, 256, LAGS), F32),
            pltpu.VMEM((16, 256, LAGS), BF),
            pltpu.VMEM((16, 256, LAGS), BF),
            pltpu.VMEM((4096, LAGS), BF),
            pltpu.VMEM((2, 512, LAGS), F32),
            pltpu.VMEM((2, 512, LAGS), F32),
            pltpu.VMEM((2, 4, 512, LAGS), BF),
            pltpu.VMEM((2, 4, 512, LAGS), BF),
            pltpu.VMEM((4, 16, 16, LAGS), BF),
            pltpu.VMEM((4, 16, 16, LAGS), BF),
            pltpu.VMEM((128, 128), F32),
            pltpu.VMEM((9, 32, 128), F32),
            pltpu.SemaphoreType.DMA((N_SEM,)),
            pltpu.SemaphoreType.DMA((N_SEM,)),
            pltpu.SemaphoreType.DMA((2,)),
            pltpu.SemaphoreType.DMA((3,)),
        ],
        compiler_params=pltpu.CompilerParams(
            collective_id=0, has_side_effects=True, vmem_limit_bytes=56 * 1024 * 1024),
        cost_estimate=pl.CostEstimate(
            flops=13_000_000_000, bytes_accessed=4_000_000, transcendentals=40_000),
    )(spectra, live_count, owner, slot, table)


def on_device(spectra, live_count, owner_list, bin_list):
    table = jnp.asarray(table_constant(FREQS, LAGS))
    return stacks(spectra, live_count, owner_list.reshape(1, -1), bin_list.reshape(1, -1), table)


def solution(mesh):
    return jax.shard_map(
        on_device,
        mesh=mesh,
        in_specs=(
            P(("group", "blk"), None, None),
            P(("group", "blk")),
            P(("group", "blk"), None),
            P(("group", "blk")),
        ),
        out_specs=P(("group", "blk"), None),
        check_vma=False,
    )
```

```python
import functools
import math

import jax
import jax.numpy as jnp
import numpy as np
from jax import lax
from jax.experimental import pallas as pl
from jax.experimental.pallas import tpu as pltpu
from jax.sharding import PartitionSpec as P

CH = 16
FREQS = 2048
LAGS = 256
BINS_DEV = 64
MESH = pl.DeviceIdType.MESH
BF = jnp.bfloat16
F32 = jnp.float32

S_SIB, S_FAR, S_CODE, S_ROWS, S_N, S_A, S_B = 0, 1, 7, 11, 27, 36, 66
N_SEM = S_B + 8
OWN, BACK, OPPOSITE, FLIP = 0, 1, 2, 3
HALF = FREQS // 2


def table_constant(width, lag_count):
    frequency = np.arange(width, dtype=np.int32)
    lag_offset = np.arange(lag_count, dtype=np.int32) - lag_count // 2
    product = frequency[:, None] * lag_offset[None, :] % (2 * width)
    angles = product.astype(np.float32) * np.float32(math.pi / width)
    norm = np.float32(1.0 / math.sqrt(width))
    whole = np.concatenate([np.cos(angles), -np.sin(angles)], axis=0) * norm
    return whole.astype(jnp.bfloat16)


def place(x, y, z, core):
    return (x * 2 + lax.rem(y, 2), lax.div(y, 2) * 8 + z * 2 + core)


def kernel(spec_hbm, live_ref, owner_hbm, bin_hbm, table_hbm, out_ref, spec, owner, bins, own, blocks, table, cross,
           codes, spots, mine, leaving, coming, rows, early, own_sum, dense, got_a, part, got_b, tally, got_n,
           send_sem, recv_sem, table_sem, in_sem):
    group, blk = lax.axis_index("group"), lax.axis_index("blk")
    mx, core = lax.div(group, 2), lax.rem(blk, 2)
    my = lax.div(blk, 8) * 2 + lax.rem(group, 2)
    mz = lax.rem(lax.div(blk, 2), 4)

    part_x = [lax.rem(mx + v, 4) * 2 for v in range(4)]
    part_y = [(lax.rem(lax.rem(my + v, 4), 2), lax.div(lax.rem(my + v, 4), 2) * 8) for v in range(4)]
    part_z = [lax.rem(mz + v, 4) * 2 + core for v in range(4)]

    def at(dx, dy, dz):
        return part_x[dx] + part_y[dy][0], part_y[dy][1] + part_z[dz]

    sibling = place(mx, my, mz, 1 - core)

    def send(src, dst, number, device):
        return pltpu.make_async_remote_copy(
            src_ref=src, dst_ref=dst, send_sem=send_sem.at[number], recv_sem=recv_sem.at[number],
            device_id=device, device_id_type=MESH)

    def apart(work):
        pl.when(core < 2)(work)

    barrier = pltpu.get_barrier_semaphore()
    pl.semaphore_signal(barrier, inc=1, device_id=sibling, device_id_type=MESH)
    for v in range(1, 4):
        for device in (at(0, 0, v), at(0, v, 0), at(v, 0, 0)):
            pl.semaphore_signal(barrier, inc=1, device_id=device, device_id_type=MESH)

    inputs = []
    for number, pair in enumerate(((spec_hbm, spec), (owner_hbm, owner), (bin_hbm, bins))):
        inputs.append(pltpu.make_async_copy(*pair, in_sem.at[number]))
        inputs[number].start()

    table_copies = []
    for side in range(2):
        here = pl.ds(pl.multiple_of(side * FREQS + core * HALF, HALF), HALF)
        table_copies.append(pltpu.make_async_copy(
            table_hbm.at[here], table.at[pl.ds(side * HALF, HALF)], table_sem.at[side]))
        table_copies[side].start()

    for copy in inputs:
        copy.wait()
    values = spec[...].astype(F32)
    real, imag = values[:, 0, :], values[:, 1, :]
    energy = real * real + imag * imag
    lane = lax.broadcasted_iota(jnp.int32, energy.shape, 1)
    smooth = energy
    for bit in (1, 2, 4):
        other = jnp.where((lane & bit) == 0, pltpu.roll(smooth, FREQS - bit, 1),
                          pltpu.roll(smooth, bit, 1))
        smooth = smooth + other
    smooth = smooth * 0.125
    level = jnp.sum(energy, axis=1, keepdims=True) * (1.0 / FREQS)
    row = lax.broadcasted_iota(jnp.int32, (CH, 1), 0)
    alive = jnp.where(row < live_ref[0], 1.0, 0.0).astype(F32)
    inverse = lax.rsqrt(smooth + 0.1 * level + 1e-06) * alive
    for side, values in enumerate((real, imag)):
        white = (values * inverse).astype(BF)
        for half in range(2):
            own[half, side] = white[:, half * HALF:(half + 1) * HALF]
    blocks[OWN, core] = own[core]
    codes[OWN, core] = owner[...] * BINS_DEV + bins[...]

    pl.semaphore_wait(barrier, 10)

    toward = {BACK: at(0, 0, 1), OPPOSITE: at(0, 0, 2), FLIP: at(0, 2, 0)}
    sib_copy = send(own.at[1 - core], blocks.at[OWN, core], S_SIB, sibling)
    sib_copy.start()
    code_copy = send(codes.at[OWN, core], codes.at[OWN, core], S_CODE, sibling)
    code_copy.start()

    def far_copy(r, j):
        q = core if j == 0 else 1 - core
        return send(blocks.at[OWN, q], blocks.at[r, q], S_FAR + 2 * (r - 1) + j, toward[r])

    def far_code(r):
        return send(codes.at[OWN], codes.at[r], S_CODE + r, toward[r])

    far_copy(FLIP, 0).start()
    far_copy(BACK, 0).start()
    sib_copy.wait_recv()
    for r in (FLIP, BACK):
        far_copy(r, 1).start()
    code_copy.wait_recv()
    for r in (FLIP, BACK, OPPOSITE):
        far_code(r).start()

    def offsets_of(code):
        owner = code // 64
        ox, oz, oc = owner // 32, owner // 2 % 4, owner % 2
        oy = owner // 8 % 2 * 2 + owner // 16 % 2
        return (ox - mx + 4) % 4, (oy - my + 4) % 4, (oz - mz + 4) % 4, oc

    def hits_of(code):
        dx, dy, dz, oc = offsets_of(code)
        whose = jnp.where(oc == core, dx * 32 + dy * 8 + dz, -1)
        down = lax.broadcasted_iota(jnp.int32, (128, 2048), 0)
        named = jnp.where(down == whose, 1.0, 0.0).astype(BF)
        binned = jnp.where(down == code % 64, 1.0, 0.0).astype(BF)
        return lax.dot_general(named, binned, (((1,), (1,)), ((), ())), preferred_element_type=F32)

    def copy_n(stage, v):
        spot = stage * 3 + v - 1
        if stage == 0:
            return send(tally.at[pl.ds(32 * v, 32)], got_n.at[spot], S_N + spot, at(v, 0, 0))
        if stage == 1:
            return send(tally.at[pl.ds(8 * v, 8)], got_n.at[spot, pl.ds(0, 8)], S_N + spot,
                        at(0, v, 0))
        return send(tally.at[pl.ds(0, 8)], got_n.at[spot, pl.ds(0, 8)], S_N + spot, at(0, 0, v))

    def tally_stage(stage):
        if stage > 0:
            rows_of = 32 if stage == 1 else 8
            total = tally[0:rows_of]
            for v in range(1, 4):
                copy_n(stage - 1, v).wait()
                total = total + got_n[(stage - 1) * 3 + v - 1, 0:rows_of]
            tally[0:rows_of] = total
        for v in range(1, 4):
            copy_n(stage, v).start()

    @apart
    def _():
        tally[...] = hits_of(codes[OWN, 0]) + hits_of(codes[OWN, 1])

    far_copy(BACK, 1).wait_send()
    for j in range(2):
        far_copy(OPPOSITE, j).start()
    tally_stage(0)

    def pair_of(first, q, second, r, steps):
        return first, q, second, r, steps + q - r

    low = 1 - lax.div(mz + 3, 4)
    high = lax.div(mz, 2)

    def pick(flag, one, other):
        return flag * one + (1 - flag) * other

    near_first, near_second = pick(low, BACK, OWN), pick(low, OWN, BACK)
    cross_first, cross_second = pick(low, FLIP, BACK), pick(low, BACK, FLIP)
    far_first, far_second = pick(high, OWN, OPPOSITE), pick(high, OPPOSITE, OWN)
    flip_first, flip_second = pick(high, OPPOSITE, FLIP), pick(high, FLIP, OPPOSITE)
    pairs = (
        [pair_of(OWN, 0, FLIP, 0, 8), pair_of(OWN, 0, FLIP, 1, 8),
         pair_of(OWN, 1, FLIP, 1, 8), pair_of(OWN, 1, OWN, 0, 0)]
        + [pair_of(near_first, q, near_second, r, pick(low, 6, 2)) for q in (0, 1) for r in (0, 1)]
        + [pair_of(cross_first, q, cross_second, r, pick(low, 2, 6)) for q in (0, 1) for r in (0, 1)]
        + [pair_of(far_first, high, far_second, r, 4) for r in (0, 1)]
        + [pair_of(flip_first, high, flip_second, r, 4) for r in (0, 1)])

    def near(mate, far):
        q, r = pick(low, far, mate), pick(low, mate, far)
        return 4 + 2 * q + r, (near_first, q, near_second, r)

    def listed(number):
        return number, pairs[number][:4]

    runs = [
        [listed(3), (core, (OWN, 0, FLIP, core)), near(0, core), near(1, core)],
        [(1 - core, (OWN, 0, FLIP, 1 - core)), listed(2), near(0, 1 - core), near(1, 1 - core)],
        [listed(number) for number in range(8, 12)],
        [listed(number) for number in (12, 13)],
        [listed(number) for number in (14, 15)],
    ]

    def form(slot, first, q, second, r):
        far_r, far_i = blocks[second, r, 0], blocks[second, r, 1]
        for i in range(CH):
            near_r = jnp.broadcast_to(blocks[first, q, 0, i:i + 1, :], (CH, HALF))
            near_i = jnp.broadcast_to(blocks[first, q, 1, i:i + 1, :], (CH, HALF))
            here = pl.ds(slot * 256 + i * CH, CH)
            cross[here, 0:HALF] = near_r * far_r + near_i * far_i
            cross[here, HALF:FREQS] = near_i * far_r - near_r * far_i

    def row_copy(number):
        return send(leaving.at[number], coming.at[number], S_ROWS + number, sibling)

    def correlate(run):
        @apart
        def _():
            for slot, (number, pair) in enumerate(run):
                form(slot, *pair)
            made = jnp.dot(cross[0:len(run) * 256], table[...], preferred_element_type=F32)
            for slot, (number, pair) in enumerate(run):
                here = made[slot * 256:(slot + 1) * 256]
                mine[number] = here
                leaving[number] = here.astype(BF)
        for number, pair in run:
            row_copy(number).start()

    def complete(begin, end):
        for number in range(begin, end):
            row_copy(number).wait_recv()

        @apart
        def _():
            for number in range(begin, end):
                total = mine[number] + coming[number].astype(F32)
                rows[number * 256:(number + 1) * 256] = total.astype(BF)

    for copy in table_copies:
        copy.wait()
    far_copy(FLIP, 0).wait_recv()
    far_copy(BACK, 0).wait_recv()
    correlate(runs[0])
    far_copy(FLIP, 1).wait_recv()
    far_copy(BACK, 1).wait_recv()
    correlate(runs[1])
    correlate(runs[2])
    tally_stage(1)
    far_copy(OPPOSITE, 0).wait_recv()
    far_copy(OPPOSITE, 1).wait_recv()
    correlate(runs[3])
    correlate(runs[4])
    tally_stage(2)

    def place_of(code):
        slot = code % 64
        dx, dy, dz, oc = offsets_of(code)
        kind = slot // 16
        side = jnp.where(core == 0, dy, dx)
        axis = jnp.where(kind == 3, jnp.where(side == 3, 2, core), kind)
        first = jnp.where(kind == 3, side, jnp.where(kind == 0, dy, dx))
        along = jnp.where(axis == 0, dx, jnp.where(axis == 1, dy, dz))
        second = jnp.where(axis < 2, dz, jnp.where((kind == 3) & (core == 0), dx, dy))
        spot = jnp.where(first < 3, (along * 4 + kind) * 192 + first * 64,
                         3072 + (along * 4 + kind) * 64) + second * 16 + slot % 16
        return jnp.where(oc == core, spot, -1)

    for r in (FLIP, BACK, OPPOSITE):
        far_code(r).wait_recv()

    @apart
    def _():
        for number, (first, q, second, r, step) in enumerate(pairs):
            from_row = pl.multiple_of((step - 1) * 256, 256)
            spots[:, number * 256:(number + 1) * 256] = codes[first, q, :, pl.ds(from_row, 256)]
        spots[...] = place_of(spots[...])

    complete(0, 12)

    def device_of(kind, offsets):
        if kind < 3:
            return at(*offsets[kind])
        one, other = at(*offsets[3]), at(*offsets[4])
        return tuple(pick(core, b, a) for a, b in zip(one, other))

    per_kind, begins = (192, 64), (0, 3072)

    def copy_a(part_of, along, kind):
        count = per_kind[part_of]
        here = pl.ds(part_of * 768 + kind * count, count)
        x, y, z = (along, 0, 0), (0, along, 0), (0, 0, along)
        last = (z, z) if part_of else (x, y)
        return send(dense.at[along, here], got_a.at[along, here],
                    S_A + (part_of * 3 + along - 1) * 4 + kind, device_of(kind, (x, y, z) + last))

    def group_of(part_of, along, begin, end):
        size = 4 * per_kind[part_of]
        down = lax.broadcasted_iota(jnp.int32, (size, end - begin), 0)
        hot = jnp.where(down == spots[:, begin:end] - (begins[part_of] + along * size), 1.0, 0.0)
        return jnp.dot(hot.astype(BF), rows[begin:end], preferred_element_type=F32)

    def rows_of(part_of):
        return pl.ds(0, 768) if part_of == 0 else pl.ds(768, 256)

    def send_group(part_of, along):
        for kind in range(4):
            copy_a(part_of, along, kind).start()

    @apart
    def _():
        early[0] = group_of(0, 2, 0, 3072)
        early[1] = group_of(0, 1, 0, 3072)

    complete(12, 16)
    for part_of, along in ((0, 2), (0, 1), (0, 3), (1, 2), (1, 1), (1, 3)):
        @apart
        def _(part_of=part_of, along=along):
            if part_of == 0 and along < 3:
                total = early[2 - along] + group_of(part_of, along, 3072, 4096)
            else:
                total = group_of(part_of, along, 0, 4096)
            dense[along, rows_of(part_of)] = total.astype(BF)

        send_group(part_of, along)

    @apart
    def _():
        for part_of in range(2):
            own_sum[rows_of(part_of)] = group_of(part_of, 0, 0, 4096)

    def copy_b(kind, spot):
        first, second = spot // 4, spot % 4
        last = ((second, 3, 0), (3, second, 0)) if first == 3 else ((0, first, second), (first, 0, second))
        offsets = ((0, first, second), (first, 0, second), (first, second, 0)) + last
        return send(part.at[kind, spot], got_b.at[kind, spot], S_B + kind * 2 + spot // 12,
                    device_of(kind, offsets))

    spots_of = (range(1, 12), range(12, 16))

    def all_b(kind, part_of):
        here = pl.ds(spots_of[part_of][0], len(spots_of[part_of]))
        return send(part.at[kind, here], got_b.at[kind, here], S_B + kind * 2 + part_of, sibling)

    for part_of in range(2):
        for along in (2, 1, 3):
            for kind in range(4):
                copy_a(part_of, along, kind).wait_recv()

        @apart
        def _(part_of=part_of):
            total = own_sum[rows_of(part_of)]
            for along in (2, 1, 3):
                total = total + got_a[along, rows_of(part_of)].astype(F32)
            total = total.astype(BF)
            count = per_kind[part_of]
            for kind in range(4):
                here = total[kind * count:(kind + 1) * count]
                part[kind, pl.ds(part_of * 12, count // 16)] = here.reshape(count // 16, 16, LAGS)

        for spot in spots_of[part_of]:
            for kind in range(4):
                copy_b(kind, spot).start()

    count = tally[0:1]
    for v in range(1, 4):
        copy_n(2, v).wait()
        count = count + got_n[5 + v, v:v + 1]
    shape = (BINS_DEV, 128)
    diagonal = lax.broadcasted_iota(jnp.int32, shape, 0) == lax.broadcasted_iota(jnp.int32, shape, 1)
    count = jnp.sum(jnp.where(diagonal, count, 0.0), axis=1, keepdims=True)
    scale = lax.rsqrt(count + 1.0)

    sib_copy.wait_send()
    code_copy.wait_send()
    for r in (FLIP, BACK, OPPOSITE):
        far_code(r).wait_send()
        for j in range(2):
            if (r, j) != (BACK, 1):
                far_copy(r, j).wait_send()
    for number in range(16):
        row_copy(number).wait_send()
    for part_of in range(2):
        for along in range(1, 4):
            for kind in range(4):
                copy_a(part_of, along, kind).wait_send()

    def gather(part_of):
        for kind in range(4):
            all_b(kind, part_of).wait_recv()

        @apart
        def _():
            for kind in range(4):
                here = pl.ds(kind * 16, 16)
                total = out_ref[here] if part_of else part[kind, 0].astype(F32)
                for spot in spots_of[part_of]:
                    total = total + got_b[kind, spot].astype(F32)
                out_ref[here] = total * scale[kind * 16:(kind + 1) * 16] if part_of else total

    for part_of in range(2):
        gather(part_of)
    for part_of in range(2):
        for kind in range(4):
            all_b(kind, part_of).wait_send()


def stacks(spectra, live_count, owner, slot, table):
    vmem, anywhere = pl.BlockSpec(memory_space=pltpu.VMEM), pl.BlockSpec(memory_space=pl.ANY)
    return pl.pallas_call(
        kernel,
        out_shape=jax.ShapeDtypeStruct((BINS_DEV, LAGS), F32),
        in_specs=[anywhere, pl.BlockSpec(memory_space=pltpu.SMEM), anywhere, anywhere, anywhere],
        out_specs=vmem,
        scratch_shapes=[
            pltpu.VMEM((CH, 2, FREQS), BF),
            pltpu.VMEM((1, 2048), jnp.int32),
            pltpu.VMEM((1, 2048), jnp.int32),
            pltpu.VMEM((2, 2, CH, HALF), BF),
            pltpu.VMEM((4, 2, 2, CH, HALF), BF),
            pltpu.VMEM((FREQS, LAGS), BF),
            pltpu.VMEM((1024, FREQS), BF),
            pltpu.VMEM((4, 2, 1, 2048), jnp.int32),
            pltpu.VMEM((1, 4096), jnp.int32),
            pltpu.VMEM((16, 256, LAGS), F32),
            pltpu.VMEM((16, 256, LAGS), BF),
            pltpu.VMEM((16, 256, LAGS), BF),
            pltpu.VMEM((4096, LAGS), BF),
            pltpu.VMEM((2, 768, LAGS), F32),
            pltpu.VMEM((1024, LAGS), F32),
            pltpu.VMEM((4, 1024, LAGS), BF),
            pltpu.VMEM((4, 1024, LAGS), BF),
            pltpu.VMEM((4, 16, 16, LAGS), BF),
            pltpu.VMEM((4, 16, 16, LAGS), BF),
            pltpu.VMEM((128, 128), F32),
            pltpu.VMEM((9, 32, 128), F32),
            pltpu.SemaphoreType.DMA((N_SEM,)),
            pltpu.SemaphoreType.DMA((N_SEM,)),
            pltpu.SemaphoreType.DMA((2,)),
            pltpu.SemaphoreType.DMA((3,)),
        ],
        compiler_params=pltpu.CompilerParams(
            collective_id=0, has_side_effects=True, vmem_limit_bytes=56 * 1024 * 1024),
        cost_estimate=pl.CostEstimate(
            flops=13_000_000_000, bytes_accessed=4_000_000, transcendentals=40_000),
    )(spectra, live_count, owner, slot, table)


def on_device(spectra, live_count, owner_list, bin_list):
    table = jnp.asarray(table_constant(FREQS, LAGS))
    return stacks(spectra, live_count, owner_list.reshape(1, -1), bin_list.reshape(1, -1), table)


def solution(mesh):
    return jax.shard_map(
        on_device,
        mesh=mesh,
        in_specs=(
            P(("group", "blk"), None, None),
            P(("group", "blk")),
            P(("group", "blk"), None),
            P(("group", "blk")),
        ),
        out_specs=P(("group", "blk"), None),
        check_vma=False,
    )
```

```python
import functools
import math

import jax
import jax.numpy as jnp
import numpy as np
from jax import lax
from jax.experimental import pallas as pl
from jax.experimental.pallas import tpu as pltpu
from jax.sharding import PartitionSpec as P

CH = 16
FREQS = 2048
LAGS = 256
BINS_DEV = 64
MESH = pl.DeviceIdType.MESH
BF = jnp.bfloat16
F32 = jnp.float32

S_SIB, S_FAR, S_CODE, S_ROWS, S_N, S_A, S_B = 0, 1, 7, 11, 27, 36, 81
N_SEM = S_B + 12
OWN, BACK, OPPOSITE, FLIP = 0, 1, 2, 3
HALF = FREQS // 2


def table_constant(width, lag_count):
    frequency = np.arange(width, dtype=np.int32)
    lag_offset = np.arange(lag_count, dtype=np.int32) - lag_count // 2
    product = frequency[:, None] * lag_offset[None, :] % (2 * width)
    angles = product.astype(np.float32) * np.float32(math.pi / width)
    norm = np.float32(1.0 / math.sqrt(width))
    whole = np.concatenate([np.cos(angles), -np.sin(angles)], axis=0) * norm
    return whole.astype(jnp.bfloat16)


def place(x, y, z, core):
    return (x * 2 + lax.rem(y, 2), lax.div(y, 2) * 8 + z * 2 + core)


def kernel(spec_hbm, live_ref, owner_hbm, bin_hbm, table_hbm, out_ref, spec, owner, bins, own, blocks, table, cross,
           codes, spots, mine, leaving, coming, rows, early, own_sum, dense, got_a, part, got_b, tally, got_n,
           send_sem, recv_sem, table_sem, in_sem):
    group, blk = lax.axis_index("group"), lax.axis_index("blk")
    mx, core = lax.div(group, 2), lax.rem(blk, 2)
    my = lax.div(blk, 8) * 2 + lax.rem(group, 2)
    mz = lax.rem(lax.div(blk, 2), 4)

    part_x = [lax.rem(mx + v, 4) * 2 for v in range(4)]
    part_y = [(lax.rem(lax.rem(my + v, 4), 2), lax.div(lax.rem(my + v, 4), 2) * 8) for v in range(4)]
    part_z = [lax.rem(mz + v, 4) * 2 + core for v in range(4)]

    def at(dx, dy, dz):
        return part_x[dx] + part_y[dy][0], part_y[dy][1] + part_z[dz]

    sibling = place(mx, my, mz, 1 - core)

    def send(src, dst, number, device):
        return pltpu.make_async_remote_copy(
            src_ref=src, dst_ref=dst, send_sem=send_sem.at[number], recv_sem=recv_sem.at[number],
            device_id=device, device_id_type=MESH)

    def apart(work):
        pl.when(core < 2)(work)

    barrier = pltpu.get_barrier_semaphore()
    pl.semaphore_signal(barrier, inc=1, device_id=sibling, device_id_type=MESH)
    for v in range(1, 4):
        for device in (at(0, 0, v), at(0, v, 0), at(v, 0, 0)):
            pl.semaphore_signal(barrier, inc=1, device_id=device, device_id_type=MESH)

    inputs = []
    for number, pair in enumerate(((spec_hbm, spec), (owner_hbm, owner), (bin_hbm, bins))):
        inputs.append(pltpu.make_async_copy(*pair, in_sem.at[number]))
        inputs[number].start()

    table_copies = []
    for side in range(2):
        here = pl.ds(pl.multiple_of(side * FREQS + core * HALF, HALF), HALF)
        table_copies.append(pltpu.make_async_copy(
            table_hbm.at[here], table.at[pl.ds(side * HALF, HALF)], table_sem.at[side]))
        table_copies[side].start()

    for copy in inputs:
        copy.wait()
    values = spec[...].astype(F32)
    real, imag = values[:, 0, :], values[:, 1, :]
    energy = real * real + imag * imag
    lane = lax.broadcasted_iota(jnp.int32, energy.shape, 1)
    smooth = energy
    for bit in (1, 2, 4):
        other = jnp.where((lane & bit) == 0, pltpu.roll(smooth, FREQS - bit, 1),
                          pltpu.roll(smooth, bit, 1))
        smooth = smooth + other
    smooth = smooth * 0.125
    level = jnp.sum(energy, axis=1, keepdims=True) * (1.0 / FREQS)
    row = lax.broadcasted_iota(jnp.int32, (CH, 1), 0)
    alive = jnp.where(row < live_ref[0], 1.0, 0.0).astype(F32)
    inverse = lax.rsqrt(smooth + 0.1 * level + 1e-06) * alive
    for side, values in enumerate((real, imag)):
        white = (values * inverse).astype(BF)
        for half in range(2):
            own[half, side] = white[:, half * HALF:(half + 1) * HALF]
    blocks[OWN, core] = own[core]
    codes[OWN, core] = owner[...] * BINS_DEV + bins[...]

    pl.semaphore_wait(barrier, 10)

    toward = {BACK: at(0, 0, 1), OPPOSITE: at(0, 0, 2), FLIP: at(0, 2, 0)}
    sib_copy = send(own.at[1 - core], blocks.at[OWN, core], S_SIB, sibling)
    sib_copy.start()
    code_copy = send(codes.at[OWN, core], codes.at[OWN, core], S_CODE, sibling)
    code_copy.start()

    def far_copy(r, j):
        q = core if j == 0 else 1 - core
        return send(blocks.at[OWN, q], blocks.at[r, q], S_FAR + 2 * (r - 1) + j, toward[r])

    def far_code(r):
        return send(codes.at[OWN], codes.at[r], S_CODE + r, toward[r])

    far_copy(FLIP, 0).start()
    far_copy(BACK, 0).start()
    sib_copy.wait_recv()
    for r in (FLIP, BACK):
        far_copy(r, 1).start()
    code_copy.wait_recv()
    for r in (FLIP, BACK, OPPOSITE):
        far_code(r).start()

    def offsets_of(code):
        owner = code // 64
        ox, oz, oc = owner // 32, owner // 2 % 4, owner % 2
        oy = owner // 8 % 2 * 2 + owner // 16 % 2
        return (ox - mx + 4) % 4, (oy - my + 4) % 4, (oz - mz + 4) % 4, oc

    def hits_of(code):
        dx, dy, dz, oc = offsets_of(code)
        whose = jnp.where(oc == core, dx * 32 + dy * 8 + dz, -1)
        down = lax.broadcasted_iota(jnp.int32, (128, 2048), 0)
        named = jnp.where(down == whose, 1.0, 0.0).astype(BF)
        binned = jnp.where(down == code % 64, 1.0, 0.0).astype(BF)
        return lax.dot_general(named, binned, (((1,), (1,)), ((), ())), preferred_element_type=F32)

    def copy_n(stage, v):
        spot = stage * 3 + v - 1
        if stage == 0:
            return send(tally.at[pl.ds(32 * v, 32)], got_n.at[spot], S_N + spot, at(v, 0, 0))
        if stage == 1:
            return send(tally.at[pl.ds(8 * v, 8)], got_n.at[spot, pl.ds(0, 8)], S_N + spot,
                        at(0, v, 0))
        return send(tally.at[pl.ds(0, 8)], got_n.at[spot, pl.ds(0, 8)], S_N + spot, at(0, 0, v))

    def tally_stage(stage):
        if stage > 0:
            rows_of = 32 if stage == 1 else 8
            total = tally[0:rows_of]
            for v in range(1, 4):
                copy_n(stage - 1, v).wait()
                total = total + got_n[(stage - 1) * 3 + v - 1, 0:rows_of]
            tally[0:rows_of] = total
        for v in range(1, 4):
            copy_n(stage, v).start()

    @apart
    def _():
        tally[...] = hits_of(codes[OWN, 0]) + hits_of(codes[OWN, 1])

    far_copy(BACK, 1).wait_send()
    for j in range(2):
        far_copy(OPPOSITE, j).start()
    tally_stage(0)

    def pair_of(first, q, second, r, steps):
        return first, q, second, r, steps + q - r

    low = 1 - lax.div(mz + 3, 4)
    high = lax.div(mz, 2)

    def pick(flag, one, other):
        return flag * one + (1 - flag) * other

    near_first, near_second = pick(low, BACK, OWN), pick(low, OWN, BACK)
    cross_first, cross_second = pick(low, FLIP, BACK), pick(low, BACK, FLIP)
    far_first, far_second = pick(high, OWN, OPPOSITE), pick(high, OPPOSITE, OWN)
    flip_first, flip_second = pick(high, OPPOSITE, FLIP), pick(high, FLIP, OPPOSITE)
    pairs = (
        [pair_of(OWN, 0, FLIP, 0, 8), pair_of(OWN, 0, FLIP, 1, 8),
         pair_of(OWN, 1, FLIP, 1, 8), pair_of(OWN, 1, OWN, 0, 0)]
        + [pair_of(near_first, q, near_second, r, pick(low, 6, 2)) for q in (0, 1) for r in (0, 1)]
        + [pair_of(cross_first, q, cross_second, r, pick(low, 2, 6)) for q in (0, 1) for r in (0, 1)]
        + [pair_of(far_first, high, far_second, r, 4) for r in (0, 1)]
        + [pair_of(flip_first, high, flip_second, r, 4) for r in (0, 1)])

    def near(mate, far):
        q, r = pick(low, far, mate), pick(low, mate, far)
        return 4 + 2 * q + r, (near_first, q, near_second, r)

    def listed(number):
        return number, pairs[number][:4]

    runs = [
        [listed(3), (core, (OWN, 0, FLIP, core)), near(0, core), near(1, core)],
        [(1 - core, (OWN, 0, FLIP, 1 - core)), listed(2), near(0, 1 - core), near(1, 1 - core)],
        [listed(number) for number in range(8, 12)],
        [listed(number) for number in range(12, 16)],
    ]

    def form(slot, first, q, second, r):
        far_r, far_i = blocks[second, r, 0], blocks[second, r, 1]
        for i in range(CH):
            near_r = jnp.broadcast_to(blocks[first, q, 0, i:i + 1, :], (CH, HALF))
            near_i = jnp.broadcast_to(blocks[first, q, 1, i:i + 1, :], (CH, HALF))
            here = pl.ds(slot * 256 + i * CH, CH)
            cross[here, 0:HALF] = near_r * far_r + near_i * far_i
            cross[here, HALF:FREQS] = near_i * far_r - near_r * far_i

    def row_copy(number):
        return send(leaving.at[number], coming.at[number], S_ROWS + number, sibling)

    def correlate(run):
        @apart
        def _():
            for slot, (number, pair) in enumerate(run):
                form(slot, *pair)
            made = jnp.dot(cross[...], table[...], preferred_element_type=F32)
            for slot, (number, pair) in enumerate(run):
                here = made[slot * 256:(slot + 1) * 256]
                mine[number] = here
                leaving[number] = here.astype(BF)
        for number, pair in run:
            row_copy(number).start()

    def complete(begin, end):
        for number in range(begin, end):
            row_copy(number).wait_recv()

        @apart
        def _():
            for number in range(begin, end):
                total = mine[number] + coming[number].astype(F32)
                rows[number * 256:(number + 1) * 256] = total.astype(BF)

    for copy in table_copies:
        copy.wait()
    far_copy(FLIP, 0).wait_recv()
    far_copy(BACK, 0).wait_recv()
    correlate(runs[0])
    far_copy(FLIP, 1).wait_recv()
    far_copy(BACK, 1).wait_recv()
    correlate(runs[1])
    correlate(runs[2])
    tally_stage(1)
    far_copy(OPPOSITE, 0).wait_recv()
    far_copy(OPPOSITE, 1).wait_recv()
    correlate(runs[3])
    tally_stage(2)

    def place_of(code):
        slot = code % 64
        dx, dy, dz, oc = offsets_of(code)
        kind = slot // 16
        side = jnp.where(core == 0, dy, dx)
        axis = jnp.where(kind == 3, jnp.where(side == 1, 2, core), kind)
        first = jnp.where(kind == 3, side, jnp.where(kind == 0, dy, dx))
        along = jnp.where(axis == 0, dx, jnp.where(axis == 1, dy, dz))
        second = jnp.where(axis < 2, dz, jnp.where((kind == 3) & (core == 0), dx, dy))
        order = jnp.where(along == 3, 2, 2 - along)
        leave = jnp.where(first < 2, order * 512 + kind * 128 + first * 64,
                          first * 768 + order * 256 + kind * 64)
        stay = jnp.where(first < 2, 3072 + kind * 128 + first * 64, 3072 + first * 256 + kind * 64)
        spot = jnp.where(along == 0, stay, leave) + second * 16 + slot % 16
        return jnp.where(oc == core, spot, -1)

    for r in (FLIP, BACK, OPPOSITE):
        far_code(r).wait_recv()

    @apart
    def _():
        for number, (first, q, second, r, step) in enumerate(pairs):
            from_row = pl.multiple_of((step - 1) * 256, 256)
            spots[:, number * 256:(number + 1) * 256] = codes[first, q, :, pl.ds(from_row, 256)]
        spots[...] = place_of(spots[...])

    complete(0, 12)

    def device_of(kind, offsets):
        if kind < 3:
            return at(*offsets[kind])
        one, other = at(*offsets[3]), at(*offsets[4])
        return tuple(pick(core, b, a) for a, b in zip(one, other))

    begins, per_kind, stays = (0, 1536, 2304), (128, 64, 64), (0, 512, 768)
    pieces = [[(0, 0, 128), (1, 128, 128), (2, 256, 128), (3, 384, 64), (3, 448, 64)],
              [(kind, kind * 64, 64) for kind in range(4)]]

    def rows_of(part_of, along):
        count = 4 * per_kind[part_of]
        return pl.ds(begins[part_of] + (2, 1, 3).index(along) * count, count)

    def pieces_of(part_of):
        return pieces[min(part_of, 1)]

    def copy_a(part_of, along, piece):
        kind, begin, count = pieces_of(part_of)[piece]
        here = pl.ds(rows_of(part_of, along).start + begin, count)
        x, y, z = (along, 0, 0), (0, along, 0), (0, 0, along)
        last = (z, z) if piece == 4 else (x, y)
        return send(dense.at[here], got_a.at[here], S_A + (part_of * 3 + along - 1) * 5 + piece,
                    device_of(kind, (x, y, z) + last))

    def group_of(base, begin, end):
        down = lax.broadcasted_iota(jnp.int32, (512, end - begin), 0)
        hot = jnp.where(down == spots[:, begin:end] - base, 1.0, 0.0).astype(BF)
        return jnp.dot(hot, rows[begin:end], preferred_element_type=F32)

    @apart
    def _():
        early[0] = group_of(0, 0, 3072)
        early[1] = group_of(512, 0, 3072)

    complete(12, 16)
    ready = [[(0, 2)], [(0, 1)], [(0, 3)], [(1, 2), (1, 1)], [(1, 3), (2, 2)], [(2, 1), (2, 3)]]
    for group, leaves in enumerate(ready):
        @apart
        def _(group=group):
            if group < 2:
                total = early[group] + group_of(group * 512, 3072, 4096)
            else:
                total = group_of(group * 512, 0, 4096)
            dense[pl.ds(group * 512, 512)] = total.astype(BF)

        for part_of, along in leaves:
            for piece in range(len(pieces_of(part_of))):
                copy_a(part_of, along, piece).start()

    @apart
    def _():
        for half in range(2):
            own_sum[pl.ds(half * 512, 512)] = group_of(3072 + half * 512, 0, 4096)

    def copy_b(kind, spot):
        first, second = spot // 4, spot % 4
        last = ((second, 1, 0), (1, second, 0)) if first == 1 else ((0, first, second), (first, 0, second))
        offsets = ((0, first, second), (first, 0, second), (first, second, 0)) + last
        return send(part.at[kind, spot], got_b.at[kind, spot], S_B + kind * 3 + max(spot // 4 - 1, 0),
                    device_of(kind, offsets))

    spots_of = (range(1, 8), range(8, 12), range(12, 16))

    def all_b(kind, part_of):
        here = pl.ds(spots_of[part_of][0], len(spots_of[part_of]))
        return send(part.at[kind, here], got_b.at[kind, here], S_B + kind * 3 + part_of, sibling)

    for part_of in range(3):
        for along in (2, 1, 3):
            for piece in range(len(pieces_of(part_of))):
                copy_a(part_of, along, piece).wait_recv()

        @apart
        def _(part_of=part_of):
            count = per_kind[part_of]
            total = own_sum[pl.ds(stays[part_of], 4 * count)]
            for along in (2, 1, 3):
                total = total + got_a[rows_of(part_of, along)].astype(F32)
            total = total.astype(BF)
            for kind in range(4):
                here = total[kind * count:(kind + 1) * count]
                part[kind, pl.ds(stays[part_of] // 64, count // 16)] = here.reshape(count // 16, 16, LAGS)

        for spot in spots_of[part_of]:
            for kind in range(4):
                copy_b(kind, spot).start()

    count = tally[0:1]
    for v in range(1, 4):
        copy_n(2, v).wait()
        count = count + got_n[5 + v, v:v + 1]
    shape = (BINS_DEV, 128)
    diagonal = lax.broadcasted_iota(jnp.int32, shape, 0) == lax.broadcasted_iota(jnp.int32, shape, 1)
    count = jnp.sum(jnp.where(diagonal, count, 0.0), axis=1, keepdims=True)
    scale = lax.rsqrt(count + 1.0)

    sib_copy.wait_send()
    code_copy.wait_send()
    for r in (FLIP, BACK, OPPOSITE):
        far_code(r).wait_send()
        for j in range(2):
            if (r, j) != (BACK, 1):
                far_copy(r, j).wait_send()
    for number in range(16):
        row_copy(number).wait_send()
    for part_of in range(3):
        for along in range(1, 4):
            for piece in range(len(pieces_of(part_of))):
                copy_a(part_of, along, piece).wait_send()

    def gather(part_of):
        for kind in range(4):
            all_b(kind, part_of).wait_recv()

        @apart
        def _():
            for kind in range(4):
                here = pl.ds(kind * 16, 16)
                total = out_ref[here] if part_of else part[kind, 0].astype(F32)
                for spot in spots_of[part_of]:
                    total = total + got_b[kind, spot].astype(F32)
                out_ref[here] = total * scale[kind * 16:(kind + 1) * 16] if part_of == 2 else total

    for part_of in range(3):
        gather(part_of)
    for part_of in range(3):
        for kind in range(4):
            all_b(kind, part_of).wait_send()


def stacks(spectra, live_count, owner, slot, table):
    vmem, anywhere = pl.BlockSpec(memory_space=pltpu.VMEM), pl.BlockSpec(memory_space=pl.ANY)
    return pl.pallas_call(
        kernel,
        out_shape=jax.ShapeDtypeStruct((BINS_DEV, LAGS), F32),
        in_specs=[anywhere, pl.BlockSpec(memory_space=pltpu.SMEM), anywhere, anywhere, anywhere],
        out_specs=vmem,
        scratch_shapes=[
            pltpu.VMEM((CH, 2, FREQS), BF),
            pltpu.VMEM((1, 2048), jnp.int32),
            pltpu.VMEM((1, 2048), jnp.int32),
            pltpu.VMEM((2, 2, CH, HALF), BF),
            pltpu.VMEM((4, 2, 2, CH, HALF), BF),
            pltpu.VMEM((FREQS, LAGS), BF),
            pltpu.VMEM((1024, FREQS), BF),
            pltpu.VMEM((4, 2, 1, 2048), jnp.int32),
            pltpu.VMEM((1, 4096), jnp.int32),
            pltpu.VMEM((16, 256, LAGS), F32),
            pltpu.VMEM((16, 256, LAGS), BF),
            pltpu.VMEM((16, 256, LAGS), BF),
            pltpu.VMEM((4096, LAGS), BF),
            pltpu.VMEM((2, 512, LAGS), F32),
            pltpu.VMEM((1024, LAGS), F32),
            pltpu.VMEM((3072, LAGS), BF),
            pltpu.VMEM((3072, LAGS), BF),
            pltpu.VMEM((4, 16, 16, LAGS), BF),
            pltpu.VMEM((4, 16, 16, LAGS), BF),
            pltpu.VMEM((128, 128), F32),
            pltpu.VMEM((9, 32, 128), F32),
            pltpu.SemaphoreType.DMA((N_SEM,)),
            pltpu.SemaphoreType.DMA((N_SEM,)),
            pltpu.SemaphoreType.DMA((2,)),
            pltpu.SemaphoreType.DMA((3,)),
        ],
        compiler_params=pltpu.CompilerParams(
            collective_id=0, has_side_effects=True, vmem_limit_bytes=56 * 1024 * 1024),
        cost_estimate=pl.CostEstimate(
            flops=13_000_000_000, bytes_accessed=4_000_000, transcendentals=40_000),
    )(spectra, live_count, owner, slot, table)


def on_device(spectra, live_count, owner_list, bin_list):
    table = jnp.asarray(table_constant(FREQS, LAGS))
    return stacks(spectra, live_count, owner_list.reshape(1, -1), bin_list.reshape(1, -1), table)


def solution(mesh):
    return jax.shard_map(
        on_device,
        mesh=mesh,
        in_specs=(
            P(("group", "blk"), None, None),
            P(("group", "blk")),
            P(("group", "blk"), None),
            P(("group", "blk")),
        ),
        out_specs=P(("group", "blk"), None),
        check_vma=False,
    )
```

```python
import functools
import math

import jax
import jax.numpy as jnp
import numpy as np
from jax import lax
from jax.experimental import pallas as pl
from jax.experimental.pallas import tpu as pltpu
from jax.sharding import PartitionSpec as P

CH = 16
FREQS = 2048
LAGS = 256
BINS_DEV = 64
MESH = pl.DeviceIdType.MESH
BF = jnp.bfloat16
F32 = jnp.float32

S_SIB, S_FAR, S_CODE, S_ROWS, S_N, S_A, S_B = 0, 1, 7, 11, 27, 36, 81
N_SEM = S_B + 12
OWN, BACK, OPPOSITE, FLIP = 0, 1, 2, 3
HALF = FREQS // 2


def table_constant(width, lag_count):
    frequency = np.arange(width, dtype=np.int32)
    lag_offset = np.arange(lag_count, dtype=np.int32) - lag_count // 2
    product = frequency[:, None] * lag_offset[None, :] % (2 * width)
    angles = product.astype(np.float32) * np.float32(math.pi / width)
    norm = np.float32(1.0 / math.sqrt(width))
    whole = np.concatenate([np.cos(angles), -np.sin(angles)], axis=0) * norm
    return whole.astype(jnp.bfloat16)


def place(x, y, z, core):
    return (x * 2 + lax.rem(y, 2), lax.div(y, 2) * 8 + z * 2 + core)


def kernel(spec_hbm, live_ref, owner_hbm, bin_hbm, table_hbm, out_ref, spec, owner, bins, own, blocks, table, cross,
           codes, spots, mine, leaving, coming, rows, early, own_sum, dense, got_a, part, got_b, tally, got_n,
           send_sem, recv_sem, table_sem, in_sem):
    group, blk = lax.axis_index("group"), lax.axis_index("blk")
    mx, core = lax.div(group, 2), lax.rem(blk, 2)
    my = lax.div(blk, 8) * 2 + lax.rem(group, 2)
    mz = lax.rem(lax.div(blk, 2), 4)

    part_x = [lax.rem(mx + v, 4) * 2 for v in range(4)]
    part_y = [(lax.rem(lax.rem(my + v, 4), 2), lax.div(lax.rem(my + v, 4), 2) * 8) for v in range(4)]
    part_z = [lax.rem(mz + v, 4) * 2 + core for v in range(4)]

    def at(dx, dy, dz):
        return part_x[dx] + part_y[dy][0], part_y[dy][1] + part_z[dz]

    sibling = place(mx, my, mz, 1 - core)

    def send(src, dst, number, device):
        return pltpu.make_async_remote_copy(
            src_ref=src, dst_ref=dst, send_sem=send_sem.at[number], recv_sem=recv_sem.at[number],
            device_id=device, device_id_type=MESH)

    def apart(work):
        pl.when(core < 2)(work)

    barrier = pltpu.get_barrier_semaphore()
    pl.semaphore_signal(barrier, inc=1, device_id=sibling, device_id_type=MESH)
    for v in range(1, 4):
        for device in (at(0, 0, v), at(0, v, 0), at(v, 0, 0)):
            pl.semaphore_signal(barrier, inc=1, device_id=device, device_id_type=MESH)

    inputs = []
    for number, pair in enumerate(((spec_hbm, spec), (owner_hbm, owner), (bin_hbm, bins))):
        inputs.append(pltpu.make_async_copy(*pair, in_sem.at[number]))
        inputs[number].start()

    table_copies = []
    for side in range(2):
        here = pl.ds(pl.multiple_of(side * FREQS + core * HALF, HALF), HALF)
        table_copies.append(pltpu.make_async_copy(
            table_hbm.at[here], table.at[pl.ds(side * HALF, HALF)], table_sem.at[side]))
        table_copies[side].start()

    for copy in inputs:
        copy.wait()
    values = spec[...].astype(F32)
    real, imag = values[:, 0, :], values[:, 1, :]
    energy = real * real + imag * imag
    lane = lax.broadcasted_iota(jnp.int32, energy.shape, 1)
    smooth = energy
    for bit in (1, 2, 4):
        other = jnp.where((lane & bit) == 0, pltpu.roll(smooth, FREQS - bit, 1),
                          pltpu.roll(smooth, bit, 1))
        smooth = smooth + other
    smooth = smooth * 0.125
    level = jnp.sum(energy, axis=1, keepdims=True) * (1.0 / FREQS)
    row = lax.broadcasted_iota(jnp.int32, (CH, 1), 0)
    alive = jnp.where(row < live_ref[0], 1.0, 0.0).astype(F32)
    inverse = lax.rsqrt(smooth + 0.1 * level + 1e-06) * alive
    for side, values in enumerate((real, imag)):
        white = (values * inverse).astype(BF)
        for half in range(2):
            own[half, side] = white[:, half * HALF:(half + 1) * HALF]
    blocks[OWN, core] = own[core]
    codes[OWN, core] = owner[...] * BINS_DEV + bins[...]

    pl.semaphore_wait(barrier, 10)

    toward = {BACK: at(0, 0, 1), OPPOSITE: at(0, 0, 2), FLIP: at(0, 2, 0)}
    sib_copy = send(own.at[1 - core], blocks.at[OWN, core], S_SIB, sibling)
    sib_copy.start()
    code_copy = send(codes.at[OWN, core], codes.at[OWN, core], S_CODE, sibling)
    code_copy.start()

    def far_copy(r, j):
        q = core if j == 0 else 1 - core
        return send(blocks.at[OWN, q], blocks.at[r, q], S_FAR + 2 * (r - 1) + j, toward[r])

    def far_code(r):
        return send(codes.at[OWN], codes.at[r], S_CODE + r, toward[r])

    far_copy(FLIP, 0).start()
    far_copy(BACK, 0).start()
    sib_copy.wait_recv()
    for r in (FLIP, BACK):
        far_copy(r, 1).start()
    code_copy.wait_recv()
    for r in (FLIP, BACK, OPPOSITE):
        far_code(r).start()

    def offsets_of(code):
        owner = code // 64
        ox, oz, oc = owner // 32, owner // 2 % 4, owner % 2
        oy = owner // 8 % 2 * 2 + owner // 16 % 2
        return (ox - mx + 4) % 4, (oy - my + 4) % 4, (oz - mz + 4) % 4, oc

    def hits_of(code):
        dx, dy, dz, oc = offsets_of(code)
        whose = jnp.where(oc == core, dx * 32 + dy * 8 + dz, -1)
        down = lax.broadcasted_iota(jnp.int32, (128, 2048), 0)
        named = jnp.where(down == whose, 1.0, 0.0).astype(BF)
        binned = jnp.where(down == code % 64, 1.0, 0.0).astype(BF)
        return lax.dot_general(named, binned, (((1,), (1,)), ((), ())), preferred_element_type=F32)

    def copy_n(stage, v):
        spot = stage * 3 + v - 1
        if stage == 0:
            return send(tally.at[pl.ds(32 * v, 32)], got_n.at[spot], S_N + spot, at(v, 0, 0))
        if stage == 1:
            return send(tally.at[pl.ds(8 * v, 8)], got_n.at[spot, pl.ds(0, 8)], S_N + spot,
                        at(0, v, 0))
        return send(tally.at[pl.ds(0, 8)], got_n.at[spot, pl.ds(0, 8)], S_N + spot, at(0, 0, v))

    def tally_stage(stage):
        if stage > 0:
            rows_of = 32 if stage == 1 else 8
            total = tally[0:rows_of]
            for v in range(1, 4):
                copy_n(stage - 1, v).wait()
                total = total + got_n[(stage - 1) * 3 + v - 1, 0:rows_of]
            tally[0:rows_of] = total
        for v in range(1, 4):
            copy_n(stage, v).start()

    @apart
    def _():
        tally[...] = hits_of(codes[OWN, 0]) + hits_of(codes[OWN, 1])

    far_copy(BACK, 1).wait_send()
    for j in range(2):
        far_copy(OPPOSITE, j).start()
    tally_stage(0)

    def pair_of(first, q, second, r, steps):
        return first, q, second, r, steps + q - r

    low = 1 - lax.div(mz + 3, 4)
    high = lax.div(mz, 2)

    def pick(flag, one, other):
        return flag * one + (1 - flag) * other

    near_first, near_second = pick(low, BACK, OWN), pick(low, OWN, BACK)
    cross_first, cross_second = pick(low, FLIP, BACK), pick(low, BACK, FLIP)
    far_first, far_second = pick(high, OWN, OPPOSITE), pick(high, OPPOSITE, OWN)
    flip_first, flip_second = pick(high, OPPOSITE, FLIP), pick(high, FLIP, OPPOSITE)
    pairs = (
        [pair_of(OWN, 0, FLIP, 0, 8), pair_of(OWN, 0, FLIP, 1, 8),
         pair_of(OWN, 1, FLIP, 1, 8), pair_of(OWN, 1, OWN, 0, 0)]
        + [pair_of(near_first, q, near_second, r, pick(low, 6, 2)) for q in (0, 1) for r in (0, 1)]
        + [pair_of(cross_first, q, cross_second, r, pick(low, 2, 6)) for q in (0, 1) for r in (0, 1)]
        + [pair_of(far_first, high, far_second, r, 4) for r in (0, 1)]
        + [pair_of(flip_first, high, flip_second, r, 4) for r in (0, 1)])

    def near(mate, far):
        q, r = pick(low, far, mate), pick(low, mate, far)
        return 4 + 2 * q + r, (near_first, q, near_second, r)

    def listed(number):
        return number, pairs[number][:4]

    runs = [
        [listed(3), (core, (OWN, 0, FLIP, core)), near(0, core), near(1, core)],
        [(1 - core, (OWN, 0, FLIP, 1 - core)), listed(2), near(0, 1 - core), near(1, 1 - core)],
        [listed(number) for number in range(8, 12)],
        [listed(number) for number in range(12, 16)],
    ]

    def form(slot, first, q, second, r):
        far_r, far_i = blocks[second, r, 0], blocks[second, r, 1]
        for i in range(CH):
            near_r = jnp.broadcast_to(blocks[first, q, 0, i:i + 1, :], (CH, HALF))
            near_i = jnp.broadcast_to(blocks[first, q, 1, i:i + 1, :], (CH, HALF))
            here = pl.ds(slot * 256 + i * CH, CH)
            cross[here, 0:HALF] = near_r * far_r + near_i * far_i
            cross[here, HALF:FREQS] = near_i * far_r - near_r * far_i

    def row_copy(number):
        return send(leaving.at[number], coming.at[number], S_ROWS + number, sibling)

    def correlate(run):
        @apart
        def _():
            for slot, (number, pair) in enumerate(run):
                form(slot, *pair)
            made = jnp.dot(cross[...], table[...], preferred_element_type=F32)
            for slot, (number, pair) in enumerate(run):
                here = made[slot * 256:(slot + 1) * 256]
                mine[number] = here
                leaving[number] = here.astype(BF)
        for number, pair in run:
            row_copy(number).start()

    def complete(begin, end):
        for number in range(begin, end):
            row_copy(number).wait_recv()

        @apart
        def _():
            for number in range(begin, end):
                total = mine[number] + coming[number].astype(F32)
                rows[number * 256:(number + 1) * 256] = total.astype(BF)

    for copy in table_copies:
        copy.wait()
    far_copy(FLIP, 0).wait_recv()
    far_copy(BACK, 0).wait_recv()
    correlate(runs[0])
    far_copy(FLIP, 1).wait_recv()
    far_copy(BACK, 1).wait_recv()
    correlate(runs[1])
    correlate(runs[2])
    tally_stage(1)
    def place_of(code):
        slot = code % 64
        dx, dy, dz, oc = offsets_of(code)
        kind = slot // 16
        side = jnp.where(core == 0, dy, dx)
        axis = jnp.where(kind == 3, jnp.where(side == 1, 2, core), kind)
        first = jnp.where(kind == 3, side, jnp.where(kind == 0, dy, dx))
        along = jnp.where(axis == 0, dx, jnp.where(axis == 1, dy, dz))
        second = jnp.where(axis < 2, dz, jnp.where((kind == 3) & (core == 0), dx, dy))
        order = jnp.where(along == 3, 2, 2 - along)
        leave = jnp.where(first < 2, order * 512 + kind * 128 + first * 64,
                          first * 768 + order * 256 + kind * 64)
        stay = jnp.where(first < 2, 3072 + kind * 128 + first * 64, 3072 + first * 256 + kind * 64)
        spot = jnp.where(along == 0, stay, leave) + second * 16 + slot % 16
        return jnp.where(oc == core, spot, -1)

    for r in (FLIP, BACK, OPPOSITE):
        far_code(r).wait_recv()

    @apart
    def _():
        for number, (first, q, second, r, step) in enumerate(pairs):
            from_row = pl.multiple_of((step - 1) * 256, 256)
            spots[:, number * 256:(number + 1) * 256] = codes[first, q, :, pl.ds(from_row, 256)]
        spots[...] = place_of(spots[...])

    far_copy(OPPOSITE, 0).wait_recv()
    far_copy(OPPOSITE, 1).wait_recv()
    correlate(runs[3])

    complete(0, 12)

    def device_of(kind, offsets):
        if kind < 3:
            return at(*offsets[kind])
        one, other = at(*offsets[3]), at(*offsets[4])
        return tuple(pick(core, b, a) for a, b in zip(one, other))

    begins, per_kind, stays = (0, 1536, 2304), (128, 64, 64), (0, 512, 768)
    pieces = [[(0, 0, 128), (1, 128, 128), (2, 256, 128), (3, 384, 64), (3, 448, 64)],
              [(kind, kind * 64, 64) for kind in range(4)]]

    def rows_of(part_of, along):
        count = 4 * per_kind[part_of]
        return pl.ds(begins[part_of] + (2, 1, 3).index(along) * count, count)

    def pieces_of(part_of):
        return pieces[min(part_of, 1)]

    def copy_a(part_of, along, piece):
        kind, begin, count = pieces_of(part_of)[piece]
        here = pl.ds(rows_of(part_of, along).start + begin, count)
        x, y, z = (along, 0, 0), (0, along, 0), (0, 0, along)
        last = (z, z) if piece == 4 else (x, y)
        return send(dense.at[here], got_a.at[here], S_A + (part_of * 3 + along - 1) * 5 + piece,
                    device_of(kind, (x, y, z) + last))

    def group_of(base, begin, end):
        down = lax.broadcasted_iota(jnp.int32, (512, end - begin), 0)
        hot = jnp.where(down == spots[:, begin:end] - base, 1.0, 0.0).astype(BF)
        return jnp.dot(hot, rows[begin:end], preferred_element_type=F32)

    @apart
    def _():
        early[0] = group_of(0, 0, 3072)
        early[1] = group_of(512, 0, 3072)

    complete(12, 16)
    ready = [[(0, 2)], [(0, 1)], [(0, 3)], [(1, 2), (1, 1)], [(1, 3), (2, 2)], [(2, 1), (2, 3)]]
    for group, leaves in enumerate(ready):
        @apart
        def _(group=group):
            if group < 2:
                total = early[group] + group_of(group * 512, 3072, 4096)
            else:
                total = group_of(group * 512, 0, 4096)
            dense[pl.ds(group * 512, 512)] = total.astype(BF)

        for part_of, along in leaves:
            for piece in range(len(pieces_of(part_of))):
                copy_a(part_of, along, piece).start()
        if group == 3:
            tally_stage(2)

    @apart
    def _():
        for half in range(2):
            own_sum[pl.ds(half * 512, 512)] = group_of(3072 + half * 512, 0, 4096)

    def copy_b(kind, spot):
        first, second = spot // 4, spot % 4
        last = ((second, 1, 0), (1, second, 0)) if first == 1 else ((0, first, second), (first, 0, second))
        offsets = ((0, first, second), (first, 0, second), (first, second, 0)) + last
        return send(part.at[kind, spot], got_b.at[kind, spot], S_B + kind * 3 + max(spot // 4 - 1, 0),
                    device_of(kind, offsets))

    spots_of = (range(1, 8), range(8, 12), range(12, 16))

    def all_b(kind, part_of):
        here = pl.ds(spots_of[part_of][0], len(spots_of[part_of]))
        return send(part.at[kind, here], got_b.at[kind, here], S_B + kind * 3 + part_of, sibling)

    for part_of in range(3):
        for along in (2, 1, 3):
            for piece in range(len(pieces_of(part_of))):
                copy_a(part_of, along, piece).wait_recv()

        @apart
        def _(part_of=part_of):
            count = per_kind[part_of]
            total = own_sum[pl.ds(stays[part_of], 4 * count)]
            for along in (2, 1, 3):
                total = total + got_a[rows_of(part_of, along)].astype(F32)
            total = total.astype(BF)
            for kind in range(4):
                here = total[kind * count:(kind + 1) * count]
                part[kind, pl.ds(stays[part_of] // 64, count // 16)] = here.reshape(count // 16, 16, LAGS)

        for spot in spots_of[part_of]:
            for kind in range(4):
                copy_b(kind, spot).start()

    count = tally[0:1]
    for v in range(1, 4):
        copy_n(2, v).wait()
        count = count + got_n[5 + v, v:v + 1]
    shape = (BINS_DEV, 128)
    diagonal = lax.broadcasted_iota(jnp.int32, shape, 0) == lax.broadcasted_iota(jnp.int32, shape, 1)
    count = jnp.sum(jnp.where(diagonal, count, 0.0), axis=1, keepdims=True)
    scale = lax.rsqrt(count + 1.0)

    sib_copy.wait_send()
    code_copy.wait_send()
    for r in (FLIP, BACK, OPPOSITE):
        far_code(r).wait_send()
        for j in range(2):
            if (r, j) != (BACK, 1):
                far_copy(r, j).wait_send()
    for number in range(16):
        row_copy(number).wait_send()
    for part_of in range(3):
        for along in range(1, 4):
            for piece in range(len(pieces_of(part_of))):
                copy_a(part_of, along, piece).wait_send()

    def gather(part_of):
        for kind in range(4):
            all_b(kind, part_of).wait_recv()

        @apart
        def _():
            for kind in range(4):
                here = pl.ds(kind * 16, 16)
                total = out_ref[here] if part_of else part[kind, 0].astype(F32)
                for spot in spots_of[part_of]:
                    total = total + got_b[kind, spot].astype(F32)
                out_ref[here] = total * scale[kind * 16:(kind + 1) * 16] if part_of == 2 else total

    for part_of in range(3):
        gather(part_of)
    for part_of in range(3):
        for kind in range(4):
            all_b(kind, part_of).wait_send()


def stacks(spectra, live_count, owner, slot, table):
    vmem, anywhere = pl.BlockSpec(memory_space=pltpu.VMEM), pl.BlockSpec(memory_space=pl.ANY)
    return pl.pallas_call(
        kernel,
        out_shape=pltpu.VMEM((BINS_DEV, LAGS), F32),
        in_specs=[anywhere, pl.BlockSpec(memory_space=pltpu.SMEM), anywhere, anywhere, anywhere],
        out_specs=vmem,
        scratch_shapes=[
            pltpu.VMEM((CH, 2, FREQS), BF),
            pltpu.VMEM((1, 2048), jnp.int32),
            pltpu.VMEM((1, 2048), jnp.int32),
            pltpu.VMEM((2, 2, CH, HALF), BF),
            pltpu.VMEM((4, 2, 2, CH, HALF), BF),
            pltpu.VMEM((FREQS, LAGS), BF),
            pltpu.VMEM((1024, FREQS), BF),
            pltpu.VMEM((4, 2, 1, 2048), jnp.int32),
            pltpu.VMEM((1, 4096), jnp.int32),
            pltpu.VMEM((16, 256, LAGS), F32),
            pltpu.VMEM((16, 256, LAGS), BF),
            pltpu.VMEM((16, 256, LAGS), BF),
            pltpu.VMEM((4096, LAGS), BF),
            pltpu.VMEM((2, 512, LAGS), F32),
            pltpu.VMEM((1024, LAGS), F32),
            pltpu.VMEM((3072, LAGS), BF),
            pltpu.VMEM((3072, LAGS), BF),
            pltpu.VMEM((4, 16, 16, LAGS), BF),
            pltpu.VMEM((4, 16, 16, LAGS), BF),
            pltpu.VMEM((128, 128), F32),
            pltpu.VMEM((9, 32, 128), F32),
            pltpu.SemaphoreType.DMA((N_SEM,)),
            pltpu.SemaphoreType.DMA((N_SEM,)),
            pltpu.SemaphoreType.DMA((2,)),
            pltpu.SemaphoreType.DMA((3,)),
        ],
        compiler_params=pltpu.CompilerParams(
            collective_id=0, has_side_effects=True, vmem_limit_bytes=56 * 1024 * 1024),
        cost_estimate=pl.CostEstimate(
            flops=13_000_000_000, bytes_accessed=4_000_000, transcendentals=40_000),
    )(spectra, live_count, owner, slot, table)


def on_device(spectra, live_count, owner_list, bin_list):
    table = jnp.asarray(table_constant(FREQS, LAGS))
    return stacks(spectra, live_count, owner_list.reshape(1, -1), bin_list.reshape(1, -1), table)


def solution(mesh):
    return jax.shard_map(
        on_device,
        mesh=mesh,
        in_specs=(
            P(("group", "blk"), None, None),
            P(("group", "blk")),
            P(("group", "blk"), None),
            P(("group", "blk")),
        ),
        out_specs=P(("group", "blk"), None),
        check_vma=False,
    )
```

```python
import functools
import math

import jax
import jax.numpy as jnp
import numpy as np
from jax import lax
from jax.experimental import pallas as pl
from jax.experimental.pallas import tpu as pltpu
from jax.sharding import PartitionSpec as P

CH = 16
FREQS = 2048
LAGS = 256
BINS_DEV = 64
MESH = pl.DeviceIdType.MESH
BF = jnp.bfloat16
F32 = jnp.float32

S_SIB, S_FAR, S_CODE, S_ROWS, S_N, S_A, S_B = 0, 1, 7, 11, 27, 36, 81
N_SEM = S_B + 12
OWN, BACK, OPPOSITE, FLIP = 0, 1, 2, 3
HALF = FREQS // 2


def table_constant(width, lag_count):
    frequency = np.arange(width, dtype=np.int32)
    lag_offset = np.arange(lag_count, dtype=np.int32) - lag_count // 2
    product = frequency[:, None] * lag_offset[None, :] % (2 * width)
    angles = product.astype(np.float32) * np.float32(math.pi / width)
    norm = np.float32(1.0 / math.sqrt(width))
    whole = np.concatenate([np.cos(angles), -np.sin(angles)], axis=0) * norm
    return whole.astype(jnp.bfloat16)


def place(x, y, z, core):
    return (x * 2 + lax.rem(y, 2), lax.div(y, 2) * 8 + z * 2 + core)


def kernel(spec_hbm, live_ref, owner_hbm, bin_hbm, table_hbm, out_ref, spec, owner, bins, own, blocks, table, cross,
           codes, spots, mine, leaving, coming, rows, early, own_sum, dense, got_a, part, got_b, tally, got_n,
           send_sem, recv_sem, table_sem, in_sem):
    group, blk = lax.axis_index("group"), lax.axis_index("blk")
    mx, core = lax.div(group, 2), lax.rem(blk, 2)
    my = lax.div(blk, 8) * 2 + lax.rem(group, 2)
    mz = lax.rem(lax.div(blk, 2), 4)

    part_x = [lax.rem(mx + v, 4) * 2 for v in range(4)]
    part_y = [(lax.rem(lax.rem(my + v, 4), 2), lax.div(lax.rem(my + v, 4), 2) * 8) for v in range(4)]
    part_z = [lax.rem(mz + v, 4) * 2 + core for v in range(4)]

    def at(dx, dy, dz):
        return part_x[dx] + part_y[dy][0], part_y[dy][1] + part_z[dz]

    sibling = place(mx, my, mz, 1 - core)

    def send(src, dst, number, device):
        return pltpu.make_async_remote_copy(
            src_ref=src, dst_ref=dst, send_sem=send_sem.at[number], recv_sem=recv_sem.at[number],
            device_id=device, device_id_type=MESH)

    def apart(work):
        pl.when(core < 2)(work)

    barrier = pltpu.get_barrier_semaphore()
    pl.semaphore_signal(barrier, inc=1, device_id=sibling, device_id_type=MESH)
    for v in range(1, 4):
        for device in (at(0, 0, v), at(0, v, 0), at(v, 0, 0)):
            pl.semaphore_signal(barrier, inc=1, device_id=device, device_id_type=MESH)

    inputs = []
    for number, pair in enumerate(((spec_hbm, spec), (owner_hbm, owner), (bin_hbm, bins))):
        inputs.append(pltpu.make_async_copy(*pair, in_sem.at[number]))
        inputs[number].start()

    table_copies = []
    for side in range(2):
        here = pl.ds(pl.multiple_of(side * FREQS + core * HALF, HALF), HALF)
        table_copies.append(pltpu.make_async_copy(
            table_hbm.at[here], table.at[pl.ds(side * HALF, HALF)], table_sem.at[side]))
        table_copies[side].start()

    for copy in inputs:
        copy.wait()
    values = spec[...].astype(F32)
    real, imag = values[:, 0, :], values[:, 1, :]
    energy = real * real + imag * imag
    lane = lax.broadcasted_iota(jnp.int32, energy.shape, 1)
    smooth = energy
    for bit in (1, 2, 4):
        other = jnp.where((lane & bit) == 0, pltpu.roll(smooth, FREQS - bit, 1),
                          pltpu.roll(smooth, bit, 1))
        smooth = smooth + other
    smooth = smooth * 0.125
    level = jnp.sum(energy, axis=1, keepdims=True) * (1.0 / FREQS)
    row = lax.broadcasted_iota(jnp.int32, (CH, 1), 0)
    alive = jnp.where(row < live_ref[0], 1.0, 0.0).astype(F32)
    inverse = lax.rsqrt(smooth + 0.1 * level + 1e-06) * alive
    for side, values in enumerate((real, imag)):
        white = (values * inverse).astype(BF)
        for half in range(2):
            own[half, side] = white[:, half * HALF:(half + 1) * HALF]
    blocks[OWN, core] = own[core]
    codes[OWN, core] = owner[...] * BINS_DEV + bins[...]

    pl.semaphore_wait(barrier, 10)

    toward = {BACK: at(0, 0, 1), OPPOSITE: at(0, 0, 2), FLIP: at(0, 2, 0)}
    sib_copy = send(own.at[1 - core], blocks.at[OWN, core], S_SIB, sibling)
    sib_copy.start()
    code_copy = send(codes.at[OWN, core], codes.at[OWN, core], S_CODE, sibling)
    code_copy.start()

    def far_copy(r, j):
        q = core if j == 0 else 1 - core
        return send(blocks.at[OWN, q], blocks.at[r, q], S_FAR + 2 * (r - 1) + j, toward[r])

    def far_code(r):
        return send(codes.at[OWN], codes.at[r], S_CODE + r, toward[r])

    far_copy(BACK, 0).start()
    far_copy(FLIP, 0).start()
    sib_copy.wait_recv()
    for r in (BACK, FLIP):
        far_copy(r, 1).start()
    code_copy.wait_recv()
    for r in (FLIP, BACK, OPPOSITE):
        far_code(r).start()

    def offsets_of(code):
        owner = code // 64
        ox, oz, oc = owner // 32, owner // 2 % 4, owner % 2
        oy = owner // 8 % 2 * 2 + owner // 16 % 2
        return (ox - mx + 4) % 4, (oy - my + 4) % 4, (oz - mz + 4) % 4, oc

    def hits_of(code):
        dx, dy, dz, oc = offsets_of(code)
        whose = jnp.where(oc == core, dx * 32 + dy * 8 + dz, -1)
        down = lax.broadcasted_iota(jnp.int32, (128, 2048), 0)
        named = jnp.where(down == whose, 1.0, 0.0).astype(BF)
        binned = jnp.where(down == code % 64, 1.0, 0.0).astype(BF)
        return lax.dot_general(named, binned, (((1,), (1,)), ((), ())), preferred_element_type=F32)

    def copy_n(stage, v):
        spot = stage * 3 + v - 1
        if stage == 0:
            return send(tally.at[pl.ds(32 * v, 32)], got_n.at[spot], S_N + spot, at(v, 0, 0))
        if stage == 1:
            return send(tally.at[pl.ds(8 * v, 8)], got_n.at[spot, pl.ds(0, 8)], S_N + spot,
                        at(0, v, 0))
        return send(tally.at[pl.ds(0, 8)], got_n.at[spot, pl.ds(0, 8)], S_N + spot, at(0, 0, v))

    def tally_stage(stage):
        if stage > 0:
            rows_of = 32 if stage == 1 else 8
            total = tally[0:rows_of]
            for v in range(1, 4):
                copy_n(stage - 1, v).wait()
                total = total + got_n[(stage - 1) * 3 + v - 1, 0:rows_of]
            tally[0:rows_of] = total
        for v in range(1, 4):
            copy_n(stage, v).start()

    @apart
    def _():
        tally[...] = hits_of(codes[OWN, 0]) + hits_of(codes[OWN, 1])

    far_copy(BACK, 1).wait_send()
    for j in range(2):
        far_copy(OPPOSITE, j).start()
    tally_stage(0)

    def pair_of(first, q, second, r, steps):
        return first, q, second, r, steps + q - r

    low = 1 - lax.div(mz + 3, 4)
    high = lax.div(mz, 2)

    def pick(flag, one, other):
        return flag * one + (1 - flag) * other

    near_first, near_second = pick(low, BACK, OWN), pick(low, OWN, BACK)
    cross_first, cross_second = pick(low, FLIP, BACK), pick(low, BACK, FLIP)
    far_first, far_second = pick(high, OWN, OPPOSITE), pick(high, OPPOSITE, OWN)
    flip_first, flip_second = pick(high, OPPOSITE, FLIP), pick(high, FLIP, OPPOSITE)
    pairs = (
        [pair_of(OWN, 0, FLIP, 0, 8), pair_of(OWN, 0, FLIP, 1, 8),
         pair_of(OWN, 1, FLIP, 1, 8), pair_of(OWN, 1, OWN, 0, 0)]
        + [pair_of(near_first, q, near_second, r, pick(low, 6, 2)) for q in (0, 1) for r in (0, 1)]
        + [pair_of(cross_first, q, cross_second, r, pick(low, 2, 6)) for q in (0, 1) for r in (0, 1)]
        + [pair_of(far_first, high, far_second, r, 4) for r in (0, 1)]
        + [pair_of(flip_first, high, flip_second, r, 4) for r in (0, 1)])

    def near(mate, far):
        q, r = pick(low, far, mate), pick(low, mate, far)
        return 4 + 2 * q + r, (near_first, q, near_second, r)

    def listed(number):
        return number, pairs[number][:4]

    runs = [
        [listed(3), (core, (OWN, 0, FLIP, core)), near(0, core), near(1, core)],
        [(1 - core, (OWN, 0, FLIP, 1 - core)), listed(2), near(0, 1 - core), near(1, 1 - core)],
        [listed(number) for number in range(8, 12)],
        [listed(number) for number in range(12, 16)],
    ]

    def form(slot, first, q, second, r):
        far_r, far_i = blocks[second, r, 0], blocks[second, r, 1]
        for i in range(CH):
            near_r = jnp.broadcast_to(blocks[first, q, 0, i:i + 1, :], (CH, HALF))
            near_i = jnp.broadcast_to(blocks[first, q, 1, i:i + 1, :], (CH, HALF))
            here = pl.ds(slot * 256 + i * CH, CH)
            cross[here, 0:HALF] = near_r * far_r + near_i * far_i
            cross[here, HALF:FREQS] = near_i * far_r - near_r * far_i

    def row_copy(number):
        return send(leaving.at[number], coming.at[number], S_ROWS + number, sibling)

    def correlate(run):
        @apart
        def _():
            for slot, (number, pair) in enumerate(run):
                form(slot, *pair)
            made = jnp.dot(cross[...], table[...], preferred_element_type=F32)
            for slot, (number, pair) in enumerate(run):
                here = made[slot * 256:(slot + 1) * 256]
                mine[number] = here
                leaving[number] = here.astype(BF)
        for number, pair in run:
            row_copy(number).start()

    def complete(begin, end):
        for number in range(begin, end):
            row_copy(number).wait_recv()

        @apart
        def _():
            for number in range(begin, end):
                total = mine[number] + coming[number].astype(F32)
                rows[number * 256:(number + 1) * 256] = total.astype(BF)

    for copy in table_copies:
        copy.wait()
    far_copy(FLIP, 0).wait_recv()
    far_copy(BACK, 0).wait_recv()
    correlate(runs[0])
    far_copy(FLIP, 1).wait_recv()
    far_copy(BACK, 1).wait_recv()
    correlate(runs[1])
    correlate(runs[2])
    tally_stage(1)
    def place_of(code):
        slot = code % 64
        dx, dy, dz, oc = offsets_of(code)
        kind = slot // 16
        side = jnp.where(core == 0, dy, dx)
        axis = jnp.where(kind == 3, jnp.where(side == 1, 2, core), kind)
        first = jnp.where(kind == 3, side, jnp.where(kind == 0, dy, dx))
        along = jnp.where(axis == 0, dx, jnp.where(axis == 1, dy, dz))
        second = jnp.where(axis < 2, dz, jnp.where((kind == 3) & (core == 0), dx, dy))
        order = jnp.where(along == 3, 2, 2 - along)
        leave = jnp.where(first < 2, order * 512 + kind * 128 + first * 64,
                          first * 768 + order * 256 + kind * 64)
        stay = jnp.where(first < 2, 3072 + kind * 128 + first * 64, 3072 + first * 256 + kind * 64)
        spot = jnp.where(along == 0, stay, leave) + second * 16 + slot % 16
        return jnp.where(oc == core, spot, -1)

    for r in (FLIP, BACK, OPPOSITE):
        far_code(r).wait_recv()

    @apart
    def _():
        for number, (first, q, second, r, step) in enumerate(pairs):
            from_row = pl.multiple_of((step - 1) * 256, 256)
            spots[:, number * 256:(number + 1) * 256] = codes[first, q, :, pl.ds(from_row, 256)]
        spots[...] = place_of(spots[...])

    complete(0, 8)
    far_copy(OPPOSITE, 0).wait_recv()
    far_copy(OPPOSITE, 1).wait_recv()
    correlate(runs[3])

    complete(8, 12)

    def device_of(kind, offsets):
        if kind < 3:
            return at(*offsets[kind])
        one, other = at(*offsets[3]), at(*offsets[4])
        return tuple(pick(core, b, a) for a, b in zip(one, other))

    begins, per_kind, stays = (0, 1536, 2304), (128, 64, 64), (0, 512, 768)
    pieces = [[(0, 0, 128), (1, 128, 128), (2, 256, 128), (3, 384, 64), (3, 448, 64)],
              [(kind, kind * 64, 64) for kind in range(4)]]

    def rows_of(part_of, along):
        count = 4 * per_kind[part_of]
        return pl.ds(begins[part_of] + (2, 1, 3).index(along) * count, count)

    def pieces_of(part_of):
        return pieces[min(part_of, 1)]

    def copy_a(part_of, along, piece):
        kind, begin, count = pieces_of(part_of)[piece]
        here = pl.ds(rows_of(part_of, along).start + begin, count)
        x, y, z = (along, 0, 0), (0, along, 0), (0, 0, along)
        last = (z, z) if piece == 4 else (x, y)
        return send(dense.at[here], got_a.at[here], S_A + (part_of * 3 + along - 1) * 5 + piece,
                    device_of(kind, (x, y, z) + last))

    def group_of(base, begin, end):
        down = lax.broadcasted_iota(jnp.int32, (512, end - begin), 0)
        hot = jnp.where(down == spots[:, begin:end] - base, 1.0, 0.0).astype(BF)
        return jnp.dot(hot, rows[begin:end], preferred_element_type=F32)

    @apart
    def _():
        early[0] = group_of(0, 0, 3072)
        early[1] = group_of(512, 0, 3072)

    complete(12, 16)
    ready = [[(0, 2)], [(0, 1)], [(0, 3)], [(1, 2), (1, 1)], [(1, 3), (2, 2)], [(2, 1), (2, 3)]]
    for group, leaves in enumerate(ready):
        @apart
        def _(group=group):
            if group < 2:
                total = early[group] + group_of(group * 512, 3072, 4096)
            else:
                total = group_of(group * 512, 0, 4096)
            dense[pl.ds(group * 512, 512)] = total.astype(BF)

        for part_of, along in leaves:
            for piece in range(len(pieces_of(part_of))):
                copy_a(part_of, along, piece).start()
        if group == 3:
            tally_stage(2)

    @apart
    def _():
        for half in range(2):
            own_sum[pl.ds(half * 512, 512)] = group_of(3072 + half * 512, 0, 4096)

    def copy_b(kind, spot):
        first, second = spot // 4, spot % 4
        last = ((second, 1, 0), (1, second, 0)) if first == 1 else ((0, first, second), (first, 0, second))
        offsets = ((0, first, second), (first, 0, second), (first, second, 0)) + last
        return send(part.at[kind, spot], got_b.at[kind, spot], S_B + kind * 3 + max(spot // 4 - 1, 0),
                    device_of(kind, offsets))

    spots_of = (range(1, 8), range(8, 12), range(12, 16))

    def all_b(kind, part_of):
        here = pl.ds(spots_of[part_of][0], len(spots_of[part_of]))
        return send(part.at[kind, here], got_b.at[kind, here], S_B + kind * 3 + part_of, sibling)

    for part_of in range(3):
        for along in (2, 1, 3):
            for piece in range(len(pieces_of(part_of))):
                copy_a(part_of, along, piece).wait_recv()

        @apart
        def _(part_of=part_of):
            count = per_kind[part_of]
            total = own_sum[pl.ds(stays[part_of], 4 * count)]
            for along in (2, 1, 3):
                total = total + got_a[rows_of(part_of, along)].astype(F32)
            total = total.astype(BF)
            for kind in range(4):
                here = total[kind * count:(kind + 1) * count]
                part[kind, pl.ds(stays[part_of] // 64, count // 16)] = here.reshape(count // 16, 16, LAGS)

        for spot in spots_of[part_of]:
            for kind in range(4):
                copy_b(kind, spot).start()

    count = tally[0:1]
    for v in range(1, 4):
        copy_n(2, v).wait()
        count = count + got_n[5 + v, v:v + 1]
    shape = (BINS_DEV, 128)
    diagonal = lax.broadcasted_iota(jnp.int32, shape, 0) == lax.broadcasted_iota(jnp.int32, shape, 1)
    count = jnp.sum(jnp.where(diagonal, count, 0.0), axis=1, keepdims=True)
    scale = lax.rsqrt(count + 1.0)

    sib_copy.wait_send()
    code_copy.wait_send()
    for r in (FLIP, BACK, OPPOSITE):
        far_code(r).wait_send()
        for j in range(2):
            if (r, j) != (BACK, 1):
                far_copy(r, j).wait_send()
    for number in range(16):
        row_copy(number).wait_send()
    for part_of in range(3):
        for along in range(1, 4):
            for piece in range(len(pieces_of(part_of))):
                copy_a(part_of, along, piece).wait_send()

    def gather(part_of):
        for kind in range(4):
            all_b(kind, part_of).wait_recv()

        @apart
        def _():
            for kind in range(4):
                here = pl.ds(kind * 16, 16)
                total = out_ref[here] if part_of else part[kind, 0].astype(F32)
                for spot in spots_of[part_of]:
                    total = total + got_b[kind, spot].astype(F32)
                out_ref[here] = total * scale[kind * 16:(kind + 1) * 16] if part_of == 2 else total

    for part_of in range(3):
        gather(part_of)
    for part_of in range(3):
        for kind in range(4):
            all_b(kind, part_of).wait_send()


def stacks(spectra, live_count, owner, slot, table):
    vmem, anywhere = pl.BlockSpec(memory_space=pltpu.VMEM), pl.BlockSpec(memory_space=pl.ANY)
    return pl.pallas_call(
        kernel,
        out_shape=pltpu.VMEM((BINS_DEV, LAGS), F32),
        in_specs=[anywhere, pl.BlockSpec(memory_space=pltpu.SMEM), anywhere, anywhere, anywhere],
        out_specs=vmem,
        scratch_shapes=[
            pltpu.VMEM((CH, 2, FREQS), BF),
            pltpu.VMEM((1, 2048), jnp.int32),
            pltpu.VMEM((1, 2048), jnp.int32),
            pltpu.VMEM((2, 2, CH, HALF), BF),
            pltpu.VMEM((4, 2, 2, CH, HALF), BF),
            pltpu.VMEM((FREQS, LAGS), BF),
            pltpu.VMEM((1024, FREQS), BF),
            pltpu.VMEM((4, 2, 1, 2048), jnp.int32),
            pltpu.VMEM((1, 4096), jnp.int32),
            pltpu.VMEM((16, 256, LAGS), F32),
            pltpu.VMEM((16, 256, LAGS), BF),
            pltpu.VMEM((16, 256, LAGS), BF),
            pltpu.VMEM((4096, LAGS), BF),
            pltpu.VMEM((2, 512, LAGS), F32),
            pltpu.VMEM((1024, LAGS), F32),
            pltpu.VMEM((3072, LAGS), BF),
            pltpu.VMEM((3072, LAGS), BF),
            pltpu.VMEM((4, 16, 16, LAGS), BF),
            pltpu.VMEM((4, 16, 16, LAGS), BF),
            pltpu.VMEM((128, 128), F32),
            pltpu.VMEM((9, 32, 128), F32),
            pltpu.SemaphoreType.DMA((N_SEM,)),
            pltpu.SemaphoreType.DMA((N_SEM,)),
            pltpu.SemaphoreType.DMA((2,)),
            pltpu.SemaphoreType.DMA((3,)),
        ],
        compiler_params=pltpu.CompilerParams(
            collective_id=0, has_side_effects=True, vmem_limit_bytes=56 * 1024 * 1024),
        cost_estimate=pl.CostEstimate(
            flops=13_000_000_000, bytes_accessed=4_000_000, transcendentals=40_000),
    )(spectra, live_count, owner, slot, table)


def on_device(spectra, live_count, owner_list, bin_list):
    table = jnp.asarray(table_constant(FREQS, LAGS))
    return stacks(spectra, live_count, owner_list.reshape(1, -1), bin_list.reshape(1, -1), table)


def solution(mesh):
    return jax.shard_map(
        on_device,
        mesh=mesh,
        in_specs=(
            P(("group", "blk"), None, None),
            P(("group", "blk")),
            P(("group", "blk"), None),
            P(("group", "blk")),
        ),
        out_specs=P(("group", "blk"), None),
        check_vma=False,
    )
```
